32 devices in a mesh: dp: 8 (over z, y), aa: 2 (over x), ba: 2 (over core).
Axes of the slice: x: 2, y: 2, z: 4, core: 2. Of those that a mesh axis runs over, the one named last changes fastest.
Arguments:
- images: bfloat16 [192, 196, 768], P(('dp', 'ba'), None, 'aa'), may hold values from -6 to 6
- counts: int32 [16], P(('dp', 'ba')), may hold values from 6 to 12, as said below
- ln1_gain: float32 [768], P('aa'), may hold values from 0.5 to 1.5
- ln1_bias: float32 [768], P('aa'), may hold values from -1.75 to 1.75
- tok_w1: bfloat16 [196, 384], replicated, may hold values from -0.4375 to 0.4375
- tok_b1: float32 [384], replicated, may hold values from -1.75 to 1.75
- tok_w2: bfloat16 [384, 196], replicated, may hold values from -0.3125 to 0.3125
- tok_b2: float32 [196], replicated, may hold values from -1.75 to 1.75
- ln2_gain: float32 [768], P('aa'), may hold values from 0.5 to 1.5
- ln2_bias: float32 [768], P('aa'), may hold values from -1.75 to 1.75
- ch_w1: bfloat16 [768, 3072], P(None, 'ba'), may hold values from -0.21875 to 0.21875
- ch_b1: float32 [3072], P('ba'), may hold values from -1.75 to 1.75
- ch_w2: bfloat16 [3072, 768], P('ba'), may hold values from -0.109375 to 0.109375
- ch_b2: float32 [768], P('aa'), may hold values from -1.75 to 1.75
- cotangent: bfloat16 [192, 196, 768], P(('dp', 'ba'), None, 'aa'), may hold values from -6 to 6
Outputs:
- output: bfloat16 [192, 196, 768], P(('dp', 'ba'), None, 'aa')
- grad_images: float32 [192, 196, 768], P(('dp', 'ba'), None, 'aa')
- grad_ln1_gain: float32 [768], P('aa')
- grad_ln1_bias: float32 [768], P('aa')
- grad_tok_w1: float32 [196, 384], replicated
- grad_tok_b1: float32 [384], replicated
- grad_tok_w2: float32 [384, 196], replicated
- grad_tok_b2: float32 [196], replicated
- grad_ln2_gain: float32 [768], P('aa')
- grad_ln2_bias: float32 [768], P('aa')
- grad_ch_w1: float32 [768, 3072], P(None, 'ba')
- grad_ch_b1: float32 [3072], P('ba')
- grad_ch_w2: float32 [3072, 768], P('ba')
- grad_ch_b2: float32 [768], P('aa')
The draws below stay inside these ranges and needn't reach their ends.
Inputs may be any that keep to these rules, and one draw needn't show every extreme that they name: Group g of 12 slots holds counts[g] real images in its first slots; at least one group is full in every draw.
All inputs are finite; a program needn't handle non-finite values.
Results may differ from the reference program's by a relative error of at most 0.007.
Values may be sent and summed in bfloat16 or wider, within the bound.
A program may use at most 192 MiB of HBM per device.

```python
import jax
import jax.numpy as jnp
from jax import lax

D = 768
S = 196
DS = 384
DC = 3072
IMG_DEV = 12
GROUPS = 16
IMAGES = 192


def draw_counts(key, part):
    key = jax.random.fold_in(key, 11)
    low_key, pick_key = jax.random.split(key)
    lowest = (IMG_DEV + 1) // 2
    values = jax.random.randint(low_key, (GROUPS,), lowest, IMG_DEV + 1)
    fullest = jax.random.randint(pick_key, (), 0, GROUPS)
    return jnp.where(jnp.arange(GROUPS) == fullest, IMG_DEV, values).astype(jnp.int32)


def steps_of(own_key, extent, cuts, low, largest):
    factor_of, own = 1.0, jax.random.fold_in(own_key, 6)
    for axis_at, parts in cuts:
        heights = jnp.exp(jax.random.uniform(jax.random.fold_in(own, axis_at), (parts,), jnp.float32, low / len(cuts), largest / len(cuts)))
        factor_of = factor_of * jnp.repeat(heights, extent[axis_at] // parts).reshape([-1 if axis == axis_at else 1 for axis in range(len(extent))])
    return factor_of


def normal_values(rng, dims, scale, limit, cuts=(), kind=jnp.bfloat16):
    drawn = scale * jax.random.normal(rng, dims, jnp.float32)
    if cuts:
        drawn = drawn * steps_of(rng, dims, cuts, -0.22, 0.18)
    return jnp.clip(drawn, -limit, limit).astype(kind)


def setup_inputs(seed: int = 0) -> dict:
    streams_of = jax.random.split(jax.random.key(seed), 16)
    return {
        "images": normal_values(streams_of[0], (IMAGES, S, D), 1.0, 6.0, ((0, 16), (2, 2))),
        "counts": draw_counts(jax.random.fold_in(streams_of[15], 71), 0),
        "ln1_gain": jnp.clip(1.0 + 0.1 * jax.random.normal(streams_of[2], (D,), jnp.float32), 0.5, 1.5),
        "ln1_bias": normal_values(streams_of[3], (D,), 0.3, 1.75, ((0, 2),), jnp.float32),
        "tok_w1": normal_values(streams_of[4], (S, DS), S ** -0.5, 0.4375),
        "tok_b1": normal_values(streams_of[5], (DS,), 0.3, 1.75, (), jnp.float32),
        "tok_w2": normal_values(streams_of[6], (DS, S), DS ** -0.5, 0.3125),
        "tok_b2": normal_values(streams_of[7], (S,), 0.3, 1.75, (), jnp.float32),
        "ln2_gain": jnp.clip(1.0 + 0.1 * jax.random.normal(streams_of[8], (D,), jnp.float32), 0.5, 1.5),
        "ln2_bias": normal_values(streams_of[9], (D,), 0.3, 1.75, ((0, 2),), jnp.float32),
        "ch_w1": normal_values(streams_of[10], (D, DC), D ** -0.5, 0.21875, ((1, 2),)),
        "ch_b1": normal_values(streams_of[11], (DC,), 0.3, 1.75, ((0, 2),), jnp.float32),
        "ch_w2": normal_values(streams_of[12], (DC, D), DC ** -0.5, 0.109375, ((0, 2),)),
        "ch_b2": normal_values(streams_of[13], (D,), 0.3, 1.75, ((0, 2),), jnp.float32),
        "cotangent": normal_values(streams_of[14], (IMAGES, S, D), 1.0, 6.0, ((0, 16), (2, 2))),
    }


epsilon = 1e-06

@jax.custom_vjp
def low(v):
    return lax.optimization_barrier(v.astype(jnp.bfloat16)).astype(jnp.float32)

@jax.custom_vjp
def low_back(v):
    return v

def low_keep(v):
    return (low(v), None)

def low_pass(kept, grad):
    return (grad,)

def back_keep(v):
    return (v, None)

def back_low(kept, grad):
    return (low(grad),)
low.defvjp(low_keep, low_pass)
low_back.defvjp(back_keep, back_low)

def layer_norm(values, gain_vec, bias_vec):
    center = lax.optimization_barrier(jnp.mean(values, -1, keepdims=True))
    spread = lax.optimization_barrier(jnp.mean((values - center) ** 2, -1, keepdims=True))
    return (values - center) * lax.rsqrt(spread + epsilon) * gain_vec + bias_vec

def group_layer(source, valid, params):
    gain_one, bias_one, tok_in, tok_bias_in, tok_out, tok_bias_out, gain_two, bias_two, chan_in, chan_bias_in, chan_out, chan_bias_out = params
    highest = lax.Precision.HIGHEST
    normed_one = low(layer_norm(source, gain_one, bias_one))
    pre_tok = low_back(jnp.einsum('sk,isc->ikc', tok_in, normed_one, precision=highest) + tok_bias_in[None, :, None])
    act_tok = low(jax.nn.gelu(pre_tok))
    token_out = low_back(jnp.einsum('ks,ikc->isc', tok_out, act_tok, precision=highest) + tok_bias_out[None, :, None])
    residual = source + token_out
    normed_two = low(layer_norm(residual, gain_two, bias_two))
    pre_chan = low_back(jnp.einsum('isc,ch->ish', normed_two, chan_in, precision=highest) + chan_bias_in)
    act_chan = low(jax.nn.gelu(pre_chan))
    chan_result = low_back(jnp.einsum('ish,hc->isc', act_chan, chan_out, precision=highest))
    return valid[:, None, None] * (residual + chan_result + chan_bias_out)

def reference(images, counts, ln1_gain, ln1_bias, tok_w1, tok_b1, tok_w2, tok_b2, ln2_gain, ln2_bias, ch_w1, ch_b1, ch_w2, ch_b2, cotangent):
    params = tuple((p.astype(jnp.float32) for p in (ln1_gain, ln1_bias, tok_w1, tok_b1, tok_w2, tok_b2, ln2_gain, ln2_bias, ch_w1, ch_b1, ch_w2, ch_b2)))
    group_count = counts.shape[0]
    source = images.astype(jnp.float32).reshape(group_count, IMG_DEV, S, D)
    slot_ids = jnp.arange(IMG_DEV, dtype=jnp.int32)
    valid = (slot_ids[None, :] < counts[:, None]).astype(jnp.float32)

    def layer_all(source_all, params_all):

        def per_group(group_item):
            return jax.checkpoint(group_layer)(group_item[0], group_item[1], params_all)
        return lax.map(per_group, (source_all, valid))
    result, pullback = jax.vjp(layer_all, source, params)
    grad_source, grads = pullback(cotangent.astype(jnp.float32).reshape(result.shape))
    return (result.reshape(IMAGES, S, D).astype(jnp.bfloat16), grad_source.reshape(IMAGES, S, D), grads[0], grads[1], grads[2], grads[3], grads[4], grads[5], grads[6], grads[7], grads[8], grads[9], grads[10], grads[11])
```

```python
import functools

import jax
import jax.numpy as jnp
from jax import lax
from jax.experimental import pallas as pl
from jax.experimental.pallas import tpu as pltpu
from jax.sharding import PartitionSpec as P

MESH = pl.DeviceIdType.MESH
EPS = 1e-06
C0 = 0.7978845608028654
C1 = C0 * 0.044715
RING = 8
LOOK = 2
F32 = jnp.float32
BF16 = jnp.bfloat16


def dot(left, right, left_dim, right_dim):
    return lax.dot_general(
        left, right, (((left_dim,), (right_dim,)), ((), ())), preferred_element_type=F32
    )


def gelu(v):
    return v * (0.5 * jnp.tanh(v * (C0 + C1 * (v * v))) + 0.5)


def gelu_both(v):
    v2 = v * v
    h = 0.5 * jnp.tanh(v * (C0 + C1 * v2)) + 0.5
    return v * h, h + (h - h * h) * (v * (2 * C0 + 6 * C1 * v2))


def mod(v):
    return lax.rem(v + 2 * RING, RING)


def layer_kernel(
    groups,
    valid,
    images,
    cot,
    vec_own,
    tw1,
    tb1,
    tw2,
    tb2,
    w1_own,
    w2_own,
    b1_own,
    out_o,
    gim_o,
    d2_o,
    d1_o,
    small_o,
    xb,
    cb,
    y2b,
    gb,
    res,
    acc,
    w1b,
    w2b,
    act,
    dg,
    stat,
    pb,
    bar,
    rs,
    xs,
    vecb,
    b1h,
    b1v,
    vacc,
    loc_x,
    snd_x,
    rcv_x,
    loc_c,
    snd_c,
    rcv_c,
    loc_w,
    snd_w,
    rcv_w,
    snd_b,
    rcv_b,
    snd_r,
    rcv_r,
    snd_e,
    rcv_e,
    snd_g,
    rcv_g,
    loc_g,
    loc_o,
    snd_o,
    rcv_o,
    loc_i,
    snd_i,
    rcv_i,
):
    imgs, patches, chans = xb.shape
    half = chans // 2
    pad = y2b.shape[0] // imgs
    piece = w1_own.shape[1]
    sub = piece // 2
    dp, aa, ba = lax.axis_index("dp"), lax.axis_index("aa"), lax.axis_index("ba")
    lo, hi = lax.rem(dp, RING), lax.div(dp, RING)
    fold = lax.rem(lo, 2)
    pos = jnp.where(fold == 0, lax.div(lo, 2), RING - 1 - lax.div(lo, 2))

    def at(place):
        place = mod(place)
        return hi * RING + jnp.where(
            place < RING // 2, 2 * place, 2 * (RING - 1 - place) + 1
        )

    dev_x = (dp, 1 - aa, ba)
    dev_c = (dp, aa, 1 - ba)
    dev_ring = ((at(pos + 1), aa, ba), (at(pos - 1), aa, ba))
    dev_hi = []
    step = 1
    while step < groups:
        partner = hi + step - 2 * step * lax.rem(lax.div(hi, step), 2)
        dev_hi.append((partner * RING + lo, aa, ba))
        step *= 2
    peers = [dev_x, dev_c, *dev_ring, *dev_hi]
    barrier = pltpu.get_barrier_semaphore()
    for peer in peers:
        pl.semaphore_signal(barrier, inc=1, device_id=peer, device_id_type=MESH)
    pl.semaphore_wait(barrier, len(peers))

    mine = pl.ds(pl.multiple_of(aa * half, half), half)
    other = pl.ds(pl.multiple_of((1 - aa) * half, half), half)
    rows_mine = pl.ds(pl.multiple_of(ba * piece, 64), piece)
    rows_other = pl.ds(pl.multiple_of((1 - ba) * piece, 64), piece)

    def remote(src, dst, send, recv, dev):
        return pltpu.make_async_remote_copy(
            src_ref=src,
            dst_ref=dst,
            send_sem=send,
            recv_sem=recv,
            device_id=dev,
            device_id_type=MESH,
        )

    def local_in(src, dst, sem, i):
        return pltpu.make_async_copy(src.at[aa * imgs + i], dst.at[i, :, mine], sem.at[i])

    def give(src, dst, send, recv, i):
        return remote(
            src.at[(1 - aa) * imgs + i], dst.at[i, :, mine], send.at[i], recv.at[i], dev_x
        )

    def take(src, dst, send, recv, i):
        return remote(
            src.at[(1 - aa) * imgs + i], dst.at[i, :, other], send.at[i], recv.at[i], dev_x
        )

    vec_copy = remote(vec_own, vecb.at[aa], snd_w.at[2], rcv_w.at[2], dev_x)
    vec_copy.start()
    vecb[aa] = vec_own[...]
    for i in range(imgs):
        local_in(images, xb, loc_x, i).start()
    for i in range(LOOK):
        give(images, xb, snd_x, rcv_x, i).start()
    b1_copy = remote(b1_own, b1h.at[ba], snd_w.at[3], rcv_w.at[3], dev_c)
    b1_copy.start()
    b1h[ba] = b1_own[...]
    w_local = []
    w_remote = []
    for k, (src, dst) in enumerate(((w1_own, w1b), (w2_own, w2b))):
        w_local.append(pltpu.make_async_copy(src, dst.at[:, rows_mine, :], loc_w.at[k]))
        w_remote.append(
            remote(src, dst.at[:, rows_mine, :], snd_w.at[k], rcv_w.at[k], dev_c)
        )
        w_local[-1].start()
        w_remote[-1].start()
    for i in range(imgs):
        local_in(cot, cb, loc_c, i).start()
    y2b[...] = jnp.zeros(y2b.shape, BF16)
    gb[...] = jnp.zeros(gb.shape, BF16)
    rs[0] = jnp.zeros(rs.shape[1:], BF16)
    vacc[...] = jnp.zeros(vacc.shape, F32)
    small_o[...] = jnp.zeros(small_o.shape, F32)
    remote(vec_own, vecb.at[1 - aa], snd_w.at[2], rcv_w.at[2], dev_x).wait()

    def vec(k):
        return jnp.concatenate([vecb[0, k : k + 1, :], vecb[1, k : k + 1, :]], axis=1)

    def token_forward(i, carry):
        local_in(images, xb, loc_x, i).wait()
        take(images, xb, snd_x, rcv_x, i).wait()

        @pl.when(i + LOOK < imgs)
        def _():
            give(images, xb, snd_x, rcv_x, i + LOOK).start()

        @pl.when(i + LOOK >= imgs)
        def _():
            give(cot, cb, snd_c, rcv_c, i + LOOK - imgs).start()

        x = xb[i].astype(F32)
        mean = jnp.mean(x, -1, keepdims=True)
        xc = x - mean
        rstd = lax.rsqrt(jnp.mean(xc * xc, -1, keepdims=True) + EPS)
        stat[0, i] = mean
        stat[1, i] = rstd
        y1 = (xc * rstd * vec(0) + vec(1)).astype(BF16)
        hid = gelu(dot(tw1[...], y1, 0, 0) + tb1[...]).astype(BF16)
        row = x + dot(tw2[...], hid, 0, 0) + tb2[...]
        res[i] = row
        mean = jnp.mean(row, -1, keepdims=True)
        xc = row - mean
        rstd = lax.rsqrt(jnp.mean(xc * xc, -1, keepdims=True) + EPS)
        stat[2, i] = mean
        stat[3, i] = rstd
        y2 = (xc * rstd * vec(2) + vec(3)).astype(BF16)
        y2b[pl.ds(pl.multiple_of(i * pad, 16), patches), :] = y2
        return carry

    lax.fori_loop(0, imgs, token_forward, 0)
    for i in range(LOOK, imgs):
        give(cot, cb, snd_c, rcv_c, i).start()

    remote(b1_own, b1h.at[1 - ba], snd_w.at[3], rcv_w.at[3], dev_c).wait()
    b1v[...] = jnp.concatenate([b1h[0], b1h[1]], axis=1)
    for k, (src, dst) in enumerate(((w1_own, w1b), (w2_own, w2b))):
        w_local[k].wait()
        remote(src, dst.at[:, rows_other, :], snd_w.at[k], rcv_w.at[k], dev_c).wait()

    chunks = 3
    size = y2b.shape[0] // chunks
    width = 2 * piece

    def chan_forward(k, carry):
        pair = lax.div(k, chunks)
        rows = pl.ds(pl.multiple_of(lax.rem(k, chunks) * size, 16), size)
        win = w1b[pl.ds(2 * pair, 2)].reshape(2 * width, chans)
        wout = w2b[pl.ds(2 * pair, 2)].reshape(2 * width, chans)
        bias = jnp.concatenate(
            [b1v[pl.ds(2 * pair, 1), :], b1v[pl.ds(2 * pair + 1, 1), :]], axis=1
        )
        val, der = gelu_both(dot(y2b[rows, :], win, 1, 1) + bias)
        val = val.astype(BF16)
        der = der.astype(BF16)
        act[2 * pair, rows, :] = val[:, :width]
        act[2 * pair + 1, rows, :] = val[:, width:]
        dg[2 * pair, rows, :] = der[:, :width]
        dg[2 * pair + 1, rows, :] = der[:, width:]
        new = dot(val, wout, 1, 0)
        acc[rows, :] = jnp.where(pair == 0, 0.0, acc[rows, :]) + new
        return carry

    lax.fori_loop(0, RING // 2 * chunks, chan_forward, 0)

    def out_local(i):
        return pltpu.make_async_copy(cb.at[i, :, mine], out_o.at[aa * imgs + i], loc_o.at[i])

    def out_remote(i, sender):
        return remote(
            cb.at[i, :, other], out_o.at[sender * imgs + i], snd_o.at[i], rcv_o.at[i], dev_x
        )

    def finish_out(i, carry):
        local_in(cot, cb, loc_c, i).wait()
        take(cot, cb, snd_c, rcv_c, i).wait()
        rows = pl.ds(pl.multiple_of(i * pad, 16), patches)
        scale = valid[aa * imgs + i]
        gb[rows, :] = (cb[i].astype(F32) * scale).astype(BF16)
        cb[i] = (scale * (res[i] + acc[rows, :] + vec(4))).astype(BF16)
        out_local(i).start()
        out_remote(i, aa).start()
        return carry

    lax.fori_loop(0, imgs, finish_out, 0)

    def to_core(par, a):
        return remote(
            pb.at[par, a, rows_other, :], bar.at[par, a], snd_b.at[par, a], rcv_b.at[par, a], dev_c
        )

    def to_ring(s, a, c):
        rows = pl.ds(c * sub, sub)
        return remote(
            rs.at[s, a, rows, :],
            rs.at[s + 1, a, rows, :],
            snd_r.at[s, a, c],
            rcv_r.at[s, a, c],
            dev_ring[a],
        )

    def chan_backward(s, carry):
        par = lax.rem(s, 2)

        @pl.when(s >= 2)
        def _():
            for a in range(2):
                to_core(par, a).wait_send()

        right = mod(pos - 1 - s)
        left = mod(pos + 1 + s)
        pb[par, 0] = dot(act[right], gb[...], 0, 0).astype(BF16)
        to_core(par, 0).start()
        grad = (dot(gb[...], w2b[left], 1, 1) * dg[left].astype(F32)).astype(BF16)
        small_o[pl.ds(416 + left, 1), :] = jnp.sum(grad.astype(F32), 0, keepdims=True)
        pb[par, 1] = dot(grad, y2b[...], 0, 0).astype(BF16)
        to_core(par, 1).start()
        acc[...] = jnp.where(s == 0, 0.0, acc[...]) + dot(grad, w1b[left], 1, 0)
        for a in range(2):
            to_core(par, a).wait_recv()
        for c in range(2):
            for a in range(2):

                @pl.when(s > 0)
                def _():
                    to_ring(s - 1, a, c).wait_recv()

                rows = pl.ds(c * sub, sub)
                own = pl.ds(pl.multiple_of(ba * piece + c * sub, 32), sub)
                total = (
                    pb[par, a, own, :].astype(F32)
                    + bar[par, a, rows, :].astype(F32)
                    + rs[s, a, rows, :].astype(F32)
                )
                rs[s, a, rows, :] = total.astype(BF16)

                @pl.when(s < RING - 1)
                def _():
                    to_ring(s, a, c).start()

        return carry

    lax.fori_loop(0, RING, chan_backward, 0)
    for par in range(2):
        for a in range(2):
            to_core(par, a).wait_send()

    last = RING - 1
    for k, dev in enumerate([dev_x, *dev_hi]):
        copies = [
            remote(rs.at[last, a], xs.at[k, a], snd_e.at[k, a], rcv_e.at[k, a], dev)
            for a in range(2)
        ]
        for copy in copies:
            copy.start()
        for a, copy in enumerate(copies):
            copy.wait()
            rs[last, a] = (rs[last, a].astype(F32) + xs[k, a].astype(F32)).astype(BF16)

    results = (d2_o, d1_o)

    def gather(t, a, c, src):
        q = mod(pos - t) if a == 0 else mod(pos + t)
        rows = pl.ds(c * sub, sub)
        dst = results[a].at[q, rows, :]
        return remote(
            dst if src is None else src.at[rows, :],
            dst,
            snd_g.at[t, a, c],
            rcv_g.at[t, a, c],
            dev_ring[a],
        )

    def gather_arrival(t, a, c):
        q = mod(pos - 1 - t) if a == 0 else mod(pos + 1 + t)
        dst = results[a].at[q, pl.ds(c * sub, sub), :]
        return remote(dst, dst, snd_g.at[t, a, c], rcv_g.at[t, a, c], dev_ring[a])

    keep = []
    for a in range(2):
        for c in range(2):
            gather(0, a, c, rs.at[last, a]).start()
        keep.append(
            pltpu.make_async_copy(rs.at[last, a], results[a].at[pos], loc_g.at[a])
        )
        keep[-1].start()

    def grad_local(i):
        return pltpu.make_async_copy(xb.at[i, :, mine], gim_o.at[aa * imgs + i], loc_i.at[i])

    def grad_remote(i, sender):
        return remote(
            xb.at[i, :, other], gim_o.at[sender * imgs + i], snd_i.at[i], rcv_i.at[i], dev_x
        )

    ones = jnp.ones((8, chans), BF16)

    def token_backward(i, carry):
        rows = pl.ds(pl.multiple_of(i * pad, 16), patches)
        up = acc[rows, :]
        grad_out = gb[rows, :].astype(F32)
        rstd = stat[3, i]
        normed = (res[i] - stat[2, i]) * rstd
        vacc[2:3, :] += jnp.sum(up * normed, 0, keepdims=True)
        vacc[3:4, :] += jnp.sum(up, 0, keepdims=True)
        vacc[4:5, :] += jnp.sum(grad_out, 0, keepdims=True)
        q = up * vec(2)
        mean = jnp.mean(q, -1, keepdims=True)
        proj = jnp.mean(q * normed, -1, keepdims=True)
        grad_res = grad_out + rstd * (q - mean - normed * proj)
        grad_tok = grad_res.astype(BF16)
        rstd = stat[1, i]
        normed = (xb[i].astype(F32) - stat[0, i]) * rstd
        y1 = (normed * vec(0) + vec(1)).astype(BF16)
        val, der = gelu_both(dot(tw1[...], y1, 0, 0) + tb1[...])
        small_o[200 : 200 + patches, :] += dot(grad_tok, val.astype(BF16), 1, 1)
        small_o[408:416, 0:patches] += dot(ones, grad_tok, 1, 1)
        grad_pre = (dot(tw2[...], grad_tok, 1, 0) * der).astype(BF16)
        small_o[0:patches, :] += dot(y1, grad_pre, 1, 1)
        small_o[400:408, :] += dot(ones, grad_pre, 1, 1)
        up = dot(tw1[...], grad_pre, 1, 0)
        vacc[0:1, :] += jnp.sum(up * normed, 0, keepdims=True)
        vacc[1:2, :] += jnp.sum(up, 0, keepdims=True)
        q = up * vec(0)
        mean = jnp.mean(q, -1, keepdims=True)
        proj = jnp.mean(q * normed, -1, keepdims=True)
        xb[i] = (grad_res + rstd * (q - mean - normed * proj)).astype(BF16)
        grad_local(i).start()
        grad_remote(i, aa).start()
        return carry

    def gather_step(t, carry):
        @pl.when(t < imgs)
        def _():
            token_backward(t, 0)

        for c in range(2):
            for a in range(2):
                gather_arrival(t, a, c).wait_recv()

                @pl.when(t + 1 < RING - 1)
                def _():
                    gather(t + 1, a, c, None).start()

        return carry

    lax.fori_loop(0, RING - 1, gather_step, 0)
    small_o[424:432, :] = vacc[:, :half]
    small_o[432:440, :] = vacc[:, half:]

    for copy in keep:
        copy.wait()

    def drain_images(i, carry):
        out_local(i).wait()
        out_remote(i, 1 - aa).wait()
        grad_local(i).wait()
        grad_remote(i, 1 - aa).wait()
        return carry

    lax.fori_loop(0, imgs, drain_images, 0)

    def drain_ring(t, carry):
        for a in range(2):
            for c in range(2):
                to_ring(t, a, c).wait_send()
                gather_arrival(t, a, c).wait_send()
        return carry

    lax.fori_loop(0, RING - 1, drain_ring, 0)


def local(groups, images, counts, ln1_gain, ln1_bias, tok_w1, tok_b1, tok_w2, tok_b2,
          ln2_gain, ln2_bias, ch_w1, ch_b1, ch_w2, ch_b2, cotangent):
    slots, patches, half = images.shape
    chans = 2 * half
    imgs = slots // 2
    pad = -(-patches // 16) * 16
    hidden = ch_w1.shape[1]
    piece = hidden // RING
    hid_tok = tok_w1.shape[1]
    valid = (jnp.arange(slots) < counts[0]).astype(F32)
    zero = jnp.zeros_like(ln1_gain)
    vec = jnp.stack([ln1_gain, ln1_bias, ln2_gain, ln2_bias, ch_b2, zero, zero, zero])
    w1 = ch_w1.T.reshape(RING, piece, chans)
    w2 = ch_w2.reshape(RING, piece, chans)
    b1 = ch_b1.reshape(RING, piece)
    steps = 1
    while 2**(steps - 1) < groups:
        steps += 1
    vmem = pl.BlockSpec(memory_space=pltpu.VMEM)
    hbm = pl.BlockSpec(memory_space=pl.ANY)
    dma = pltpu.SemaphoreType.DMA
    per_image = [dma((imgs,))] * 3
    out, gim, d2, d1, small = pl.pallas_call(
        functools.partial(layer_kernel, groups),
        out_shape=[
            jax.ShapeDtypeStruct((slots, patches, half), BF16),
            jax.ShapeDtypeStruct((slots, patches, half), BF16),
            jax.ShapeDtypeStruct((RING, piece, chans), BF16),
            jax.ShapeDtypeStruct((RING, piece, chans), BF16),
            jax.ShapeDtypeStruct((512, hid_tok), F32),
        ],
        in_specs=[pl.BlockSpec(memory_space=pltpu.SMEM), hbm, hbm]
        + [vmem] * 5
        + [hbm] * 2
        + [vmem],
        out_specs=[hbm] * 4 + [vmem],
        scratch_shapes=[
            pltpu.VMEM((imgs, patches, chans), BF16),
            pltpu.VMEM((imgs, patches, chans), BF16),
            pltpu.VMEM((imgs * pad, chans), BF16),
            pltpu.VMEM((imgs * pad, chans), BF16),
            pltpu.VMEM((imgs, patches, chans), F32),
            pltpu.VMEM((imgs * pad, chans), F32),
            pltpu.VMEM((RING, 2 * piece, chans), BF16),
            pltpu.VMEM((RING, 2 * piece, chans), BF16),
            pltpu.VMEM((RING, imgs * pad, 2 * piece), BF16),
            pltpu.VMEM((RING, imgs * pad, 2 * piece), BF16),
            pltpu.VMEM((4, imgs, patches, 1), F32),
            pltpu.VMEM((2, 2, 2 * piece, chans), BF16),
            pltpu.VMEM((2, 2, piece, chans), BF16),
            pltpu.VMEM((RING, 2, piece, chans), BF16),
            pltpu.VMEM((steps, 2, piece, chans), BF16),
            pltpu.VMEM((2, 8, half), F32),
            pltpu.VMEM((2, RING, piece), F32),
            pltpu.VMEM((RING, 2 * piece), F32),
            pltpu.VMEM((8, chans), F32),
            *per_image,
            *per_image,
            dma((2,)),
            dma((4,)),
            dma((4,)),
            dma((2, 2)),
            dma((2, 2)),
            dma((RING, 2, 2)),
            dma((RING, 2, 2)),
            dma((steps, 2)),
            dma((steps, 2)),
            dma((RING, 2, 2)),
            dma((RING, 2, 2)),
            dma((2,)),
            *per_image,
            *per_image,
        ],
        compiler_params=pltpu.CompilerParams(
            collective_id=0, has_side_effects=True, vmem_limit_bytes=63 * 2**20
        ),
    )(
        valid,
        images,
        cotangent,
        vec,
        tok_w1,
        tok_b1[:, None],
        tok_w2,
        tok_b2[:, None],
        w1,
        w2,
        b1,
    )
    small = lax.psum(small, ("dp", "aa", "ba"))
    aa, ba = lax.axis_index("aa"), lax.axis_index("ba")
    rows = lax.dynamic_slice_in_dim(small, 424 + 8 * aa, 8, 0)
    grad_b1 = lax.dynamic_slice_in_dim(small[416:424], ba * piece, piece, 1).reshape(hidden)
    return (
        out,
        gim.astype(F32),
        rows[0],
        rows[1],
        small[0:patches],
        small[400],
        small[200 : 200 + patches].T,
        small[408, :patches],
        rows[2],
        rows[3],
        d1.reshape(hidden, chans).T.astype(F32),
        grad_b1,
        d2.reshape(hidden, chans).astype(F32),
        rows[4],
    )


def solution(mesh):
    rows = P(("dp", "ba"), None, "aa")
    chan = P("aa")
    placed = (rows, P(("dp", "ba")), chan, chan, P(), P(), P(), P(), chan, chan,
              P(None, "ba"), P("ba"), P("ba", None), chan, rows)
    given = (rows, rows, chan, chan, P(), P(), P(), P(), chan, chan,
             P(None, "ba"), P("ba"), P("ba", None), chan)
    return jax.shard_map(
        functools.partial(local, mesh.shape["dp"] // RING),
        mesh=mesh,
        in_specs=placed,
        out_specs=given,
        check_vma=False,
    )
```

```python
import functools

import jax
import jax.numpy as jnp
from jax import lax
from jax.experimental import pallas as pl
from jax.experimental.pallas import tpu as pltpu
from jax.sharding import PartitionSpec as P

MESH = pl.DeviceIdType.MESH
EPS = 1e-06
C0 = 0.7978845608028654
C1 = C0 * 0.044715
RING = 8
LOOK = 2
SOLO = 48
F32 = jnp.float32
BF16 = jnp.bfloat16


def dot(left, right, left_dim, right_dim):
    return lax.dot_general(
        left, right, (((left_dim,), (right_dim,)), ((), ())), preferred_element_type=F32
    )


def gelu(v):
    return v * (0.5 * jnp.tanh(v * (C0 + C1 * (v * v))) + 0.5)


def gelu_both(v):
    v2 = v * v
    h = 0.5 * jnp.tanh(v * (C0 + C1 * v2)) + 0.5
    return v * h, h + (h - h * h) * (v * (2 * C0 + 6 * C1 * v2))


def mod(v):
    return lax.rem(v + 2 * RING, RING)


def flip(index, step):
    return index + step - 2 * step * lax.rem(lax.div(index, step), 2)


def column(row, length):
    return jnp.transpose(jnp.broadcast_to(row.reshape(1, length), (8, length)))[:, 0:1]


def layer_kernel(
    groups,
    counts,
    images,
    cot,
    gain1,
    bias1,
    gain2,
    bias2,
    biasc,
    tw1,
    tb1,
    tw2,
    tb2,
    w1_own,
    w2_own,
    b1_own,
    out_o,
    gim_o,
    d2_o,
    d1_o,
    small_o,
    xh,
    xb,
    cb,
    ob,
    y2b,
    gb,
    res,
    acc,
    w1b,
    w2b,
    act,
    dg,
    stat,
    pb,
    bar,
    xr,
    rs,
    xs,
    vecb,
    b1h,
    b1v,
    t1v,
    t2v,
    vacc,
    small,
    small_c,
    small_x,
    small_s,
    small_r,
    loc_x,
    snd_x,
    rcv_x,
    loc_c,
    snd_c,
    rcv_c,
    loc_w,
    snd_w,
    rcv_w,
    snd_b,
    rcv_b,
    snd_h,
    rcv_h,
    snd_r,
    rcv_r,
    snd_e,
    rcv_e,
    snd_g,
    rcv_g,
    snd_f,
    rcv_f,
    loc_g,
    loc_o,
    snd_o,
    rcv_o,
    loc_i,
    snd_i,
    rcv_i,
    snd_s,
    rcv_s,
):
    imgs, patches, chans = xb.shape
    half = chans // 2
    pad = y2b.shape[0] // imgs
    piece = w2_own.shape[1]
    both = piece - 2 * SOLO
    keep_rows = SOLO + both
    dp, aa, ba = lax.axis_index("dp"), lax.axis_index("aa"), lax.axis_index("ba")
    lo, hi = lax.rem(dp, RING), lax.div(dp, RING)
    pos = jnp.where(lax.rem(lo, 2) == 0, lax.div(lo, 2), RING - 1 - lax.div(lo, 2))

    def at(place):
        place = mod(place)
        return hi * RING + jnp.where(
            place < RING // 2, 2 * place, 2 * (RING - 1 - place) + 1
        )

    dev_x = (dp, 1 - aa, ba)
    dev_c = (dp, aa, 1 - ba)
    dev_ring = ((at(pos + 1), aa, ba), (at(pos - 1), aa, ba))
    dev_fly = []
    step = 1
    while step < RING * groups:
        dev_fly.append((flip(dp, step), aa, ba))
        step *= 2
    dev_hi = dev_fly[3:]
    peers = [dev_x, dev_c, *dev_ring, *dev_fly]
    barrier = pltpu.get_barrier_semaphore()
    for peer in peers:
        pl.semaphore_signal(barrier, inc=1, device_id=peer, device_id_type=MESH)

    mine = pl.ds(pl.multiple_of(aa * half, half), half)
    other = pl.ds(pl.multiple_of((1 - aa) * half, half), half)
    rows_mine = pl.ds(pl.multiple_of(ba * piece, 64), piece)
    rows_other = pl.ds(pl.multiple_of((1 - ba) * piece, 64), piece)

    def remote(src, dst, send, recv, dev):
        return pltpu.make_async_remote_copy(
            src_ref=src,
            dst_ref=dst,
            send_sem=send,
            recv_sem=recv,
            device_id=dev,
            device_id_type=MESH,
        )

    def local_in(src, dst, sem, i):
        return pltpu.make_async_copy(src.at[aa * imgs + i], dst.at[i, :, mine], sem.at[i])

    def give(src, dst, send, recv, i):
        return remote(
            src.at[(1 - aa) * imgs + i], dst.at[i, :, mine], send.at[i], recv.at[i], dev_x
        )

    def take(src, dst, send, recv, i):
        return remote(
            src.at[(1 - aa) * imgs + i], dst.at[i, :, other], send.at[i], recv.at[i], dev_x
        )

    cols = 2 * piece
    parts = w1_own.shape[1] // cols

    def w1_in(k):
        return pltpu.make_async_copy(
            w1_own.at[:, pl.ds(k * cols, cols)], act.at[k, pl.ds(0, chans), :], loc_w.at[1 + k]
        )

    for k in range(parts):
        w1_in(k).start()
    for i in range(imgs):
        local_in(images, xb, loc_x, i).start()
    w2_local = pltpu.make_async_copy(w2_own, w2b.at[:, rows_mine, :], loc_w.at[0])
    w2_local.start()
    for i in range(imgs):
        local_in(cot, cb, loc_c, i).start()
    for k, ref in enumerate((gain1, bias1, gain2, bias2, biasc)):
        vecb[aa, k : k + 1, :] = ref[...].reshape(1, half)
    b1h[ba] = b1_own[...].reshape(1, parts * cols)

    pl.semaphore_wait(barrier, len(peers))

    vec_copy = remote(vecb.at[aa], vecb.at[aa], snd_w.at[2], rcv_w.at[2], dev_x)
    vec_copy.start()
    for i in range(LOOK):
        give(images, xb, snd_x, rcv_x, i).start()
    b1_copy = remote(b1h.at[ba], b1h.at[ba], snd_w.at[3], rcv_w.at[3], dev_c)
    b1_copy.start()
    w2_copy = remote(w2_own, w2b.at[:, rows_mine, :], snd_w.at[0], rcv_w.at[0], dev_c)
    w2_copy.start()
    y2b[...] = jnp.zeros(y2b.shape, BF16)
    gb[...] = jnp.zeros(gb.shape, BF16)
    rs[0] = jnp.zeros(rs.shape[1:], BF16)
    vacc[...] = jnp.zeros(vacc.shape, F32)
    small[...] = jnp.zeros(small.shape, F32)
    t1v[...] = column(tb1[...], t1v.shape[0])
    t2v[...] = column(tb2[...], patches)
    for k in range(parts):
        w1_in(k).wait()
        turned = jnp.transpose(act[k, 0:chans, :])
        w1b[2 * k, rows_mine, :] = turned[:piece]
        w1b[2 * k + 1, rows_mine, :] = turned[piece:]
    w1_copy = remote(
        w1b.at[:, rows_mine, :], w1b.at[:, rows_mine, :], snd_w.at[1], rcv_w.at[1], dev_c
    )
    w1_copy.start()
    vec_copy.wait_send()
    remote(vecb.at[aa], vecb.at[1 - aa], snd_w.at[2], rcv_w.at[2], dev_x).wait_recv()
    b1_copy.wait_send()
    remote(b1h.at[ba], b1h.at[1 - ba], snd_w.at[3], rcv_w.at[3], dev_c).wait_recv()
    for q in range(RING):
        b1v[q : q + 1, :] = jnp.concatenate(
            [b1h[0, :, q * piece : (q + 1) * piece], b1h[1, :, q * piece : (q + 1) * piece]],
            axis=1,
        )

    def vec(k):
        return jnp.concatenate([vecb[0, k : k + 1, :], vecb[1, k : k + 1, :]], axis=1)

    def token_forward(i):
        local_in(images, xb, loc_x, i).wait()
        take(images, xb, snd_x, rcv_x, i).wait()

        @pl.when(i + LOOK < imgs)
        def _():
            give(images, xb, snd_x, rcv_x, i + LOOK).start()

        @pl.when(i + LOOK >= imgs)
        def _():
            give(cot, cb, snd_c, rcv_c, i + LOOK - imgs).start()

        x = xb[i].astype(F32)
        mean = jnp.mean(x, -1, keepdims=True)
        xc = x - mean
        rstd = lax.rsqrt(jnp.mean(xc * xc, -1, keepdims=True) + EPS)
        stat[i, :, 0 : 1] = mean
        stat[i, :, 1 : 2] = rstd
        y1 = (xc * rstd * vec(0) + vec(1)).astype(BF16)
        hid = gelu(dot(tw1[...], y1, 0, 0) + t1v[...]).astype(BF16)
        row = x + dot(tw2[...], hid, 1, 0) + t2v[...]
        res[i] = row
        mean = jnp.mean(row, -1, keepdims=True)
        xc = row - mean
        rstd = lax.rsqrt(jnp.mean(xc * xc, -1, keepdims=True) + EPS)
        stat[i, :, 2 : 3] = mean
        stat[i, :, 3 : 4] = rstd
        y2 = (xc * rstd * vec(2) + vec(3)).astype(BF16)
        y2b[pl.ds(pl.multiple_of(i * pad, 16), patches), :] = y2

    def weight(i):
        return jnp.where(aa * imgs + i < counts[0], 1.0, 0.0).astype(F32)

    chunks = 3
    size = y2b.shape[0] // chunks
    each = imgs // chunks

    def chan_forward(chunk, pair):
        rows = pl.ds(pl.multiple_of(chunk * size, 16), size)
        win = w1b[pl.ds(2 * pair, 2)].reshape(2 * cols, chans)
        wout = w2b[pl.ds(2 * pair, 2)].reshape(2 * cols, chans)
        bias = jnp.concatenate(
            [b1v[pl.ds(2 * pair, 1), :], b1v[pl.ds(2 * pair + 1, 1), :]], axis=1
        )
        val, der = gelu_both(dot(y2b[rows, :], win, 1, 1) + bias)
        val = val.astype(BF16)
        der = der.astype(BF16)
        act[2 * pair, rows, :] = val[:, :cols]
        act[2 * pair + 1, rows, :] = val[:, cols:]
        dg[2 * pair, rows, :] = der[:, :cols]
        dg[2 * pair + 1, rows, :] = der[:, cols:]
        new = dot(val, wout, 1, 0)
        acc[rows, :] = jnp.where(pair == 0, 0.0, acc[rows, :]) + new

    def forward_chunk(chunk, carry):
        def one(k, carry):
            token_forward(chunk * each + k)
            return carry

        lax.fori_loop(0, each, one, 0)

        @pl.when(chunk == 0)
        def _():
            w2_local.wait()
            w2_copy.wait_send()
            remote(
                w2_own, w2b.at[:, rows_other, :], snd_w.at[0], rcv_w.at[0], dev_c
            ).wait_recv()
            w1_copy.wait_send()
            remote(
                w1b.at[:, rows_mine, :], w1b.at[:, rows_other, :], snd_w.at[1], rcv_w.at[1], dev_c
            ).wait_recv()

        def two(k, carry):
            chan_forward(chunk, k)
            return carry

        lax.fori_loop(0, RING // 2, two, 0)

        def three(k, carry):
            i = chunk * each + k
            rows = pl.ds(pl.multiple_of(i * pad, 16), patches)
            ob[i] = (weight(i) * (res[i] + acc[rows, :] + vec(4))).astype(BF16)
            return carry

        lax.fori_loop(0, each, three, 0)
        return carry

    lax.fori_loop(0, chunks, forward_chunk, 0)
    for i in range(LOOK, imgs):
        give(cot, cb, snd_c, rcv_c, i).start()

    def mask_cot(i, carry):
        local_in(cot, cb, loc_c, i).wait()
        take(cot, cb, snd_c, rcv_c, i).wait()
        rows = pl.ds(pl.multiple_of(i * pad, 16), patches)
        gb[rows, :] = (cb[i].astype(F32) * weight(i)).astype(BF16)
        return carry

    lax.fori_loop(0, imgs, mask_cot, 0)

    def out_local(i):
        return pltpu.make_async_copy(ob.at[i, :, mine], out_o.at[aa * imgs + i], loc_o.at[i])

    def out_remote(i, sender):
        return remote(
            ob.at[i, :, other], out_o.at[sender * imgs + i], snd_o.at[i], rcv_o.at[i], dev_x
        )

    def grad_local(i):
        return pltpu.make_async_copy(xb.at[i, :, mine], gim_o.at[aa * imgs + i], loc_i.at[i])

    def grad_remote(i, sender):
        return remote(
            xb.at[i, :, other], gim_o.at[sender * imgs + i], snd_i.at[i], rcv_i.at[i], dev_x
        )

    ones = jnp.ones((8, chans), BF16)

    def token_backward(i):
        rows = pl.ds(pl.multiple_of(i * pad, 16), patches)
        up = acc[rows, :]
        grad_out = gb[rows, :].astype(F32)
        rstd = stat[i, :, 3 : 4]
        normed = (res[i] - stat[i, :, 2 : 3]) * rstd
        vacc[2:3, :] += jnp.sum(up * normed, 0, keepdims=True)
        vacc[3:4, :] += jnp.sum(up, 0, keepdims=True)
        vacc[4:5, :] += jnp.sum(grad_out, 0, keepdims=True)
        q = up * vec(2)
        mean = jnp.mean(q, -1, keepdims=True)
        proj = jnp.mean(q * normed, -1, keepdims=True)
        grad_res = grad_out + rstd * (q - mean - normed * proj)
        grad_tok = grad_res.astype(BF16)
        rstd = stat[i, :, 1 : 2]
        normed = (xb[i].astype(F32) - stat[i, :, 0 : 1]) * rstd
        y1 = (normed * vec(0) + vec(1)).astype(BF16)
        val, der = gelu_both(dot(tw1[...], y1, 0, 0) + t1v[...])
        small[200 : 200 + patches, :] += dot(grad_tok, val.astype(BF16), 1, 1)
        small[408:416, 0:patches] += dot(ones, grad_tok, 1, 1)
        grad_pre = (dot(tw2[...], grad_tok, 0, 0) * der).astype(BF16)
        small[0:patches, :] += dot(y1, grad_pre, 1, 1)
        small[400:408, :] += dot(ones, grad_pre, 1, 1)
        up = dot(tw1[...], grad_pre, 1, 0)
        vacc[0:1, :] += jnp.sum(up * normed, 0, keepdims=True)
        vacc[1:2, :] += jnp.sum(up, 0, keepdims=True)
        q = up * vec(0)
        mean = jnp.mean(q, -1, keepdims=True)
        proj = jnp.mean(q * normed, -1, keepdims=True)
        xb[i] = (grad_res + rstd * (q - mean - normed * proj)).astype(BF16)
        grad_local(i).start()
        grad_remote(i, aa).start()

    bars = bar.shape[0]
    solo_mine = pl.ds(pl.multiple_of(aa * SOLO, 16), SOLO)
    solo_other = pl.ds(pl.multiple_of((1 - aa) * SOLO, 16), SOLO)
    shared = pl.ds(2 * SOLO, both)

    def own_rows(place, size):
        return pl.ds(pl.multiple_of(ba * piece + place, 16), size)

    def to_core(s, a):
        return remote(
            pb.at[lax.rem(s, 2), a, rows_other, :],
            bar.at[lax.rem(s, bars), a],
            snd_b.at[lax.rem(s, bars), a],
            rcv_b.at[lax.rem(s, bars), a],
            dev_c,
        )

    def to_x(s, a):
        return remote(
            bar.at[lax.rem(s, bars), a, solo_other, :],
            xr.at[lax.rem(s, 2), a],
            snd_h.at[lax.rem(s, 2), a],
            rcv_h.at[lax.rem(s, 2), a],
            dev_x,
        )

    ring_rows = (pl.ds(0, SOLO), pl.ds(SOLO, both))

    def to_ring(s, a, c):
        return remote(
            rs.at[s, a, ring_rows[c], :],
            rs.at[s + 1, a, ring_rows[c], :],
            snd_r.at[s, a, c],
            rcv_r.at[s, a, c],
            dev_ring[a],
        )

    def first_sum(s, a):
        to_core(s, a).wait_recv()
        slot = lax.rem(s, bars)
        own = own_rows((1 - aa) * SOLO, SOLO)
        total = pb[lax.rem(s, 2), a, own, :].astype(F32) + bar[slot, a, solo_other, :].astype(F32)
        bar[slot, a, solo_other, :] = total.astype(BF16)
        to_x(s, a).start()

    def second_sum(s, a):
        par = lax.rem(s, 2)
        slot = lax.rem(s, bars)
        for c in (1, 0):
            if c == 0:
                to_x(s, a).wait()

            @pl.when(s > 0)
            def _():
                to_ring(s - 1, a, c).wait_recv()

            if c == 0:
                more = (
                    pb[par, a, own_rows(aa * SOLO, SOLO), :].astype(F32)
                    + bar[slot, a, solo_mine, :].astype(F32)
                    + xr[par, a].astype(F32)
                )
            else:
                more = pb[par, a, own_rows(2 * SOLO, both), :].astype(F32) + bar[
                    slot, a, shared, :
                ].astype(F32)
            rs[s, a, ring_rows[c], :] = (rs[s, a, ring_rows[c], :].astype(F32) + more).astype(BF16)

            @pl.when(s < RING - 1)
            def _():
                to_ring(s, a, c).start()

    def chan_backward(j, carry):
        @pl.when(j < RING)
        def _():
            par = lax.rem(j, 2)

            @pl.when(j >= 2)
            def _():
                for a in range(2):
                    to_core(j - 2, a).wait_send()

            pb[par, 0] = dot(act[mod(pos - 1 - j)], gb[...], 0, 0).astype(BF16)
            to_core(j, 0).start()

        @pl.when(j > 0)
        def _():
            for a in range(2):
                first_sum(j - 1, a)

        @pl.when(j < RING)
        def _():
            left = mod(pos + 1 + j)
            grad = (dot(gb[...], w2b[left], 1, 1) * dg[left].astype(F32)).astype(BF16)
            small[pl.ds(416 + left, 1), :] = jnp.sum(grad.astype(F32), 0, keepdims=True)
            pb[lax.rem(j, 2), 1] = dot(grad, y2b[...], 0, 0).astype(BF16)
            to_core(j, 1).start()
            acc[...] = jnp.where(j == 0, 0.0, acc[...]) + dot(grad, w1b[left], 1, 0)

        @pl.when(j == RING)
        def _():
            token_backward(0)

        @pl.when(j > 0)
        def _():
            for a in range(2):
                second_sum(j - 1, a)

        @pl.when(j < imgs)
        def _():
            out_local(j).start()
            out_remote(j, aa).start()

        return carry

    lax.fori_loop(0, RING + 1, chan_backward, 0)
    for s in (RING - 2, RING - 1):
        for a in range(2):
            to_core(s, a).wait_send()

    last = RING - 1
    results = (d2_o, d1_o)
    gather_rows = (solo_mine, shared)

    def gather(t, a, c, src):
        q = mod(pos - t) if a == 0 else mod(pos + t)
        dst = results[a].at[q, gather_rows[c], :]
        return remote(
            dst if src is None else src, dst, snd_g.at[t, a, c], rcv_g.at[t, a, c], dev_ring[a]
        )

    def gather_arrival(t, a, c):
        q = mod(pos - 1 - t) if a == 0 else mod(pos + 1 + t)
        dst = results[a].at[q, gather_rows[c], :]
        return remote(dst, dst, snd_g.at[t, a, c], rcv_g.at[t, a, c], dev_ring[a])

    def across(t, a, src):
        q = mod(pos - t) if a == 0 else mod(pos + t)
        dst = results[a].at[q, solo_mine, :]
        return remote(dst if src is None else src, dst, snd_f.at[t, a], rcv_f.at[t, a], dev_x)

    def across_arrival(t, a):
        q = mod(pos - t) if a == 0 else mod(pos + t)
        dst = results[a].at[q, solo_other, :]
        return remote(dst, dst, snd_f.at[t, a], rcv_f.at[t, a], dev_x)

    def add_hi(c):
        for k, dev in enumerate(dev_hi):
            for a in range(2):
                src = rs.at[last, a, ring_rows[c], :]
                landed = xh.at[k, a, ring_rows[c], :]
                near = pb.at[0, 0, ring_rows[c], :]
                copy = remote(src, landed, snd_e.at[1 + k, a, c], rcv_e.at[1 + k, a, c], dev)
                copy.start()
                copy.wait()
                back = pltpu.make_async_copy(landed, near, loc_g.at[a, c])
                back.start()
                back.wait()
                rs[last, a, ring_rows[c], :] = (
                    rs[last, a, ring_rows[c], :].astype(F32) + pb[0, 0, ring_rows[c], :].astype(F32)
                ).astype(BF16)

    keep = []

    def start_gather(c):
        add_hi(c)
        for a in range(2):
            src = rs.at[last, a, ring_rows[c], :]
            gather(0, a, c, src).start()
            if c == 0:
                across(0, a, src).start()
            keep.append(
                pltpu.make_async_copy(
                    src, results[a].at[pos, gather_rows[c], :], loc_g.at[a, c]
                )
            )
            keep[-1].start()

    swaps = [
        remote(rs.at[last, a, ring_rows[1], :], xs.at[a], snd_e.at[0, a, 1], rcv_e.at[0, a, 1], dev_x)
        for a in range(2)
    ]
    for copy in swaps:
        copy.start()
    start_gather(0)
    token_backward(1)
    for a, copy in enumerate(swaps):
        copy.wait()
        total = rs[last, a, ring_rows[1], :].astype(F32) + xs[a].astype(F32)
        rs[last, a, ring_rows[1], :] = total.astype(BF16)
    start_gather(1)

    def pass_on(t):
        for c in range(2):
            for a in range(2):
                gather_arrival(t, a, c).wait_recv()

                @pl.when(t + 1 < RING - 1)
                def _():
                    gather(t + 1, a, c, None).start()

                if c == 0:
                    across(t + 1, a, None).start()

    def token_and_gather(t, carry):
        token_backward(t + 2)
        pass_on(t)
        return carry

    lax.fori_loop(0, imgs - 2, token_and_gather, 0)
    small[424:432, :] = vacc[:, :half]
    small[432:440, :] = vacc[:, half:]

    total_rows = small.shape[0]
    half_rows, quarter = total_rows // 2, total_rows // 4
    own_half = pl.ds(pl.multiple_of(ba * half_rows, 256), half_rows)
    other_half = pl.ds(pl.multiple_of((1 - ba) * half_rows, 256), half_rows)
    own_quarter = pl.ds(pl.multiple_of(ba * half_rows + aa * quarter, 128), quarter)
    other_quarter = pl.ds(pl.multiple_of(ba * half_rows + (1 - aa) * quarter, 128), quarter)
    flies = len(dev_fly)

    small_steps = [
        remote(small.at[other_half, :], small_c, snd_s.at[0], rcv_s.at[0], dev_c),
        remote(small.at[other_quarter, :], small_x, snd_s.at[1], rcv_s.at[1], dev_x),
    ]
    for k, dev in enumerate(dev_fly):
        small_steps.append(
            remote(small_s.at[k], small_r.at[k], snd_s.at[2 + k], rcv_s.at[2 + k], dev)
        )
    for k, (rows, dev) in enumerate(((own_quarter, dev_x), (own_half, dev_c))):
        region = small_o.at[rows, :]
        n = 2 + flies + k
        small_steps.append(remote(region, region, snd_s.at[n], rcv_s.at[n], dev))

    def small_start(n):
        if n == 2:
            small_s[0] = small[own_quarter, :].astype(BF16)
        small_steps[n].start()

    def small_finish(n):
        if n < 2 + flies:
            small_steps[n].wait()
        if n == 0:
            small[own_half, :] += small_c[...]
        elif n == 1:
            small[own_quarter, :] += small_x[...]
        elif n < 2 + flies:
            total = small_s[n - 2].astype(F32) + small_r[n - 2].astype(F32)
            if n + 1 < 2 + flies:
                small_s[n - 1] = total.astype(BF16)
            else:
                small_o[own_quarter, :] = total.astype(BF16)
        else:
            rows = other_quarter if n == 2 + flies else other_half
            region = small_o.at[rows, :]
            small_steps[n].wait_send()
            remote(region, region, snd_s.at[n], rcv_s.at[n], dev_x).wait_recv()

    small_start(0)
    done = 0
    for t in range(imgs - 2, RING - 1):
        pass_on(t)
        small_finish(done)
        done += 1
        small_start(done)
    while done < len(small_steps):
        small_finish(done)
        done += 1
        if done < len(small_steps):
            small_start(done)

    for copy in keep:
        copy.wait()

    def drain_images(i, carry):
        out_local(i).wait()
        out_remote(i, 1 - aa).wait()
        grad_local(i).wait()
        grad_remote(i, 1 - aa).wait()
        return carry

    lax.fori_loop(0, imgs, drain_images, 0)

    def drain_ring(t, carry):
        for a in range(2):
            across_arrival(t, a).wait()

            @pl.when(t < RING - 1)
            def _():
                for c in range(2):
                    to_ring(t, a, c).wait_send()
                    gather_arrival(t, a, c).wait_send()

        return carry

    lax.fori_loop(0, RING, drain_ring, 0)


def finish_kernel(gim, d2, d1, small, gim_o, w2_o, w1_o, tw1_o, tw2_o, tb1_o, tb2_o, b1_o, *vec_o):
    count, piece, chans = d1.shape
    gim_o[...] = gim[...].astype(F32)
    w2_o[...] = d2[...].reshape(count * piece, chans).astype(F32)
    w1_o[...] = jnp.transpose(d1[...].reshape(count * piece, chans)).astype(F32)

    @pl.when(pl.program_id(0) == 0)
    def _():
        aa, ba = lax.axis_index("aa"), lax.axis_index("ba")
        patches = tw1_o.shape[0]
        tw1_o[...] = small[0:patches, :].astype(F32)
        tw2_o[...] = small[200 : 200 + patches, :].astype(F32)
        tb1_o[...] = small[400:401, :].astype(F32).reshape(tb1_o.shape)
        tb2_o[...] = small[408:409, 0:patches].astype(F32).reshape(patches)
        rows = small[416:424, :].astype(F32)
        rows = jnp.where(ba == 0, rows[:, :piece], rows[:, piece:])
        rows = jnp.concatenate([rows[q : q + 1, :] for q in range(RING)], axis=1)
        b1_o[...] = rows.reshape(b1_o.shape)
        rows = jnp.where(aa == 0, small[424:432, :].astype(F32), small[432:440, :].astype(F32))
        for k, ref in enumerate(vec_o):
            ref[...] = rows[k : k + 1, :].reshape(ref.shape)


def local(groups, images, counts, ln1_gain, ln1_bias, tok_w1, tok_b1, tok_w2, tok_b2,
          ln2_gain, ln2_bias, ch_w1, ch_b1, ch_w2, ch_b2, cotangent):
    slots, patches, half = images.shape
    chans = 2 * half
    imgs = slots // 2
    pad = -(-patches // 16) * 16
    hidden = ch_w1.shape[1]
    piece = hidden // RING
    both = piece - 2 * SOLO
    keep_rows = SOLO + both
    hid_tok = tok_w1.shape[1]
    total = 512
    flies = 3
    while RING * groups > 2**flies:
        flies += 1
    his = max(flies - 3, 1)
    vmem = pl.BlockSpec(memory_space=pltpu.VMEM)
    hbm = pl.BlockSpec(memory_space=pl.ANY)
    dma = pltpu.SemaphoreType.DMA
    per_image = [dma((imgs,))] * 3
    out, gim, d2, d1, small, _ = pl.pallas_call(
        functools.partial(layer_kernel, groups),
        out_shape=[
            jax.ShapeDtypeStruct((slots, patches, half), BF16),
            jax.ShapeDtypeStruct((slots, patches, half), BF16),
            jax.ShapeDtypeStruct((RING, piece, chans), BF16),
            jax.ShapeDtypeStruct((RING, piece, chans), BF16),
            jax.ShapeDtypeStruct((total, hid_tok), BF16),
            jax.ShapeDtypeStruct((his, 2, keep_rows if groups > 1 else 16, chans), BF16),
        ],
        in_specs=[pl.BlockSpec(memory_space=pltpu.SMEM), hbm, hbm]
        + [vmem] * 9
        + [hbm] * 2
        + [vmem],
        out_specs=[hbm] * 4 + [vmem, hbm],
        scratch_shapes=[
            pltpu.VMEM((imgs, patches, chans), BF16),
            pltpu.VMEM((imgs, patches, chans), BF16),
            pltpu.VMEM((imgs, patches, chans), BF16),
            pltpu.VMEM((imgs * pad, chans), BF16),
            pltpu.VMEM((imgs * pad, chans), BF16),
            pltpu.VMEM((imgs, patches, chans), F32),
            pltpu.VMEM((imgs * pad, chans), F32),
            pltpu.VMEM((RING, 2 * piece, chans), BF16),
            pltpu.VMEM((RING, 2 * piece, chans), BF16),
            pltpu.VMEM((RING, imgs * pad, 2 * piece), BF16),
            pltpu.VMEM((RING, imgs * pad, 2 * piece), BF16),
            pltpu.VMEM((imgs, patches, 4), F32),
            pltpu.VMEM((2, 2, 2 * piece, chans), BF16),
            pltpu.VMEM((4, 2, piece, chans), BF16),
            pltpu.VMEM((2, 2, SOLO, chans), BF16),
            pltpu.VMEM((RING, 2, keep_rows, chans), BF16),
            pltpu.VMEM((2, both, chans), BF16),
            pltpu.VMEM((2, 8, half), F32),
            pltpu.VMEM((2, 1, hidden), F32),
            pltpu.VMEM((RING, 2 * piece), F32),
            pltpu.VMEM((hid_tok, 1), F32),
            pltpu.VMEM((patches, 1), F32),
            pltpu.VMEM((8, chans), F32),
            pltpu.VMEM((total, hid_tok), F32),
            pltpu.VMEM((total // 2, hid_tok), F32),
            pltpu.VMEM((total // 4, hid_tok), F32),
            pltpu.VMEM((flies, total // 4, hid_tok), BF16),
            pltpu.VMEM((flies, total // 4, hid_tok), BF16),
            *per_image,
            *per_image,
            dma((5,)),
            dma((4,)),
            dma((4,)),
            dma((4, 2)),
            dma((4, 2)),
            dma((2, 2)),
            dma((2, 2)),
            dma((RING, 2, 2)),
            dma((RING, 2, 2)),
            dma((1 + his, 2, 2)),
            dma((1 + his, 2, 2)),
            dma((RING, 2, 2)),
            dma((RING, 2, 2)),
            dma((RING, 2)),
            dma((RING, 2)),
            dma((2, 2)),
            *per_image,
            *per_image,
            dma((4 + flies,)),
            dma((4 + flies,)),
        ],
        compiler_params=pltpu.CompilerParams(
            collective_id=0, has_side_effects=True, vmem_limit_bytes=65100 * 1024
        ),
    )(
        counts,
        images,
        cotangent,
        ln1_gain,
        ln1_bias,
        ln2_gain,
        ln2_bias,
        ch_b2,
        tok_w1,
        tok_b1,
        tok_w2.T,
        tok_b2,
        ch_w1,
        ch_w2.reshape(RING, piece, chans),
        ch_b1,
    )
    steps = RING // 2
    row = jax.ShapeDtypeStruct((half,), F32)

    def whole(*shape):
        return pl.BlockSpec(shape, lambda k: (0,) * len(shape))

    some = pl.BlockSpec((slots // steps, patches, half), lambda k: (k, 0, 0))
    pair = pl.BlockSpec((2, piece, chans), lambda k: (k, 0, 0))
    gim, w2, w1, tw1, tw2, tb1, tb2, b1, g1, n1, g2, n2, c2 = pl.pallas_call(
        finish_kernel,
        grid=(steps,),
        out_shape=[
            jax.ShapeDtypeStruct((slots, patches, half), F32),
            jax.ShapeDtypeStruct((hidden, chans), F32),
            jax.ShapeDtypeStruct((chans, hidden), F32),
            jax.ShapeDtypeStruct((patches, hid_tok), F32),
            jax.ShapeDtypeStruct((patches, hid_tok), F32),
            jax.ShapeDtypeStruct((hid_tok,), F32),
            jax.ShapeDtypeStruct((patches,), F32),
            jax.ShapeDtypeStruct((hidden,), F32),
        ]
        + [row] * 5,
        in_specs=[some, pair, pair, whole(total, hid_tok)],
        out_specs=[
            some,
            pl.BlockSpec((2 * piece, chans), lambda k: (k, 0)),
            pl.BlockSpec((chans, 2 * piece), lambda k: (0, k)),
            whole(patches, hid_tok),
            whole(patches, hid_tok),
            whole(hid_tok),
            whole(patches),
            whole(hidden),
        ]
        + [whole(half)] * 5,
        compiler_params=pltpu.CompilerParams(vmem_limit_bytes=62 * 2**20),
    )(gim, d2, d1, small)
    return out, gim, g1, n1, tw1, tb1, tw2.T, tb2, g2, n2, w1, b1, w2, c2


def solution(mesh):
    rows = P(("dp", "ba"), None, "aa")
    chan = P("aa")
    placed = (rows, P(("dp", "ba")), chan, chan, P(), P(), P(), P(), chan, chan,
              P(None, "ba"), P("ba"), P("ba", None), chan, rows)
    given = (rows, rows, chan, chan, P(), P(), P(), P(), chan, chan,
             P(None, "ba"), P("ba"), P("ba", None), chan)
    return jax.shard_map(
        functools.partial(local, mesh.shape["dp"] // RING),
        mesh=mesh,
        in_specs=placed,
        out_specs=given,
        check_vma=False,
    )
```

```python
import functools

import jax
import jax.numpy as jnp
from jax import lax
from jax.experimental import pallas as pl
from jax.experimental.pallas import tpu as pltpu
from jax.sharding import PartitionSpec as P

MESH = pl.DeviceIdType.MESH
EPS = 1e-06
C0 = 0.7978845608028654
C1 = C0 * 0.044715
RING = 8
LOOK = 3
SOLO = 32
F32 = jnp.float32
BF16 = jnp.bfloat16


def dot(left, right, left_dim, right_dim):
    return lax.dot_general(
        left, right, (((left_dim,), (right_dim,)), ((), ())), preferred_element_type=F32
    )


def gelu(v):
    return v * (0.5 * jnp.tanh(v * (C0 + C1 * (v * v))) + 0.5)


def gelu_both(v):
    v2 = v * v
    h = 0.5 * jnp.tanh(v * (C0 + C1 * v2)) + 0.5
    return v * h, h + (h - h * h) * (v * (2 * C0 + 6 * C1 * v2))


def mod(v):
    return lax.rem(v + 2 * RING, RING)


def flip(index, step):
    return index + step - 2 * step * lax.rem(lax.div(index, step), 2)


def column(row, length):
    return jnp.transpose(jnp.broadcast_to(row.reshape(1, length), (8, length)))[:, 0:1]


def layer_kernel(
    groups,
    counts,
    images,
    cot,
    gain1,
    bias1,
    gain2,
    bias2,
    biasc,
    tw1,
    tb1,
    tw2,
    tb2,
    w1_own,
    w2_own,
    b1_own,
    out_o,
    gim_o,
    d2_o,
    d1_o,
    small_o,
    xh,
    xb,
    cb,
    y2b,
    gb,
    res,
    acc,
    w1b,
    w2b,
    act,
    dg,
    stat,
    pb,
    bar,
    xr,
    held,
    rs,
    xs,
    fs,
    vecb,
    b1h,
    b1v,
    t1v,
    t2v,
    vacc,
    small,
    small_c,
    small_x,
    small_s,
    small_r,
    loc_x,
    snd_x,
    rcv_x,
    loc_c,
    snd_c,
    rcv_c,
    loc_w,
    snd_w,
    rcv_w,
    snd_b,
    rcv_b,
    snd_h,
    rcv_h,
    snd_r,
    rcv_r,
    snd_e,
    rcv_e,
    snd_g,
    rcv_g,
    loc_g,
    loc_o,
    snd_o,
    rcv_o,
    loc_i,
    snd_i,
    rcv_i,
    snd_s,
    rcv_s,
):
    _, imgs, patches, half = xb.shape
    chans = 2 * half
    pad = y2b.shape[0] // imgs
    piece = w2_own.shape[1]
    both = piece - 2 * SOLO
    dp, aa, ba = lax.axis_index("dp"), lax.axis_index("aa"), lax.axis_index("ba")
    lo, hi = lax.rem(dp, RING), lax.div(dp, RING)
    pos = jnp.where(lax.rem(lo, 2) == 0, lax.div(lo, 2), RING - 1 - lax.div(lo, 2))

    def at(place):
        place = mod(place)
        return hi * RING + jnp.where(
            place < RING // 2, 2 * place, 2 * (RING - 1 - place) + 1
        )

    dev_x = (dp, 1 - aa, ba)
    dev_c = (dp, aa, 1 - ba)
    dev_ring = ((at(pos + 1), aa, ba), (at(pos - 1), aa, ba))
    dev_fly = []
    step = 1
    while step < RING * groups:
        dev_fly.append((flip(dp, step), aa, ba))
        step *= 2
    dev_hi = dev_fly[3:]
    peers = [dev_x, dev_c, *dev_ring, *dev_fly]
    barrier = pltpu.get_barrier_semaphore()
    for peer in peers:
        pl.semaphore_signal(barrier, inc=1, device_id=peer, device_id_type=MESH)

    rows_mine = pl.ds(pl.multiple_of(ba * piece, 64), piece)
    rows_other = pl.ds(pl.multiple_of((1 - ba) * piece, 64), piece)

    def remote(src, dst, send, recv, dev):
        return pltpu.make_async_remote_copy(
            src_ref=src,
            dst_ref=dst,
            send_sem=send,
            recv_sem=recv,
            device_id=dev,
            device_id_type=MESH,
        )

    def local_in(src, dst, sem, i):
        return pltpu.make_async_copy(src.at[aa * imgs + i], dst.at[aa, i], sem.at[i])

    def give(src, dst, send, recv, i):
        return remote(
            src.at[(1 - aa) * imgs + i], dst.at[aa, i], send.at[i], recv.at[i], dev_x
        )

    def take(src, dst, send, recv, i):
        return remote(
            src.at[(1 - aa) * imgs + i], dst.at[1 - aa, i], send.at[i], recv.at[i], dev_x
        )

    def wide(ref, i):
        return jnp.concatenate([ref[0, i], ref[1, i]], axis=1).astype(F32)

    def put(ref, i, rows):
        rows = rows.astype(BF16)
        ref[0, i] = rows[:, :half]
        ref[1, i] = rows[:, half:]

    cols = 2 * piece
    parts = w1_own.shape[1] // cols

    def w1_in(k):
        return pltpu.make_async_copy(
            w1_own.at[:, pl.ds(k * cols, cols)], act.at[k, pl.ds(0, chans), :], loc_w.at[1 + k]
        )

    for k in range(parts):
        w1_in(k).start()
    for i in range(imgs):
        local_in(images, xb, loc_x, i).start()
    w2_local = pltpu.make_async_copy(w2_own, w2b.at[:, rows_mine, :], loc_w.at[0])
    w2_local.start()
    for i in range(imgs):
        local_in(cot, cb, loc_c, i).start()
    for k, ref in enumerate((gain1, bias1, gain2, bias2, biasc)):
        vecb[aa, k : k + 1, :] = ref[...].reshape(1, half)
    b1h[ba] = b1_own[...].reshape(1, parts * cols)

    pl.semaphore_wait(barrier, len(peers))

    vec_copy = remote(vecb.at[aa], vecb.at[aa], snd_w.at[2], rcv_w.at[2], dev_x)
    vec_copy.start()
    for i in range(LOOK):
        give(images, xb, snd_x, rcv_x, i).start()
    b1_copy = remote(b1h.at[ba], b1h.at[ba], snd_w.at[3], rcv_w.at[3], dev_c)
    b1_copy.start()
    w2_copy = remote(w2_own, w2b.at[:, rows_mine, :], snd_w.at[0], rcv_w.at[0], dev_c)
    w2_copy.start()
    y2b[...] = jnp.zeros(y2b.shape, BF16)
    gb[...] = jnp.zeros(gb.shape, BF16)
    vacc[...] = jnp.zeros(vacc.shape, F32)
    small[...] = jnp.zeros(small.shape, F32)
    t1v[...] = column(tb1[...], t1v.shape[0])
    t2v[...] = column(tb2[...], patches)
    for k in range(parts):
        w1_in(k).wait()
        turned = jnp.transpose(act[k, 0:chans, :])
        w1b[2 * k, rows_mine, :] = turned[:piece]
        w1b[2 * k + 1, rows_mine, :] = turned[piece:]
    w1_copy = remote(
        w1b.at[:, rows_mine, :], w1b.at[:, rows_mine, :], snd_w.at[1], rcv_w.at[1], dev_c
    )
    w1_copy.start()
    vec_copy.wait_send()
    remote(vecb.at[aa], vecb.at[1 - aa], snd_w.at[2], rcv_w.at[2], dev_x).wait_recv()
    b1_copy.wait_send()
    remote(b1h.at[ba], b1h.at[1 - ba], snd_w.at[3], rcv_w.at[3], dev_c).wait_recv()
    for q in range(RING):
        b1v[q : q + 1, :] = jnp.concatenate(
            [b1h[0, :, q * piece : (q + 1) * piece], b1h[1, :, q * piece : (q + 1) * piece]],
            axis=1,
        )

    def vec(k):
        return jnp.concatenate([vecb[0, k : k + 1, :], vecb[1, k : k + 1, :]], axis=1)

    def token_forward(i):
        local_in(images, xb, loc_x, i).wait()
        take(images, xb, snd_x, rcv_x, i).wait()

        @pl.when(i + LOOK < imgs)
        def _():
            give(images, xb, snd_x, rcv_x, i + LOOK).start()

        @pl.when(i + LOOK >= imgs)
        def _():
            give(cot, cb, snd_c, rcv_c, i + LOOK - imgs).start()

        @pl.when(i == imgs - 1)
        def _():
            for n in range(LOOK, imgs):
                give(cot, cb, snd_c, rcv_c, n).start()

        x = wide(xb, i)
        mean = jnp.mean(x, -1, keepdims=True)
        xc = x - mean
        rstd = lax.rsqrt(jnp.mean(xc * xc, -1, keepdims=True) + EPS)
        stat[i, :, 0 : 1] = mean
        stat[i, :, 1 : 2] = rstd
        y1 = (xc * rstd * vec(0) + vec(1)).astype(BF16)
        hid = gelu(dot(tw1[...], y1, 0, 0) + t1v[...]).astype(BF16)
        row = x + dot(tw2[...], hid, 1, 0) + t2v[...]
        res[i] = row
        mean = jnp.mean(row, -1, keepdims=True)
        xc = row - mean
        rstd = lax.rsqrt(jnp.mean(xc * xc, -1, keepdims=True) + EPS)
        stat[i, :, 2 : 3] = mean
        stat[i, :, 3 : 4] = rstd
        y2 = (xc * rstd * vec(2) + vec(3)).astype(BF16)
        y2b[pl.ds(pl.multiple_of(i * pad, 16), patches), :] = y2

    def weight(i):
        return jnp.where(aa * imgs + i < counts[0], 1.0, 0.0).astype(F32)

    chunks = 3
    size = y2b.shape[0] // chunks
    each = imgs // chunks

    def chan_forward(chunk, pair):
        rows = pl.ds(pl.multiple_of(chunk * size, 16), size)
        win = w1b[pl.ds(2 * pair, 2)].reshape(2 * cols, chans)
        wout = w2b[pl.ds(2 * pair, 2)].reshape(2 * cols, chans)
        bias = jnp.concatenate(
            [b1v[pl.ds(2 * pair, 1), :], b1v[pl.ds(2 * pair + 1, 1), :]], axis=1
        )
        val, der = gelu_both(dot(y2b[rows, :], win, 1, 1) + bias)
        val = val.astype(BF16)
        der = der.astype(BF16)
        act[2 * pair, rows, :] = val[:, :cols]
        act[2 * pair + 1, rows, :] = val[:, cols:]
        dg[2 * pair, rows, :] = der[:, :cols]
        dg[2 * pair + 1, rows, :] = der[:, cols:]
        new = dot(val, wout, 1, 0)
        acc[rows, :] = jnp.where(pair == 0, 0.0, acc[rows, :]) + new

    def forward_chunk(chunk, carry):
        def one(k, carry):
            token_forward(chunk * each + k)
            return carry

        lax.fori_loop(0, each, one, 0)

        @pl.when(chunk == 0)
        def _():
            w2_local.wait()
            w2_copy.wait_send()
            remote(
                w2_own, w2b.at[:, rows_other, :], snd_w.at[0], rcv_w.at[0], dev_c
            ).wait_recv()
            w1_copy.wait_send()
            remote(
                w1b.at[:, rows_mine, :], w1b.at[:, rows_other, :], snd_w.at[1], rcv_w.at[1], dev_c
            ).wait_recv()

        def two(k, carry):
            chan_forward(chunk, k)
            return carry

        lax.fori_loop(0, RING // 2, two, 0)
        return carry

    lax.fori_loop(0, chunks, forward_chunk, 0)
    def out_local(i):
        return pltpu.make_async_copy(cb.at[aa, i], out_o.at[aa * imgs + i], loc_o.at[i])

    def out_remote(i, sender):
        return remote(
            cb.at[1 - aa, i], out_o.at[sender * imgs + i], snd_o.at[i], rcv_o.at[i], dev_x
        )

    def mask_cot(i, carry):
        local_in(cot, cb, loc_c, i).wait()
        take(cot, cb, snd_c, rcv_c, i).wait()
        rows = pl.ds(pl.multiple_of(i * pad, 16), patches)
        scale = weight(i)
        gb[rows, :] = (wide(cb, i) * scale).astype(BF16)
        put(cb, i, scale * (res[i] + acc[rows, :] + vec(4)))
        return carry

    lax.fori_loop(0, imgs, mask_cot, 0)

    def grad_local(i):
        return pltpu.make_async_copy(xb.at[aa, i], gim_o.at[aa * imgs + i], loc_i.at[i])

    def grad_remote(i, sender):
        return remote(
            xb.at[1 - aa, i], gim_o.at[sender * imgs + i], snd_i.at[i], rcv_i.at[i], dev_x
        )

    ones = jnp.ones((8, chans), BF16)

    def token_backward(i):
        rows = pl.ds(pl.multiple_of(i * pad, 16), patches)
        up = acc[rows, :]
        grad_out = gb[rows, :].astype(F32)
        rstd = stat[i, :, 3 : 4]
        normed = (res[i] - stat[i, :, 2 : 3]) * rstd
        vacc[2:3, :] += jnp.sum(up * normed, 0, keepdims=True)
        vacc[3:4, :] += jnp.sum(up, 0, keepdims=True)
        vacc[4:5, :] += jnp.sum(grad_out, 0, keepdims=True)
        q = up * vec(2)
        mean = jnp.mean(q, -1, keepdims=True)
        proj = jnp.mean(q * normed, -1, keepdims=True)
        grad_res = grad_out + rstd * (q - mean - normed * proj)
        grad_tok = grad_res.astype(BF16)
        rstd = stat[i, :, 1 : 2]
        normed = (wide(xb, i) - stat[i, :, 0 : 1]) * rstd
        y1 = (normed * vec(0) + vec(1)).astype(BF16)
        val, der = gelu_both(dot(tw1[...], y1, 0, 0) + t1v[...])
        small[200 : 200 + patches, :] += dot(grad_tok, val.astype(BF16), 1, 1)
        small[408:416, 0:patches] += dot(ones, grad_tok, 1, 1)
        grad_pre = (dot(tw2[...], grad_tok, 0, 0) * der).astype(BF16)
        small[0:patches, :] += dot(y1, grad_pre, 1, 1)
        small[400:408, :] += dot(ones, grad_pre, 1, 1)
        up = dot(tw1[...], grad_pre, 1, 0)
        vacc[0:1, :] += jnp.sum(up * normed, 0, keepdims=True)
        vacc[1:2, :] += jnp.sum(up, 0, keepdims=True)
        q = up * vec(0)
        mean = jnp.mean(q, -1, keepdims=True)
        proj = jnp.mean(q * normed, -1, keepdims=True)
        put(xb, i, grad_res + rstd * (q - mean - normed * proj))
        grad_local(i).start()
        grad_remote(i, aa).start()

    bars = bar.shape[0]
    solo_mine = pl.ds(pl.multiple_of(aa * SOLO, 16), SOLO)
    solo_other = pl.ds(pl.multiple_of((1 - aa) * SOLO, 16), SOLO)

    def own_rows(place, size):
        return pl.ds(pl.multiple_of(ba * piece + place, 16), size)

    def to_core(s, par, a):
        return remote(
            pb.at[par, a, rows_other, :],
            bar.at[lax.rem(s, bars), a],
            snd_b.at[lax.rem(s, bars), a],
            rcv_b.at[lax.rem(s, bars), a],
            dev_c,
        )

    def to_x(s, a):
        slot = lax.rem(s, bars)
        return remote(
            bar.at[slot, a, solo_other, :],
            xr.at[slot, a],
            snd_h.at[slot, a],
            rcv_h.at[slot, a],
            dev_x,
        )

    part = both // 2
    ring_rows = (pl.ds(0, SOLO), pl.ds(SOLO, part), pl.ds(SOLO + part, part))
    own_at = (aa * SOLO, 2 * SOLO, 2 * SOLO + part)
    order = (1, 2, 0)
    last = RING - 1

    def to_ring(s, a, c):
        return remote(
            rs.at[s, a, ring_rows[c], :],
            rs.at[s + 1, a, ring_rows[c], :],
            snd_r.at[s, a, c],
            rcv_r.at[s, a, c],
            dev_ring[a],
        )

    def swap(a, c):
        src = rs.at[last, a, ring_rows[c], :]
        dst = fs.at[a, solo_mine, :] if c == 0 else xs.at[a, pl.ds((c - 1) * part, part), :]
        return remote(src, dst, snd_e.at[0, a, c], rcv_e.at[0, a, c], dev_x)

    def first_sum(s, par, wait=True):
        slot = lax.rem(s, bars)
        for a in range(2):
            if wait:
                to_core(s, par, a).wait_recv()
            own = own_rows((1 - aa) * SOLO, SOLO)
            total = pb[par, a, own, :].astype(F32) + bar[slot, a, solo_other, :].astype(F32)
            bar[slot, a, solo_other, :] = total.astype(BF16)
            to_x(s, a).start()
            own = own_rows(aa * SOLO, SOLO)
            held[par, a] = pb[par, a, own, :].astype(F32) + bar[slot, a, solo_mine, :].astype(F32)

    def pass_sum(s, a, c, total, first, final):
        if not first:
            to_ring(s - 1, a, c).wait_recv()
            total = total + rs[s, a, ring_rows[c], :].astype(F32)
        total = total.astype(BF16)
        rs[s, a, ring_rows[c], :] = total
        if not final:
            to_ring(s, a, c).start()
        else:
            if c == 0:
                fs[a, solo_mine, :] = total
            swap(a, c).start()

    def shared_sum(s, par, a, first=False, final=False):
        slot = lax.rem(s, bars)
        for c in (1, 2):
            total = pb[par, a, own_rows(own_at[c], part), :].astype(F32)
            total = total + bar[slot, a, pl.ds(own_at[c], part), :].astype(F32)
            pass_sum(s, a, c, total, first, final)

    def solo_sum(s, par, first=False, final=False):
        for a in range(2):
            to_x(s, a).wait()
            total = held[par, a] + xr[lax.rem(s, bars), a].astype(F32)
            pass_sum(s, a, 0, total, first, final)

    def lefts(k):
        return mod(pos + 1 + 2 * k), mod(pos + 2 + 2 * k)

    def grad_hidden(k):
        pair = lefts(k)
        rows = jnp.concatenate([w2b[n] for n in pair], axis=0)
        slope = jnp.concatenate([dg[n] for n in pair], axis=1).astype(F32)
        grad = (dot(gb[...], rows, 1, 1) * slope).astype(BF16)
        total = jnp.sum(grad.astype(F32), 0, keepdims=True)
        for n, left in enumerate(pair):
            dg[left] = grad[:, n * cols : (n + 1) * cols]
            small[pl.ds(416 + left, 1), :] = total[:, n * cols : (n + 1) * cols]

    def grad_rows(k, first=False):
        pair = lefts(k)
        grad = jnp.concatenate([dg[n] for n in pair], axis=1)
        new = dot(grad, jnp.concatenate([w1b[n] for n in pair], axis=0), 1, 0)
        acc[...] = new if first else acc[...] + new

    def weight_out(j, par):
        pb[par, 0] = dot(act[mod(pos - 1 - j)], gb[...], 0, 0).astype(BF16)
        to_core(j, par, 0).start()

    def weight_in(j, par):
        pb[par, 1] = dot(dg[mod(pos + 1 + j)], y2b[...], 0, 0).astype(BF16)
        to_core(j, par, 1).start()

    def sent_to_core(j, par):
        for a in range(2):
            to_core(j, par, a).wait_send()

    def send_out(i):
        out_local(i).start()
        out_remote(i, aa).start()

    weight_out(0, 0)
    grad_hidden(0)
    weight_in(0, 0)
    to_core(0, 0, 0).wait_recv()
    shared_sum(0, 0, 0, first=True)
    weight_out(1, 1)
    to_core(0, 0, 1).wait_recv()
    shared_sum(0, 0, 1, first=True)
    first_sum(0, 0, wait=False)
    weight_in(1, 1)
    grad_hidden(1)
    first_sum(1, 1)

    def chan_backward(k, carry):
        sent_to_core(2 * k - 2, 0)
        weight_out(2 * k, 0)
        weight_in(2 * k, 0)
        shared_sum(2 * k - 1, 1, 0)
        shared_sum(2 * k - 1, 1, 1)

        @pl.when(k == 1)
        def _():
            solo_sum(0, 0, first=True)
            grad_rows(0, first=True)

        @pl.when(k > 1)
        def _():
            solo_sum(2 * k - 2, 0)
            grad_rows(k - 1)

        send_out(2 * k - 2)
        first_sum(2 * k, 0)
        sent_to_core(2 * k - 1, 1)
        weight_out(2 * k + 1, 1)
        weight_in(2 * k + 1, 1)
        shared_sum(2 * k, 0, 0)
        shared_sum(2 * k, 0, 1)
        solo_sum(2 * k - 1, 1)
        send_out(2 * k - 1)

        @pl.when(k + 1 < RING // 2)
        def _():
            grad_hidden(k + 1)

        @pl.when(k + 1 == RING // 2)
        def _():
            grad_rows(k)

        first_sum(2 * k + 1, 1)
        return carry

    lax.fori_loop(1, RING // 2, chan_backward, 0)

    results = (d2_o, d1_o)
    gather_rows = (pl.ds(0, 2 * SOLO), pl.ds(2 * SOLO, part), pl.ds(2 * SOLO + part, part))

    def gather(t, a, c, src):
        q = mod(pos - t) if a == 0 else mod(pos + t)
        dst = results[a].at[q, gather_rows[c], :]
        return remote(
            dst if src is None else src, dst, snd_g.at[t, a, c], rcv_g.at[t, a, c], dev_ring[a]
        )

    def gather_arrival(t, a, c):
        q = mod(pos - 1 - t) if a == 0 else mod(pos + 1 + t)
        dst = results[a].at[q, gather_rows[c], :]
        return remote(dst, dst, snd_g.at[t, a, c], rcv_g.at[t, a, c], dev_ring[a])

    def keep(a, c):
        return pltpu.make_async_copy(
            fs.at[a, gather_rows[c], :], results[a].at[pos, gather_rows[c], :], loc_g.at[a, c]
        )

    def start_gather(c):
        for a in range(2):
            rows = gather_rows[c]
            swap(a, c).wait_send()
            if c == 0:
                remote(
                    fs.at[a, solo_mine, :],
                    fs.at[a, solo_other, :],
                    snd_e.at[0, a, c],
                    rcv_e.at[0, a, c],
                    dev_x,
                ).wait_recv()
            else:
                swap(a, c).wait_recv()
                fs[a, rows, :] = (
                    rs[last, a, ring_rows[c], :].astype(F32)
                    + xs[a, (c - 1) * part : c * part, :].astype(F32)
                ).astype(BF16)
            for k, dev in enumerate(dev_hi):
                src = fs.at[a, rows, :]
                landed = xh.at[k, a, rows, :]
                near = pb.at[0, 0, rows, :]
                copy = remote(src, landed, snd_e.at[1 + k, a, c], rcv_e.at[1 + k, a, c], dev)
                copy.start()
                copy.wait()
                back = pltpu.make_async_copy(landed, near, loc_g.at[a, c])
                back.start()
                back.wait()
                fs[a, rows, :] = (
                    fs[a, rows, :].astype(F32) + pb[0, 0, rows, :].astype(F32)
                ).astype(BF16)
            gather(0, a, c, fs.at[a, rows, :]).start()
            keep(a, c).start()

    def pass_on(t):
        for c in order:
            for a in range(2):
                gather_arrival(t, a, c).wait_recv()
                if t + 1 < RING - 1:
                    gather(t + 1, a, c, None).start()

    def token_and_gather(i, carry):
        token_backward(i)

        @pl.when(i == 0)
        def _():
            sent_to_core(RING - 2, 0)
            sent_to_core(last, 1)
            for a in range(2):
                shared_sum(last, 1, a, final=True)
            solo_sum(RING - 2, 0)
            solo_sum(last, 1, final=True)

        @pl.when(i == 1)
        def _():
            start_gather(1)

        @pl.when(i == 3)
        def _():
            start_gather(2)
            start_gather(0)

        return carry

    lax.fori_loop(0, imgs, token_and_gather, 0)
    small[424:432, :] = vacc[:, :half]
    small[432:440, :] = vacc[:, half:]

    total_rows = small.shape[0]
    half_rows, quarter = total_rows // 2, total_rows // 4
    own_half = pl.ds(pl.multiple_of(ba * half_rows, 256), half_rows)
    other_half = pl.ds(pl.multiple_of((1 - ba) * half_rows, 256), half_rows)
    own_quarter = pl.ds(pl.multiple_of(ba * half_rows + aa * quarter, 128), quarter)
    other_quarter = pl.ds(pl.multiple_of(ba * half_rows + (1 - aa) * quarter, 128), quarter)
    flies = len(dev_fly)

    small_steps = [
        remote(small.at[other_half, :], small_c, snd_s.at[0], rcv_s.at[0], dev_c),
        remote(small.at[other_quarter, :], small_x, snd_s.at[1], rcv_s.at[1], dev_x),
    ]
    for k, dev in enumerate(dev_fly):
        small_steps.append(
            remote(small_s.at[k], small_r.at[k], snd_s.at[2 + k], rcv_s.at[2 + k], dev)
        )
    for k, (rows, dev) in enumerate(((own_quarter, dev_x), (own_half, dev_c))):
        region = small_o.at[rows, :]
        n = 2 + flies + k
        small_steps.append(remote(region, region, snd_s.at[n], rcv_s.at[n], dev))

    def small_start(n):
        if n == 2:
            small_s[0] = small[own_quarter, :].astype(BF16)
        small_steps[n].start()

    def small_finish(n):
        if n < 2 + flies:
            small_steps[n].wait()
        if n == 0:
            small[own_half, :] += small_c[...]
        elif n == 1:
            small[own_quarter, :] += small_x[...]
        elif n < 2 + flies:
            total = small_s[n - 2].astype(F32) + small_r[n - 2].astype(F32)
            if n + 1 < 2 + flies:
                small_s[n - 1] = total.astype(BF16)
            else:
                small_o[own_quarter, :] = total.astype(BF16)
        else:
            rows = other_quarter if n == 2 + flies else other_half
            region = small_o.at[rows, :]
            small_steps[n].wait_send()
            remote(region, region, snd_s.at[n], rcv_s.at[n], dev_x).wait_recv()

    small_start(0)
    for t in range(RING - 1):
        pass_on(t)
        small_finish(t)
        if t + 1 < len(small_steps):
            small_start(t + 1)
    for n in range(RING - 1, len(small_steps)):
        small_finish(n)
        if n + 1 < len(small_steps):
            small_start(n + 1)

    for a in range(2):
        for c in range(3):
            keep(a, c).wait()

    def drain_images(i, carry):
        out_local(i).wait()
        out_remote(i, 1 - aa).wait()
        grad_local(i).wait()
        grad_remote(i, 1 - aa).wait()
        return carry

    lax.fori_loop(0, imgs, drain_images, 0)

    def drain_ring(t, carry):
        for a in range(2):
            for c in range(3):
                to_ring(t, a, c).wait_send()
                gather_arrival(t, a, c).wait_send()
        return carry

    lax.fori_loop(0, RING - 1, drain_ring, 0)


def finish_kernel(gim, d2, d1, small, gim_o, w2_o, w1_o, tw1_o, tw2_o, tb1_o, tb2_o, b1_o, *vec_o):
    count, piece, chans = d1.shape
    gim_o[...] = gim[...].astype(F32)
    w2_o[...] = d2[...].reshape(count * piece, chans).astype(F32)
    w1_o[...] = jnp.transpose(d1[...].reshape(count * piece, chans)).astype(F32)

    @pl.when(pl.program_id(0) == 0)
    def _():
        aa, ba = lax.axis_index("aa"), lax.axis_index("ba")
        patches = tw1_o.shape[0]
        tw1_o[...] = small[0:patches, :].astype(F32)
        tw2_o[...] = small[200 : 200 + patches, :].astype(F32)
        tb1_o[...] = small[400:401, :].astype(F32).reshape(tb1_o.shape)
        tb2_o[...] = small[408:409, 0:patches].astype(F32).reshape(patches)
        rows = small[416:424, :].astype(F32)
        rows = jnp.where(ba == 0, rows[:, :piece], rows[:, piece:])
        rows = jnp.concatenate([rows[q : q + 1, :] for q in range(RING)], axis=1)
        b1_o[...] = rows.reshape(b1_o.shape)
        rows = jnp.where(aa == 0, small[424:432, :].astype(F32), small[432:440, :].astype(F32))
        for k, ref in enumerate(vec_o):
            ref[...] = rows[k : k + 1, :].reshape(ref.shape)


def local(groups, images, counts, ln1_gain, ln1_bias, tok_w1, tok_b1, tok_w2, tok_b2,
          ln2_gain, ln2_bias, ch_w1, ch_b1, ch_w2, ch_b2, cotangent):
    slots, patches, half = images.shape
    chans = 2 * half
    imgs = slots // 2
    pad = -(-patches // 16) * 16
    hidden = ch_w1.shape[1]
    piece = hidden // RING
    both = piece - 2 * SOLO
    keep_rows = SOLO + both
    hid_tok = tok_w1.shape[1]
    total = 512
    flies = 3
    while RING * groups > 2**flies:
        flies += 1
    his = max(flies - 3, 1)
    vmem = pl.BlockSpec(memory_space=pltpu.VMEM)
    hbm = pl.BlockSpec(memory_space=pl.ANY)
    dma = pltpu.SemaphoreType.DMA
    per_image = [dma((imgs,))] * 3
    out, gim, d2, d1, small, _ = pl.pallas_call(
        functools.partial(layer_kernel, groups),
        out_shape=[
            jax.ShapeDtypeStruct((slots, patches, half), BF16),
            jax.ShapeDtypeStruct((slots, patches, half), BF16),
            jax.ShapeDtypeStruct((RING, piece, chans), BF16),
            jax.ShapeDtypeStruct((RING, piece, chans), BF16),
            jax.ShapeDtypeStruct((total, hid_tok), BF16),
            jax.ShapeDtypeStruct((his, 2, piece if groups > 1 else 16, chans), BF16),
        ],
        in_specs=[pl.BlockSpec(memory_space=pltpu.SMEM), hbm, hbm]
        + [vmem] * 9
        + [hbm] * 2
        + [vmem],
        out_specs=[hbm] * 4 + [vmem, hbm],
        scratch_shapes=[
            pltpu.VMEM((2, imgs, patches, half), BF16),
            pltpu.VMEM((2, imgs, patches, half), BF16),
            pltpu.VMEM((imgs * pad, chans), BF16),
            pltpu.VMEM((imgs * pad, chans), BF16),
            pltpu.VMEM((imgs, patches, chans), F32),
            pltpu.VMEM((imgs * pad, chans), F32),
            pltpu.VMEM((RING, 2 * piece, chans), BF16),
            pltpu.VMEM((RING, 2 * piece, chans), BF16),
            pltpu.VMEM((RING, imgs * pad, 2 * piece), BF16),
            pltpu.VMEM((RING, imgs * pad, 2 * piece), BF16),
            pltpu.VMEM((imgs, patches, 4), F32),
            pltpu.VMEM((2, 2, 2 * piece, chans), BF16),
            pltpu.VMEM((4, 2, piece, chans), BF16),
            pltpu.VMEM((4, 2, SOLO, chans), BF16),
            pltpu.VMEM((2, 2, SOLO, chans), F32),
            pltpu.VMEM((RING, 2, keep_rows, chans), BF16),
            pltpu.VMEM((2, both, chans), BF16),
            pltpu.VMEM((2, piece, chans), BF16),
            pltpu.VMEM((2, 8, half), F32),
            pltpu.VMEM((2, 1, hidden), F32),
            pltpu.VMEM((RING, 2 * piece), F32),
            pltpu.VMEM((hid_tok, 1), F32),
            pltpu.VMEM((patches, 1), F32),
            pltpu.VMEM((8, chans), F32),
            pltpu.VMEM((total, hid_tok), F32),
            pltpu.VMEM((total // 2, hid_tok), F32),
            pltpu.VMEM((total // 4, hid_tok), F32),
            pltpu.VMEM((flies, total // 4, hid_tok), BF16),
            pltpu.VMEM((flies, total // 4, hid_tok), BF16),
            *per_image,
            *per_image,
            dma((5,)),
            dma((4,)),
            dma((4,)),
            dma((4, 2)),
            dma((4, 2)),
            dma((4, 2)),
            dma((4, 2)),
            dma((RING, 2, 3)),
            dma((RING, 2, 3)),
            dma((1 + his, 2, 3)),
            dma((1 + his, 2, 3)),
            dma((RING, 2, 3)),
            dma((RING, 2, 3)),
            dma((2, 3)),
            *per_image,
            *per_image,
            dma((4 + flies,)),
            dma((4 + flies,)),
        ],
        compiler_params=pltpu.CompilerParams(
            collective_id=0, has_side_effects=True, vmem_limit_bytes=65100 * 1024
        ),
    )(
        counts,
        images,
        cotangent,
        ln1_gain,
        ln1_bias,
        ln2_gain,
        ln2_bias,
        ch_b2,
        tok_w1,
        tok_b1,
        tok_w2.T,
        tok_b2,
        ch_w1,
        ch_w2.reshape(RING, piece, chans),
        ch_b1,
    )
    steps = RING // 2
    row = jax.ShapeDtypeStruct((half,), F32)

    def whole(*shape):
        return pl.BlockSpec(shape, lambda k: (0,) * len(shape))

    some = pl.BlockSpec((slots // steps, patches, half), lambda k: (k, 0, 0))
    pair = pl.BlockSpec((2, piece, chans), lambda k: (k, 0, 0))
    gim, w2, w1, tw1, tw2, tb1, tb2, b1, g1, n1, g2, n2, c2 = pl.pallas_call(
        finish_kernel,
        grid=(steps,),
        out_shape=[
            jax.ShapeDtypeStruct((slots, patches, half), F32),
            jax.ShapeDtypeStruct((hidden, chans), F32),
            jax.ShapeDtypeStruct((chans, hidden), F32),
            jax.ShapeDtypeStruct((patches, hid_tok), F32),
            jax.ShapeDtypeStruct((patches, hid_tok), F32),
            jax.ShapeDtypeStruct((hid_tok,), F32),
            jax.ShapeDtypeStruct((patches,), F32),
            jax.ShapeDtypeStruct((hidden,), F32),
        ]
        + [row] * 5,
        in_specs=[some, pair, pair, whole(total, hid_tok)],
        out_specs=[
            some,
            pl.BlockSpec((2 * piece, chans), lambda k: (k, 0)),
            pl.BlockSpec((chans, 2 * piece), lambda k: (0, k)),
            whole(patches, hid_tok),
            whole(patches, hid_tok),
            whole(hid_tok),
            whole(patches),
            whole(hidden),
        ]
        + [whole(half)] * 5,
        compiler_params=pltpu.CompilerParams(vmem_limit_bytes=62 * 2**20),
    )(gim, d2, d1, small)
    return out, gim, g1, n1, tw1, tb1, tw2.T, tb2, g2, n2, w1, b1, w2, c2


def solution(mesh):
    rows = P(("dp", "ba"), None, "aa")
    chan = P("aa")
    placed = (rows, P(("dp", "ba")), chan, chan, P(), P(), P(), P(), chan, chan,
              P(None, "ba"), P("ba"), P("ba", None), chan, rows)
    given = (rows, rows, chan, chan, P(), P(), P(), P(), chan, chan,
             P(None, "ba"), P("ba"), P("ba", None), chan)
    return jax.shard_map(
        functools.partial(local, mesh.shape["dp"] // RING),
        mesh=mesh,
        in_specs=placed,
        out_specs=given,
        check_vma=False,
    )
```

```python
import functools

import jax
import jax.numpy as jnp
from jax import lax
from jax.experimental import pallas as pl
from jax.experimental.pallas import tpu as pltpu
from jax.sharding import PartitionSpec as P

MESH = pl.DeviceIdType.MESH
EPS = 1e-06
C0 = 0.7978845608028654
C1 = C0 * 0.044715
RING = 8
LOOK = 3
SOLO = 48
SLOTS = 2
SMALL_STEPS = 7
PLAN = (
    ("D", 0), ("G", 0), ("I", 0), ("S", 0, 0, 1), ("S", 0, 0, 2), ("F", 0, 0), ("D", 1), ("I", 1),
    ("S", 0, 1, 1), ("S", 0, 1, 2), ("F", 0, 1), ("D", 2), ("S", 1, 0, 1), ("Z", 0, 0),
    ("F", 1, 0), ("G", 1), ("S", 1, 1, 1), ("S", 1, 0, 2), ("Z", 0, 1), ("F", 1, 1), ("F", 2, 0),
    ("I", 2), ("S", 1, 1, 2), ("S", 2, 0, 1), ("D", 3), ("Z", 1, 0), ("O", 0), ("I", 3),
    ("S", 2, 1, 1), ("F", 2, 1), ("S", 2, 0, 2), ("G", 2), ("S", 3, 0, 1), ("Z", 1, 1),
    ("F", 3, 0), ("S", 2, 1, 2), ("F", 3, 1), ("D", 4), ("Z", 2, 0), ("S", 3, 1, 1), ("I", 4),
    ("S", 3, 0, 2), ("G", 3), ("S", 4, 0, 1), ("Z", 2, 1), ("S", 3, 1, 2), ("F", 4, 0),
    ("F", 4, 1), ("D", 5), ("Z", 3, 0), ("S", 4, 1, 1), ("I", 5), ("S", 4, 0, 2), ("Y", 0),
    ("S", 5, 0, 1), ("Z", 3, 1), ("F", 5, 0), ("S", 4, 1, 2), ("F", 5, 1), ("D", 6), ("Z", 4, 0),
    ("S", 5, 1, 1), ("I", 6), ("S", 5, 0, 2), ("O", 1), ("Y", 1), ("S", 6, 0, 1), ("Z", 4, 1),
    ("S", 5, 1, 2), ("F", 6, 0), ("F", 6, 1), ("D", 7), ("Z", 5, 0), ("S", 6, 1, 1), ("I", 7),
    ("S", 6, 0, 2), ("Y", 2), ("S", 7, 0, 1), ("Z", 5, 1), ("F", 7, 0), ("S", 6, 1, 2),
    ("F", 7, 1), ("Y", 3), ("S", 7, 1, 1), ("Z", 6, 0), ("T", 0), ("S", 7, 0, 2), ("S", 7, 1, 2),
    ("E", 0, 1), ("Z", 6, 1), ("Z", 7, 0), ("T", 1), ("E", 1, 1), ("P", 0, 0, 1), ("Z", 7, 1),
    ("T", 2), ("E", 0, 2), ("E", 1, 2), ("P", 0, 1, 1), ("P", 1, 0, 1), ("T", 3), ("E", 0, 0),
    ("P", 0, 0, 2), ("O", 2), ("E", 1, 0), ("P", 0, 1, 2), ("T", 4), ("P", 1, 1, 1),
    ("P", 2, 0, 1), ("O", 3), ("T", 5), ("P", 0, 0, 0), ("P", 0, 1, 0), ("R", 0), ("O", 4),
    ("P", 1, 0, 2), ("P", 1, 1, 2), ("P", 3, 0, 1), ("R", 1), ("P", 2, 1, 1), ("P", 1, 0, 0),
    ("P", 1, 1, 0), ("P", 2, 0, 2), ("P", 2, 1, 2), ("O", 5), ("P", 4, 0, 1), ("P", 3, 1, 1),
    ("R", 2), ("M", 0), ("P", 2, 0, 0), ("P", 2, 1, 0), ("P", 3, 0, 2), ("P", 3, 1, 2), ("M", 1),
    ("P", 5, 0, 1), ("P", 4, 1, 1), ("M", 2), ("R", 3), ("P", 3, 1, 0), ("P", 4, 1, 2),
    ("P", 3, 0, 0), ("M", 3), ("P", 5, 1, 1), ("P", 4, 0, 2), ("P", 6, 0, 1), ("M", 4), ("R", 4),
    ("P", 4, 0, 0), ("P", 4, 1, 0), ("M", 5), ("P", 5, 0, 2), ("P", 5, 1, 2), ("P", 6, 1, 1),
    ("R", 5), ("P", 5, 1, 0), ("P", 5, 0, 0), ("P", 6, 1, 2), ("P", 6, 0, 2), ("R", 6), ("R", 7),
    ("P", 6, 1, 0), ("P", 6, 0, 0),
)
F32 = jnp.float32
BF16 = jnp.bfloat16


def dot(left, right, left_dim, right_dim):
    return lax.dot_general(
        left, right, (((left_dim,), (right_dim,)), ((), ())), preferred_element_type=F32
    )


def gelu(v):
    return v * (0.5 * jnp.tanh(v * (C0 + C1 * (v * v))) + 0.5)


def gelu_both(v):
    v2 = v * v
    h = 0.5 * jnp.tanh(v * (C0 + C1 * v2)) + 0.5
    return v * h, h + (h - h * h) * (v * (2 * C0 + 6 * C1 * v2))


def mod(v):
    return lax.rem(v + 2 * RING, RING)


def flip(index, step):
    return index + step - 2 * step * lax.rem(lax.div(index, step), 2)


def column(row, length):
    return jnp.transpose(jnp.broadcast_to(row.reshape(1, length), (8, length)))[:, 0:1]


def layer_kernel(
    groups,
    counts,
    images,
    cot,
    gain1,
    bias1,
    gain2,
    bias2,
    biasc,
    tw1,
    tb1,
    tw2,
    tb2,
    w1_own,
    w2_own,
    b1_own,
    out_o,
    gim_o,
    d2_o,
    d1_o,
    small_o,
    xh,
    xb,
    cb,
    y2b,
    gb,
    res,
    acc,
    w1b,
    w2b,
    act,
    dg,
    stat,
    pb,
    bar,
    xr,
    held,
    rs,
    xs,
    fs,
    vecb,
    b1h,
    b1v,
    t1v,
    t2v,
    vacc,
    small,
    small_c,
    small_x,
    small_s,
    small_r,
    loc_x,
    snd_x,
    rcv_x,
    loc_c,
    snd_c,
    rcv_c,
    loc_w,
    snd_w,
    rcv_w,
    snd_b,
    rcv_b,
    snd_h,
    rcv_h,
    snd_r,
    rcv_r,
    snd_e,
    rcv_e,
    snd_g,
    rcv_g,
    loc_g,
    loc_o,
    snd_o,
    rcv_o,
    loc_i,
    snd_i,
    rcv_i,
    snd_s,
    rcv_s,
):
    _, imgs, patches, half = xb.shape
    chans = 2 * half
    pad = y2b.shape[0] // imgs
    piece = w2_own.shape[1]
    both = piece - 2 * SOLO
    dp, aa, ba = lax.axis_index("dp"), lax.axis_index("aa"), lax.axis_index("ba")
    lo, hi = lax.rem(dp, RING), lax.div(dp, RING)
    pos = jnp.where(lax.rem(lo, 2) == 0, lax.div(lo, 2), RING - 1 - lax.div(lo, 2))

    def at(place):
        place = mod(place)
        return hi * RING + jnp.where(
            place < RING // 2, 2 * place, 2 * (RING - 1 - place) + 1
        )

    dev_x = (dp, 1 - aa, ba)
    dev_c = (dp, aa, 1 - ba)
    dev_ring = ((at(pos + 1), aa, ba), (at(pos - 1), aa, ba))
    dev_fly = []
    step = 1
    while step < RING * groups:
        dev_fly.append((flip(dp, step), aa, ba))
        step *= 2
    dev_hi = dev_fly[3:]
    peers = [dev_x, dev_c, *dev_ring, *dev_fly]
    barrier = pltpu.get_barrier_semaphore()
    for peer in peers:
        pl.semaphore_signal(barrier, inc=1, device_id=peer, device_id_type=MESH)

    rows_mine = pl.ds(pl.multiple_of(ba * piece, 64), piece)
    rows_other = pl.ds(pl.multiple_of((1 - ba) * piece, 64), piece)

    def remote(src, dst, send, recv, dev):
        return pltpu.make_async_remote_copy(
            src_ref=src,
            dst_ref=dst,
            send_sem=send,
            recv_sem=recv,
            device_id=dev,
            device_id_type=MESH,
        )

    def local_in(src, dst, sem, i):
        return pltpu.make_async_copy(src.at[aa * imgs + i], dst.at[aa, i], sem.at[i])

    def give(src, dst, send, recv, i):
        return remote(
            src.at[(1 - aa) * imgs + i], dst.at[aa, i], send.at[i], recv.at[i], dev_x
        )

    def take(src, dst, send, recv, i):
        return remote(
            src.at[(1 - aa) * imgs + i], dst.at[1 - aa, i], send.at[i], recv.at[i], dev_x
        )

    def wide(ref, i):
        return jnp.concatenate([ref[0, i], ref[1, i]], axis=1).astype(F32)

    def put(ref, i, rows):
        rows = rows.astype(BF16)
        ref[0, i] = rows[:, :half]
        ref[1, i] = rows[:, half:]

    cols = 2 * piece
    parts = w1_own.shape[1] // cols

    def w1_in(k):
        return pltpu.make_async_copy(
            w1_own.at[:, pl.ds(k * cols, cols)], act.at[k, pl.ds(0, chans), :], loc_w.at[1 + k]
        )

    for k in range(parts):
        w1_in(k).start()
    for i in range(imgs):
        local_in(images, xb, loc_x, i).start()
    w2_local = pltpu.make_async_copy(w2_own, w2b.at[:, rows_mine, :], loc_w.at[0])
    w2_local.start()
    for i in range(imgs):
        local_in(cot, cb, loc_c, i).start()
    for k, ref in enumerate((gain1, bias1, gain2, bias2, biasc)):
        vecb[aa, k : k + 1, :] = ref[...].reshape(1, half)
    b1h[ba] = b1_own[...].reshape(1, parts * cols)

    pl.semaphore_wait(barrier, len(peers))

    vec_copy = remote(vecb.at[aa], vecb.at[aa], snd_w.at[2], rcv_w.at[2], dev_x)
    vec_copy.start()
    for i in range(LOOK):
        give(images, xb, snd_x, rcv_x, i).start()
    b1_copy = remote(b1h.at[ba], b1h.at[ba], snd_w.at[3], rcv_w.at[3], dev_c)
    b1_copy.start()
    w2_copy = remote(w2_own, w2b.at[:, rows_mine, :], snd_w.at[0], rcv_w.at[0], dev_c)
    w2_copy.start()
    y2b[...] = jnp.zeros(y2b.shape, BF16)
    gb[...] = jnp.zeros(gb.shape, BF16)
    vacc[...] = jnp.zeros(vacc.shape, F32)
    small[...] = jnp.zeros(small.shape, F32)
    t1v[...] = column(tb1[...], t1v.shape[0])
    t2v[...] = column(tb2[...], patches)
    for k in range(parts):
        w1_in(k).wait()
        turned = jnp.transpose(act[k, 0:chans, :])
        w1b[2 * k, rows_mine, :] = turned[:piece]
        w1b[2 * k + 1, rows_mine, :] = turned[piece:]
    w1_copy = remote(
        w1b.at[:, rows_mine, :], w1b.at[:, rows_mine, :], snd_w.at[1], rcv_w.at[1], dev_c
    )
    w1_copy.start()
    vec_copy.wait_send()
    remote(vecb.at[aa], vecb.at[1 - aa], snd_w.at[2], rcv_w.at[2], dev_x).wait_recv()
    b1_copy.wait_send()
    remote(b1h.at[ba], b1h.at[1 - ba], snd_w.at[3], rcv_w.at[3], dev_c).wait_recv()
    for q in range(RING):
        b1v[q : q + 1, :] = jnp.concatenate(
            [b1h[0, :, q * piece : (q + 1) * piece], b1h[1, :, q * piece : (q + 1) * piece]],
            axis=1,
        )

    def vec(k):
        return jnp.concatenate([vecb[0, k : k + 1, :], vecb[1, k : k + 1, :]], axis=1)

    def token_forward(i):
        local_in(images, xb, loc_x, i).wait()
        take(images, xb, snd_x, rcv_x, i).wait()

        @pl.when(i + LOOK < imgs)
        def _():
            give(images, xb, snd_x, rcv_x, i + LOOK).start()

        @pl.when(i + LOOK >= imgs)
        def _():
            give(cot, cb, snd_c, rcv_c, i + LOOK - imgs).start()

        @pl.when(i == imgs - 1)
        def _():
            for n in range(LOOK, imgs):
                give(cot, cb, snd_c, rcv_c, n).start()

        x = wide(xb, i)
        mean = jnp.mean(x, -1, keepdims=True)
        xc = x - mean
        rstd = lax.rsqrt(jnp.mean(xc * xc, -1, keepdims=True) + EPS)
        stat[i, :, 0 : 1] = mean
        stat[i, :, 1 : 2] = rstd
        y1 = (xc * rstd * vec(0) + vec(1)).astype(BF16)
        hid = gelu(dot(tw1[...], y1, 0, 0) + t1v[...]).astype(BF16)
        row = x + dot(tw2[...], hid, 1, 0) + t2v[...]
        res[i] = row
        mean = jnp.mean(row, -1, keepdims=True)
        xc = row - mean
        rstd = lax.rsqrt(jnp.mean(xc * xc, -1, keepdims=True) + EPS)
        stat[i, :, 2 : 3] = mean
        stat[i, :, 3 : 4] = rstd
        y2 = (xc * rstd * vec(2) + vec(3)).astype(BF16)
        y2b[pl.ds(pl.multiple_of(i * pad, 16), patches), :] = y2

    def weight(i):
        return jnp.where(aa * imgs + i < counts[0], 1.0, 0.0).astype(F32)

    chunks = 3
    size = y2b.shape[0] // chunks
    each = imgs // chunks

    def chan_forward(chunk, pair):
        rows = pl.ds(pl.multiple_of(chunk * size, 16), size)
        win = w1b[pl.ds(2 * pair, 2)].reshape(2 * cols, chans)
        wout = w2b[pl.ds(2 * pair, 2)].reshape(2 * cols, chans)
        bias = jnp.concatenate(
            [b1v[pl.ds(2 * pair, 1), :], b1v[pl.ds(2 * pair + 1, 1), :]], axis=1
        )
        val, der = gelu_both(dot(y2b[rows, :], win, 1, 1) + bias)
        val = val.astype(BF16)
        der = der.astype(BF16)
        act[2 * pair, rows, :] = val[:, :cols]
        act[2 * pair + 1, rows, :] = val[:, cols:]
        dg[2 * pair, rows, :] = der[:, :cols]
        dg[2 * pair + 1, rows, :] = der[:, cols:]
        new = dot(val, wout, 1, 0)
        acc[rows, :] = jnp.where(pair == 0, 0.0, acc[rows, :]) + new

    def forward_chunk(chunk, carry):
        def one(k, carry):
            token_forward(chunk * each + k)
            return carry

        lax.fori_loop(0, each, one, 0)

        @pl.when(chunk == 0)
        def _():
            w2_local.wait()
            w2_copy.wait_send()
            remote(
                w2_own, w2b.at[:, rows_other, :], snd_w.at[0], rcv_w.at[0], dev_c
            ).wait_recv()
            w1_copy.wait_send()
            remote(
                w1b.at[:, rows_mine, :], w1b.at[:, rows_other, :], snd_w.at[1], rcv_w.at[1], dev_c
            ).wait_recv()

        def two(k, carry):
            chan_forward(chunk, k)
            return carry

        lax.fori_loop(0, RING // 2, two, 0)
        return carry

    lax.fori_loop(0, chunks, forward_chunk, 0)
    def out_local(i):
        return pltpu.make_async_copy(cb.at[aa, i], out_o.at[aa * imgs + i], loc_o.at[i])

    def out_remote(i, sender):
        return remote(
            cb.at[1 - aa, i], out_o.at[sender * imgs + i], snd_o.at[i], rcv_o.at[i], dev_x
        )

    def mask_cot(i, carry):
        local_in(cot, cb, loc_c, i).wait()
        take(cot, cb, snd_c, rcv_c, i).wait()
        rows = pl.ds(pl.multiple_of(i * pad, 16), patches)
        scale = weight(i)
        gb[rows, :] = (wide(cb, i) * scale).astype(BF16)
        put(cb, i, scale * (res[i] + acc[rows, :] + vec(4)))
        return carry

    lax.fori_loop(0, imgs, mask_cot, 0)

    def grad_local(i):
        return pltpu.make_async_copy(xb.at[aa, i], gim_o.at[aa * imgs + i], loc_i.at[i])

    def grad_remote(i, sender):
        return remote(
            xb.at[1 - aa, i], gim_o.at[sender * imgs + i], snd_i.at[i], rcv_i.at[i], dev_x
        )

    ones = jnp.ones((8, chans), BF16)

    def token_backward(i):
        rows = pl.ds(i * pad, patches)
        up = acc[rows, :]
        grad_out = gb[rows, :].astype(F32)
        rstd = stat[i, :, 3 : 4]
        normed = (res[i] - stat[i, :, 2 : 3]) * rstd
        vacc[2:3, :] += jnp.sum(up * normed, 0, keepdims=True)
        vacc[3:4, :] += jnp.sum(up, 0, keepdims=True)
        vacc[4:5, :] += jnp.sum(grad_out, 0, keepdims=True)
        q = up * vec(2)
        mean = jnp.mean(q, -1, keepdims=True)
        proj = jnp.mean(q * normed, -1, keepdims=True)
        grad_res = grad_out + rstd * (q - mean - normed * proj)
        grad_tok = grad_res.astype(BF16)
        rstd = stat[i, :, 1 : 2]
        normed = (wide(xb, i) - stat[i, :, 0 : 1]) * rstd
        y1 = (normed * vec(0) + vec(1)).astype(BF16)
        val, der = gelu_both(dot(tw1[...], y1, 0, 0) + t1v[...])
        small[200 : 200 + patches, :] += dot(grad_tok, val.astype(BF16), 1, 1)
        small[408:416, 0:patches] += dot(ones, grad_tok, 1, 1)
        grad_pre = (dot(tw2[...], grad_tok, 0, 0) * der).astype(BF16)
        small[0:patches, :] += dot(y1, grad_pre, 1, 1)
        small[400:408, :] += dot(ones, grad_pre, 1, 1)
        up = dot(tw1[...], grad_pre, 1, 0)
        vacc[0:1, :] += jnp.sum(up * normed, 0, keepdims=True)
        vacc[1:2, :] += jnp.sum(up, 0, keepdims=True)
        q = up * vec(0)
        mean = jnp.mean(q, -1, keepdims=True)
        proj = jnp.mean(q * normed, -1, keepdims=True)
        put(xb, i, grad_res + rstd * (q - mean - normed * proj))

    solo_mine = pl.ds(pl.multiple_of(aa * SOLO, 16), SOLO)
    solo_other = pl.ds(pl.multiple_of((1 - aa) * SOLO, 16), SOLO)
    part = both // 2
    ring_rows = (pl.ds(0, SOLO), pl.ds(SOLO, part), pl.ds(SOLO + part, part))
    own_at = (aa * SOLO, 2 * SOLO, 2 * SOLO + part)
    last = RING - 1

    def own_rows(place, size):
        return pl.ds(pl.multiple_of(ba * piece + place, 16), size)

    def to_core(s, a):
        return remote(
            pb.at[s % SLOTS, a, rows_other, :],
            bar.at[s, a],
            snd_b.at[s, a],
            rcv_b.at[s, a],
            dev_c,
        )

    def to_x(s, a):
        return remote(
            bar.at[s, a, solo_other, :], xr.at[s, a], snd_h.at[s, a], rcv_h.at[s, a], dev_x
        )

    def to_ring(s, a, c):
        return remote(
            rs.at[s, a, ring_rows[c], :],
            rs.at[s + 1, a, ring_rows[c], :],
            snd_r.at[s, a, c],
            rcv_r.at[s, a, c],
            dev_ring[a],
        )

    def swap(a, c):
        src = rs.at[last, a, ring_rows[c], :]
        dst = fs.at[a, solo_mine, :] if c == 0 else xs.at[a, pl.ds((c - 1) * part, part), :]
        return remote(src, dst, snd_e.at[0, a, c], rcv_e.at[0, a, c], dev_x)

    arrived = set()

    def core_arrival(s, a):
        if (s, a) not in arrived:
            arrived.add((s, a))
            to_core(s, a).wait_recv()

    def lefts(k):
        return mod(pos + 1 + 2 * k), mod(pos + 2 + 2 * k)

    def weight_out(j):
        if j >= SLOTS:
            to_core(j - SLOTS, 0).wait_send()
        pb[j % SLOTS, 0] = dot(act[mod(pos - 1 - j)], gb[...], 0, 0).astype(BF16)
        to_core(j, 0).start()

    def weight_in(j):
        if j >= SLOTS:
            to_core(j - SLOTS, 1).wait_send()
        pb[j % SLOTS, 1] = dot(dg[mod(pos + 1 + j)], y2b[...], 0, 0).astype(BF16)
        to_core(j, 1).start()

    def grad_hidden(k):
        pair = lefts(k)
        rows = jnp.concatenate([w2b[n] for n in pair], axis=0)
        slope = jnp.concatenate([dg[n] for n in pair], axis=1).astype(F32)
        grad = (dot(gb[...], rows, 1, 1) * slope).astype(BF16)
        total = jnp.sum(grad.astype(F32), 0, keepdims=True)
        for n, left in enumerate(pair):
            dg[left] = grad[:, n * cols : (n + 1) * cols]
            small[pl.ds(416 + left, 1), :] = total[:, n * cols : (n + 1) * cols]

    def grad_rows(k):
        pair = lefts(k)
        grad = jnp.concatenate([dg[n] for n in pair], axis=1)
        new = dot(grad, jnp.concatenate([w1b[n] for n in pair], axis=0), 1, 0)
        acc[...] = new if k == 0 else acc[...] + new

    def first_sum(s, a):
        core_arrival(s, a)
        own = own_rows((1 - aa) * SOLO, SOLO)
        total = pb[s % SLOTS, a, own, :].astype(F32) + bar[s, a, solo_other, :].astype(F32)
        bar[s, a, solo_other, :] = total.astype(BF16)
        to_x(s, a).start()
        own = own_rows(aa * SOLO, SOLO)
        held[s, a] = pb[s % SLOTS, a, own, :].astype(F32) + bar[s, a, solo_mine, :].astype(F32)

    def pass_sum(s, a, c, total):
        if s > 0:
            to_ring(s - 1, a, c).wait_recv()
            total = total + rs[s, a, ring_rows[c], :].astype(F32)
        total = total.astype(BF16)
        rs[s, a, ring_rows[c], :] = total
        if s < last:
            to_ring(s, a, c).start()
        else:
            if c == 0:
                fs[a, solo_mine, :] = total
            swap(a, c).start()

    def shared_sum(s, a, c):
        core_arrival(s, a)
        total = pb[s % SLOTS, a, own_rows(own_at[c], part), :].astype(F32)
        pass_sum(s, a, c, total + bar[s, a, pl.ds(own_at[c], part), :].astype(F32))

    def solo_sum(s, a):
        to_x(s, a).wait()
        pass_sum(s, a, 0, held[s, a] + xr[s, a].astype(F32))

    def send_out(i):
        out_local(i).start()
        out_remote(i, aa).start()

    def send_grad(i):
        grad_local(i).start()
        grad_remote(i, aa).start()

    results = (d2_o, d1_o)
    gather_rows = (pl.ds(0, 2 * SOLO), pl.ds(2 * SOLO, part), pl.ds(2 * SOLO + part, part))

    def gather(t, a, c, src):
        q = mod(pos - t) if a == 0 else mod(pos + t)
        dst = results[a].at[q, gather_rows[c], :]
        return remote(
            dst if src is None else src, dst, snd_g.at[t, a, c], rcv_g.at[t, a, c], dev_ring[a]
        )

    def gather_arrival(t, a, c):
        q = mod(pos - 1 - t) if a == 0 else mod(pos + 1 + t)
        dst = results[a].at[q, gather_rows[c], :]
        return remote(dst, dst, snd_g.at[t, a, c], rcv_g.at[t, a, c], dev_ring[a])

    def keep(a, c):
        return pltpu.make_async_copy(
            fs.at[a, gather_rows[c], :], results[a].at[pos, gather_rows[c], :], loc_g.at[a, c]
        )

    def start_gather(a, c):
        rows = gather_rows[c]
        swap(a, c).wait_send()
        if c == 0:
            region = fs.at[a, solo_other, :]
            remote(region, region, snd_e.at[0, a, c], rcv_e.at[0, a, c], dev_x).wait_recv()
        else:
            swap(a, c).wait_recv()
            fs[a, rows, :] = (
                rs[last, a, ring_rows[c], :].astype(F32)
                + xs[a, (c - 1) * part : c * part, :].astype(F32)
            ).astype(BF16)
        for k, dev in enumerate(dev_hi):
            landed = xh.at[k, a, rows, :]
            near = bar.at[0, a, pl.ds(0, rows.size), :]
            copy = remote(
                fs.at[a, rows, :], landed, snd_e.at[1 + k, a, c], rcv_e.at[1 + k, a, c], dev
            )
            copy.start()
            copy.wait()
            back = pltpu.make_async_copy(landed, near, loc_g.at[a, c])
            back.start()
            back.wait()
            fs[a, rows, :] = (
                fs[a, rows, :].astype(F32) + bar[0, a, : rows.size, :].astype(F32)
            ).astype(BF16)
        gather(0, a, c, fs.at[a, rows, :]).start()
        keep(a, c).start()

    def pass_on(t, a, c):
        gather_arrival(t, a, c).wait_recv()
        if t + 1 < RING - 1:
            gather(t + 1, a, c, None).start()

    total_rows = small.shape[0]
    half_rows, quarter = total_rows // 2, total_rows // 4
    own_half = pl.ds(pl.multiple_of(ba * half_rows, 256), half_rows)
    other_half = pl.ds(pl.multiple_of((1 - ba) * half_rows, 256), half_rows)
    own_quarter = pl.ds(pl.multiple_of(ba * half_rows + aa * quarter, 128), quarter)
    other_quarter = pl.ds(pl.multiple_of(ba * half_rows + (1 - aa) * quarter, 128), quarter)
    flies = len(dev_fly)

    small_steps = [
        remote(small.at[other_half, :], small_c, snd_s.at[0], rcv_s.at[0], dev_c),
        remote(small.at[other_quarter, :], small_x, snd_s.at[1], rcv_s.at[1], dev_x),
    ]
    for k, dev in enumerate(dev_fly):
        small_steps.append(
            remote(small_s.at[k], small_r.at[k], snd_s.at[2 + k], rcv_s.at[2 + k], dev)
        )
    for k, (rows, dev) in enumerate(((own_quarter, dev_x), (own_half, dev_c))):
        region = small_o.at[rows, :]
        n = 2 + flies + k
        small_steps.append(remote(region, region, snd_s.at[n], rcv_s.at[n], dev))

    def small_start(n):
        if n == 2:
            small_s[0] = small[own_quarter, :].astype(BF16)
        small_steps[n].start()

    def small_finish(n):
        if n < 2 + flies:
            small_steps[n].wait()
        if n == 0:
            small[own_half, :] += small_c[...]
        elif n == 1:
            small[own_quarter, :] += small_x[...]
        elif n < 2 + flies:
            total = small_s[n - 2].astype(F32) + small_r[n - 2].astype(F32)
            if n + 1 < 2 + flies:
                small_s[n - 1] = total.astype(BF16)
            else:
                small_o[own_quarter, :] = total.astype(BF16)
        else:
            rows = other_quarter if n == 2 + flies else other_half
            region = small_o.at[rows, :]
            small_steps[n].wait_send()
            remote(region, region, snd_s.at[n], rcv_s.at[n], dev_x).wait_recv()

    def small_step(n):
        if n == 0:
            small[424:432, :] = vacc[:, :half]
            small[432:440, :] = vacc[:, half:]
        else:
            small_finish(n - 1)
        if n < len(small_steps):
            small_start(n)

    work = {
        "D": weight_out,
        "I": weight_in,
        "G": grad_hidden,
        "Y": grad_rows,
        "F": first_sum,
        "S": shared_sum,
        "Z": solo_sum,
        "E": start_gather,
        "P": pass_on,
        "T": token_backward,
        "M": send_grad,
        "O": send_out,
        "R": small_step,
    }
    for name, *index in PLAN:
        work[name](*index)
    for n in range(SMALL_STEPS + 1, len(small_steps) + 1):
        small_step(n)

    for s in range(RING - SLOTS, RING):
        for a in range(2):
            to_core(s, a).wait_send()
    for a in range(2):
        for c in range(3):
            keep(a, c).wait()

    def drain_images(i, carry):
        out_local(i).wait()
        out_remote(i, 1 - aa).wait()
        grad_local(i).wait()
        grad_remote(i, 1 - aa).wait()
        return carry

    lax.fori_loop(0, imgs, drain_images, 0)

    for t in range(RING - 1):
        for a in range(2):
            for c in range(3):
                to_ring(t, a, c).wait_send()
                gather_arrival(t, a, c).wait_send()


def finish_kernel(gim, d2, d1, small, gim_o, w2_o, w1_o, tw1_o, tw2_o, tb1_o, tb2_o, b1_o, *vec_o):
    count, piece, lanes = d1.shape
    gim_o[...] = gim[...].astype(F32)
    w2_o[...] = d2[...].astype(F32)
    w1_o[...] = jnp.transpose(d1[...].reshape(count * piece, lanes)).astype(F32)

    @pl.when(pl.program_id(0) == 0)
    def _():
        aa, ba = lax.axis_index("aa"), lax.axis_index("ba")
        patches = tw1_o.shape[0]
        tw1_o[...] = small[0:patches, :].astype(F32)
        tw2_o[...] = small[200 : 200 + patches, :].astype(F32)
        tb1_o[...] = small[400:401, :].astype(F32).reshape(tb1_o.shape)
        tb2_o[...] = small[408:409, 0:patches].astype(F32).reshape(patches)
        rows = small[416:424, :].astype(F32)
        rows = jnp.where(ba == 0, rows[:, :piece], rows[:, piece:])
        rows = jnp.concatenate([rows[q : q + 1, :] for q in range(RING)], axis=1)
        b1_o[...] = rows.reshape(b1_o.shape)
        rows = jnp.where(aa == 0, small[424:432, :].astype(F32), small[432:440, :].astype(F32))
        for k, ref in enumerate(vec_o):
            ref[...] = rows[k : k + 1, :].reshape(ref.shape)


def local(groups, images, counts, ln1_gain, ln1_bias, tok_w1, tok_b1, tok_w2, tok_b2,
          ln2_gain, ln2_bias, ch_w1, ch_b1, ch_w2, ch_b2, cotangent):
    slots, patches, half = images.shape
    chans = 2 * half
    imgs = slots // 2
    pad = -(-patches // 16) * 16
    hidden = ch_w1.shape[1]
    piece = hidden // RING
    both = piece - 2 * SOLO
    keep_rows = SOLO + both
    hid_tok = tok_w1.shape[1]
    total = 512
    flies = 3
    while RING * groups > 2**flies:
        flies += 1
    his = max(flies - 3, 1)
    vmem = pl.BlockSpec(memory_space=pltpu.VMEM)
    hbm = pl.BlockSpec(memory_space=pl.ANY)
    dma = pltpu.SemaphoreType.DMA
    per_image = [dma((imgs,))] * 3
    out, gim, d2, d1, small, _ = pl.pallas_call(
        functools.partial(layer_kernel, groups),
        out_shape=[
            jax.ShapeDtypeStruct((slots, patches, half), BF16),
            jax.ShapeDtypeStruct((slots, patches, half), BF16),
            jax.ShapeDtypeStruct((RING, piece, chans), BF16),
            jax.ShapeDtypeStruct((RING, piece, chans), BF16),
            jax.ShapeDtypeStruct((total, hid_tok), BF16),
            jax.ShapeDtypeStruct((his, 2, piece if groups > 1 else 16, chans), BF16),
        ],
        in_specs=[pl.BlockSpec(memory_space=pltpu.SMEM), hbm, hbm]
        + [vmem] * 9
        + [hbm] * 2
        + [vmem],
        out_specs=[hbm] * 4 + [vmem, hbm],
        scratch_shapes=[
            pltpu.VMEM((2, imgs, patches, half), BF16),
            pltpu.VMEM((2, imgs, patches, half), BF16),
            pltpu.VMEM((imgs * pad, chans), BF16),
            pltpu.VMEM((imgs * pad, chans), BF16),
            pltpu.VMEM((imgs, patches, chans), F32),
            pltpu.VMEM((imgs * pad, chans), F32),
            pltpu.VMEM((RING, 2 * piece, chans), BF16),
            pltpu.VMEM((RING, 2 * piece, chans), BF16),
            pltpu.VMEM((RING, imgs * pad, 2 * piece), BF16),
            pltpu.VMEM((RING, imgs * pad, 2 * piece), BF16),
            pltpu.VMEM((imgs, patches, 4), F32),
            pltpu.VMEM((SLOTS, 2, 2 * piece, chans), BF16),
            pltpu.VMEM((RING, 2, piece, chans), BF16),
            pltpu.VMEM((RING, 2, SOLO, chans), BF16),
            pltpu.VMEM((RING, 2, SOLO, chans), F32),
            pltpu.VMEM((RING, 2, keep_rows, chans), BF16),
            pltpu.VMEM((2, both, chans), BF16),
            pltpu.VMEM((2, piece, chans), BF16),
            pltpu.VMEM((2, 8, half), F32),
            pltpu.VMEM((2, 1, hidden), F32),
            pltpu.VMEM((RING, 2 * piece), F32),
            pltpu.VMEM((hid_tok, 1), F32),
            pltpu.VMEM((patches, 1), F32),
            pltpu.VMEM((8, chans), F32),
            pltpu.VMEM((total, hid_tok), F32),
            pltpu.VMEM((total // 2, hid_tok), F32),
            pltpu.VMEM((total // 4, hid_tok), F32),
            pltpu.VMEM((flies, total // 4, hid_tok), BF16),
            pltpu.VMEM((flies, total // 4, hid_tok), BF16),
            *per_image,
            *per_image,
            dma((5,)),
            dma((4,)),
            dma((4,)),
            dma((RING, 2)),
            dma((RING, 2)),
            dma((RING, 2)),
            dma((RING, 2)),
            dma((RING, 2, 3)),
            dma((RING, 2, 3)),
            dma((1 + his, 2, 3)),
            dma((1 + his, 2, 3)),
            dma((RING, 2, 3)),
            dma((RING, 2, 3)),
            dma((2, 3)),
            *per_image,
            *per_image,
            dma((4 + flies,)),
            dma((4 + flies,)),
        ],
        compiler_params=pltpu.CompilerParams(
            collective_id=0, has_side_effects=True, vmem_limit_bytes=65100 * 1024
        ),
    )(
        counts,
        images,
        cotangent,
        ln1_gain,
        ln1_bias,
        ln2_gain,
        ln2_bias,
        ch_b2,
        tok_w1,
        tok_b1,
        tok_w2.T,
        tok_b2,
        ch_w1,
        ch_w2.reshape(RING, piece, chans),
        ch_b1,
    )
    steps = chans // 128
    row = jax.ShapeDtypeStruct((half,), F32)

    def whole(*shape):
        return pl.BlockSpec(shape, lambda k: (0,) * len(shape))

    some = pl.BlockSpec((slots // steps, patches, half), lambda k: (k, 0, 0))
    gim, w2, w1, tw1, tw2, tb1, tb2, b1, g1, n1, g2, n2, c2 = pl.pallas_call(
        finish_kernel,
        grid=(steps,),
        out_shape=[
            jax.ShapeDtypeStruct((slots, patches, half), F32),
            jax.ShapeDtypeStruct((hidden, chans), F32),
            jax.ShapeDtypeStruct((chans, hidden), F32),
            jax.ShapeDtypeStruct((patches, hid_tok), F32),
            jax.ShapeDtypeStruct((patches, hid_tok), F32),
            jax.ShapeDtypeStruct((hid_tok,), F32),
            jax.ShapeDtypeStruct((patches,), F32),
            jax.ShapeDtypeStruct((hidden,), F32),
        ]
        + [row] * 5,
        in_specs=[
            some,
            pl.BlockSpec((hidden // steps, chans), lambda k: (k, 0)),
            pl.BlockSpec((RING, piece, 128), lambda k: (0, 0, k)),
            whole(total, hid_tok),
        ],
        out_specs=[
            some,
            pl.BlockSpec((hidden // steps, chans), lambda k: (k, 0)),
            pl.BlockSpec((128, hidden), lambda k: (k, 0)),
            whole(patches, hid_tok),
            whole(patches, hid_tok),
            whole(hid_tok),
            whole(patches),
            whole(hidden),
        ]
        + [whole(half)] * 5,
        compiler_params=pltpu.CompilerParams(vmem_limit_bytes=62 * 2**20),
    )(gim, d2.reshape(hidden, chans), d1, small)
    return out, gim, g1, n1, tw1, tb1, tw2.T, tb2, g2, n2, w1, b1, w2, c2


def solution(mesh):
    rows = P(("dp", "ba"), None, "aa")
    chan = P("aa")
    placed = (rows, P(("dp", "ba")), chan, chan, P(), P(), P(), P(), chan, chan,
              P(None, "ba"), P("ba"), P("ba", None), chan, rows)
    given = (rows, rows, chan, chan, P(), P(), P(), P(), chan, chan,
             P(None, "ba"), P("ba"), P("ba", None), chan)
    return jax.shard_map(
        functools.partial(local, mesh.shape["dp"] // RING),
        mesh=mesh,
        in_specs=placed,
        out_specs=given,
        check_vma=False,
    )
```

```python
import functools

import jax
import jax.numpy as jnp
from jax import lax
from jax.experimental import pallas as pl
from jax.experimental.pallas import tpu as pltpu
from jax.sharding import PartitionSpec as P

MESH = pl.DeviceIdType.MESH
EPS = 1e-06
C0 = 0.7978845608028654
C1 = C0 * 0.044715
RING = 8
SOLO = 48
SLOTS = 3
SMALL_STEPS = 7
PLAN = (
    ("D", 0), ("G", 0), ("I", 0), ("S", 0, 0, 1), ("S", 0, 0, 2), ("F", 0, 0), ("D", 1), ("I", 1),
    ("S", 0, 1, 1), ("S", 0, 1, 2), ("F", 0, 1), ("D", 2), ("S", 1, 0, 1), ("F", 1, 0),
    ("Z", 0, 0), ("G", 1), ("S", 1, 1, 1), ("S", 1, 0, 2), ("F", 1, 1), ("F", 2, 0), ("Z", 0, 1),
    ("I", 2), ("S", 1, 1, 2), ("S", 2, 0, 1), ("D", 3), ("Z", 1, 0), ("O", 0), ("I", 3),
    ("S", 2, 1, 1), ("F", 2, 1), ("S", 2, 0, 2), ("D", 4), ("F", 3, 0), ("Z", 1, 1), ("G", 2),
    ("S", 2, 1, 2), ("S", 3, 0, 1), ("F", 3, 1), ("F", 4, 0), ("Z", 2, 0), ("S", 3, 1, 1),
    ("I", 4), ("S", 3, 0, 2), ("D", 5), ("Z", 2, 1), ("I", 5), ("S", 3, 1, 2), ("S", 4, 0, 1),
    ("F", 4, 1), ("D", 6), ("S", 4, 1, 1), ("F", 5, 0), ("Z", 3, 0), ("G", 3), ("S", 4, 0, 2),
    ("F", 5, 1), ("F", 6, 0), ("Z", 3, 1), ("S", 5, 0, 1), ("I", 6), ("S", 4, 1, 2), ("D", 7),
    ("S", 5, 1, 1), ("Z", 4, 0), ("I", 7), ("S", 5, 0, 2), ("F", 6, 1), ("Z", 4, 1), ("Y", 0),
    ("S", 5, 1, 2), ("S", 6, 0, 1), ("F", 7, 0), ("F", 7, 1), ("Y", 1), ("S", 6, 1, 1),
    ("Z", 5, 0), ("S", 6, 0, 2), ("Y", 2), ("S", 7, 0, 1), ("Z", 5, 1), ("S", 6, 1, 2), ("Y", 3),
    ("S", 7, 1, 1), ("Z", 6, 0), ("T", 0), ("E", 0, 1), ("S", 7, 0, 2), ("S", 7, 1, 2),
    ("Z", 6, 1), ("E", 1, 1), ("Z", 7, 0), ("T", 1), ("P", 0, 0, 1), ("E", 0, 2), ("Z", 7, 1),
    ("T", 2), ("E", 1, 2), ("P", 0, 1, 1), ("O", 1), ("P", 1, 0, 1), ("E", 0, 0), ("T", 3),
    ("E", 1, 0), ("P", 0, 0, 2), ("P", 0, 1, 2), ("O", 2), ("P", 2, 0, 1), ("T", 4),
    ("P", 1, 1, 1), ("O", 3), ("T", 5), ("P", 0, 0, 0), ("P", 0, 1, 0), ("P", 1, 0, 2), ("R", 0),
    ("O", 4), ("P", 1, 1, 2), ("P", 3, 0, 1), ("R", 1), ("P", 2, 1, 1), ("P", 1, 0, 0),
    ("P", 1, 1, 0), ("P", 2, 0, 2), ("P", 2, 1, 2), ("P", 4, 0, 1), ("O", 5), ("P", 3, 1, 1),
    ("R", 2), ("P", 2, 0, 0), ("M", 0), ("P", 2, 1, 0), ("P", 3, 0, 2), ("P", 3, 1, 2),
    ("P", 5, 0, 1), ("M", 1), ("P", 4, 1, 1), ("R", 3), ("M", 2), ("P", 3, 1, 0), ("P", 3, 0, 0),
    ("P", 4, 1, 2), ("P", 4, 0, 2), ("M", 3), ("P", 5, 1, 1), ("P", 6, 0, 1), ("M", 4), ("R", 4),
    ("P", 4, 0, 0), ("P", 4, 1, 0), ("P", 5, 0, 2), ("M", 5), ("P", 5, 1, 2), ("P", 6, 1, 1),
    ("R", 5), ("P", 5, 0, 0), ("P", 5, 1, 0), ("P", 6, 0, 2), ("P", 6, 1, 2), ("R", 6), ("R", 7),
    ("P", 6, 0, 0), ("P", 6, 1, 0),
)
F32 = jnp.float32
BF16 = jnp.bfloat16


def dot(left, right, left_dim, right_dim):
    return lax.dot_general(
        left, right, (((left_dim,), (right_dim,)), ((), ())), preferred_element_type=F32
    )


def gelu(v):
    return v * (0.5 * jnp.tanh(v * (C0 + C1 * (v * v))) + 0.5)


def gelu_both(v):
    v2 = v * v
    h = 0.5 * jnp.tanh(v * (C0 + C1 * v2)) + 0.5
    return v * h, h + (h - h * h) * (v * (2 * C0 + 6 * C1 * v2))


def mod(v):
    return lax.rem(v + 2 * RING, RING)


def flip(index, step):
    return index + step - 2 * step * lax.rem(lax.div(index, step), 2)


def column(row, length):
    return jnp.transpose(jnp.broadcast_to(row.reshape(1, length), (8, length)))[:, 0:1]


def layer_kernel(
    groups,
    counts,
    images,
    cot,
    gain1,
    bias1,
    gain2,
    bias2,
    biasc,
    tw1,
    tb1,
    tw2,
    tb2,
    w1_own,
    w2_own,
    b1_own,
    out_o,
    gim_o,
    d2_o,
    d1_o,
    small_o,
    xh,
    xb,
    cb,
    y2b,
    gb,
    res,
    acc,
    w1b,
    w2b,
    act,
    dg,
    stat,
    pb,
    bar,
    xr,
    held,
    rs,
    xs,
    fs,
    vecb,
    b1h,
    b1v,
    t1v,
    t2v,
    vacc,
    small,
    small_c,
    small_x,
    small_s,
    small_r,
    loc_x,
    snd_x,
    rcv_x,
    loc_c,
    snd_c,
    rcv_c,
    loc_w,
    snd_w,
    rcv_w,
    snd_b,
    rcv_b,
    snd_h,
    rcv_h,
    snd_r,
    rcv_r,
    snd_e,
    rcv_e,
    snd_g,
    rcv_g,
    loc_g,
    loc_o,
    snd_o,
    rcv_o,
    loc_i,
    snd_i,
    rcv_i,
    snd_s,
    rcv_s,
):
    _, imgs, patches, half = xb.shape
    chans = 2 * half
    pad = y2b.shape[0] // imgs
    piece = w2_own.shape[1]
    both = piece - 2 * SOLO
    dp, aa, ba = lax.axis_index("dp"), lax.axis_index("aa"), lax.axis_index("ba")
    lo, hi = lax.rem(dp, RING), lax.div(dp, RING)
    pos = jnp.where(lax.rem(lo, 2) == 0, lax.div(lo, 2), RING - 1 - lax.div(lo, 2))

    def at(place):
        place = mod(place)
        return hi * RING + jnp.where(
            place < RING // 2, 2 * place, 2 * (RING - 1 - place) + 1
        )

    dev_x = (dp, 1 - aa, ba)
    dev_c = (dp, aa, 1 - ba)
    dev_ring = ((at(pos + 1), aa, ba), (at(pos - 1), aa, ba))
    dev_fly = []
    step = 1
    while step < RING * groups:
        dev_fly.append((flip(dp, step), aa, ba))
        step *= 2
    dev_hi = dev_fly[3:]
    peers = [dev_x, dev_c, *dev_ring, *dev_fly]
    barrier = pltpu.get_barrier_semaphore()
    for peer in peers:
        pl.semaphore_signal(barrier, inc=1, device_id=peer, device_id_type=MESH)

    rows_mine = pl.ds(pl.multiple_of(ba * piece, 64), piece)
    rows_other = pl.ds(pl.multiple_of((1 - ba) * piece, 64), piece)

    def remote(src, dst, send, recv, dev):
        return pltpu.make_async_remote_copy(
            src_ref=src,
            dst_ref=dst,
            send_sem=send,
            recv_sem=recv,
            device_id=dev,
            device_id_type=MESH,
        )

    def local_in(src, dst, sem, i):
        return pltpu.make_async_copy(src.at[aa * imgs + i], dst.at[aa, i], sem.at[i])

    def give(src, dst, send, recv, i):
        return remote(
            src.at[(1 - aa) * imgs + i], dst.at[aa, i], send.at[i], recv.at[i], dev_x
        )

    def take(src, dst, send, recv, i):
        return remote(
            src.at[(1 - aa) * imgs + i], dst.at[1 - aa, i], send.at[i], recv.at[i], dev_x
        )

    def wide(ref, i):
        return jnp.concatenate([ref[0, i], ref[1, i]], axis=1).astype(F32)

    def put(ref, i, rows):
        rows = rows.astype(BF16)
        ref[0, i] = rows[:, :half]
        ref[1, i] = rows[:, half:]

    cols = 2 * piece
    parts = w1_own.shape[1] // cols

    def w1_in(k):
        return pltpu.make_async_copy(
            w1_own.at[:, pl.ds(k * cols, cols)], act.at[k, pl.ds(0, chans), :], loc_w.at[1 + k]
        )

    for k in range(parts):
        w1_in(k).start()
    for i in range(imgs):
        local_in(images, xb, loc_x, i).start()
    w2_local = pltpu.make_async_copy(w2_own, w2b.at[:, rows_mine, :], loc_w.at[0])
    w2_local.start()
    for i in range(imgs):
        local_in(cot, cb, loc_c, i).start()
    for k, ref in enumerate((gain1, bias1, gain2, bias2, biasc)):
        vecb[aa, k : k + 1, :] = ref[...].reshape(1, half)
    b1h[ba] = b1_own[...].reshape(1, parts * cols)

    pl.semaphore_wait(barrier, len(peers))

    vec_copy = remote(vecb.at[aa], vecb.at[aa], snd_w.at[2], rcv_w.at[2], dev_x)
    vec_copy.start()
    for i in range(imgs):
        give(images, xb, snd_x, rcv_x, i).start()
    for i in range(imgs):
        give(cot, cb, snd_c, rcv_c, i).start()
    b1_copy = remote(b1h.at[ba], b1h.at[ba], snd_w.at[3], rcv_w.at[3], dev_c)
    b1_copy.start()
    w2_copy = remote(w2_own, w2b.at[:, rows_mine, :], snd_w.at[0], rcv_w.at[0], dev_c)
    w2_copy.start()
    y2b[...] = jnp.zeros(y2b.shape, BF16)
    gb[...] = jnp.zeros(gb.shape, BF16)
    vacc[...] = jnp.zeros(vacc.shape, F32)
    small[...] = jnp.zeros(small.shape, F32)
    t1v[...] = column(tb1[...], t1v.shape[0])
    t2v[...] = column(tb2[...], patches)
    for k in range(parts):
        w1_in(k).wait()
        turned = jnp.transpose(act[k, 0:chans, :])
        w1b[2 * k, rows_mine, :] = turned[:piece]
        w1b[2 * k + 1, rows_mine, :] = turned[piece:]
    w1_copy = remote(
        w1b.at[:, rows_mine, :], w1b.at[:, rows_mine, :], snd_w.at[1], rcv_w.at[1], dev_c
    )
    w1_copy.start()
    vec_copy.wait_send()
    remote(vecb.at[aa], vecb.at[1 - aa], snd_w.at[2], rcv_w.at[2], dev_x).wait_recv()
    b1_copy.wait_send()
    remote(b1h.at[ba], b1h.at[1 - ba], snd_w.at[3], rcv_w.at[3], dev_c).wait_recv()
    for q in range(RING):
        b1v[q : q + 1, :] = jnp.concatenate(
            [b1h[0, :, q * piece : (q + 1) * piece], b1h[1, :, q * piece : (q + 1) * piece]],
            axis=1,
        )

    def vec(k):
        return jnp.concatenate([vecb[0, k : k + 1, :], vecb[1, k : k + 1, :]], axis=1)

    def token_forward(i):
        local_in(images, xb, loc_x, i).wait()
        take(images, xb, snd_x, rcv_x, i).wait()

        x = wide(xb, i)
        mean = jnp.mean(x, -1, keepdims=True)
        xc = x - mean
        rstd = lax.rsqrt(jnp.mean(xc * xc, -1, keepdims=True) + EPS)
        stat[i, :, 0 : 1] = mean
        stat[i, :, 1 : 2] = rstd
        y1 = (xc * rstd * vec(0) + vec(1)).astype(BF16)
        hid = gelu(dot(tw1[...], y1, 0, 0) + t1v[...]).astype(BF16)
        row = x + dot(tw2[...], hid, 1, 0) + t2v[...]
        res[i] = row
        mean = jnp.mean(row, -1, keepdims=True)
        xc = row - mean
        rstd = lax.rsqrt(jnp.mean(xc * xc, -1, keepdims=True) + EPS)
        stat[i, :, 2 : 3] = mean
        stat[i, :, 3 : 4] = rstd
        y2 = (xc * rstd * vec(2) + vec(3)).astype(BF16)
        y2b[pl.ds(pl.multiple_of(i * pad, 16), patches), :] = y2

    def weight(i):
        return jnp.where(aa * imgs + i < counts[0], 1.0, 0.0).astype(F32)

    chunks = 3
    size = y2b.shape[0] // chunks
    each = imgs // chunks

    def chan_forward(chunk, pair):
        rows = pl.ds(pl.multiple_of(chunk * size, 16), size)
        win = w1b[pl.ds(2 * pair, 2)].reshape(2 * cols, chans)
        wout = w2b[pl.ds(2 * pair, 2)].reshape(2 * cols, chans)
        bias = jnp.concatenate(
            [b1v[pl.ds(2 * pair, 1), :], b1v[pl.ds(2 * pair + 1, 1), :]], axis=1
        )
        val, der = gelu_both(dot(y2b[rows, :], win, 1, 1) + bias)
        val = val.astype(BF16)
        der = der.astype(BF16)
        act[2 * pair, rows, :] = val[:, :cols]
        act[2 * pair + 1, rows, :] = val[:, cols:]
        dg[2 * pair, rows, :] = der[:, :cols]
        dg[2 * pair + 1, rows, :] = der[:, cols:]
        new = dot(val, wout, 1, 0)
        acc[rows, :] = jnp.where(pair == 0, 0.0, acc[rows, :]) + new

    def forward_chunk(chunk, carry):
        def one(k, carry):
            token_forward(chunk * each + k)
            return carry

        lax.fori_loop(0, each, one, 0)

        @pl.when(chunk == 0)
        def _():
            w2_local.wait()
            w2_copy.wait_send()
            remote(
                w2_own, w2b.at[:, rows_other, :], snd_w.at[0], rcv_w.at[0], dev_c
            ).wait_recv()
            w1_copy.wait_send()
            remote(
                w1b.at[:, rows_mine, :], w1b.at[:, rows_other, :], snd_w.at[1], rcv_w.at[1], dev_c
            ).wait_recv()

        def two(k, carry):
            chan_forward(chunk, k)
            return carry

        lax.fori_loop(0, RING // 2, two, 0)
        return carry

    lax.fori_loop(0, chunks, forward_chunk, 0)
    def out_local(i):
        return pltpu.make_async_copy(cb.at[aa, i], out_o.at[aa * imgs + i], loc_o.at[i])

    def out_remote(i, sender):
        return remote(
            cb.at[1 - aa, i], out_o.at[sender * imgs + i], snd_o.at[i], rcv_o.at[i], dev_x
        )

    def mask_cot(i, carry):
        local_in(cot, cb, loc_c, i).wait()
        take(cot, cb, snd_c, rcv_c, i).wait()
        rows = pl.ds(pl.multiple_of(i * pad, 16), patches)
        scale = weight(i)
        gb[rows, :] = (wide(cb, i) * scale).astype(BF16)
        put(cb, i, scale * (res[i] + acc[rows, :] + vec(4)))
        return carry

    lax.fori_loop(0, imgs, mask_cot, 0)

    def grad_local(i):
        return pltpu.make_async_copy(xb.at[aa, i], gim_o.at[aa * imgs + i], loc_i.at[i])

    def grad_remote(i, sender):
        return remote(
            xb.at[1 - aa, i], gim_o.at[sender * imgs + i], snd_i.at[i], rcv_i.at[i], dev_x
        )

    ones = jnp.ones((8, chans), BF16)

    def token_backward(i):
        rows = pl.ds(i * pad, patches)
        up = acc[rows, :]
        grad_out = gb[rows, :].astype(F32)
        rstd = stat[i, :, 3 : 4]
        normed = (res[i] - stat[i, :, 2 : 3]) * rstd
        vacc[2:3, :] += jnp.sum(up * normed, 0, keepdims=True)
        vacc[3:4, :] += jnp.sum(up, 0, keepdims=True)
        vacc[4:5, :] += jnp.sum(grad_out, 0, keepdims=True)
        q = up * vec(2)
        mean = jnp.mean(q, -1, keepdims=True)
        proj = jnp.mean(q * normed, -1, keepdims=True)
        grad_res = grad_out + rstd * (q - mean - normed * proj)
        grad_tok = grad_res.astype(BF16)
        rstd = stat[i, :, 1 : 2]
        normed = (wide(xb, i) - stat[i, :, 0 : 1]) * rstd
        y1 = (normed * vec(0) + vec(1)).astype(BF16)
        val, der = gelu_both(dot(tw1[...], y1, 0, 0) + t1v[...])
        small[200 : 200 + patches, :] += dot(grad_tok, val.astype(BF16), 1, 1)
        small[408:416, 0:patches] += dot(ones, grad_tok, 1, 1)
        grad_pre = (dot(tw2[...], grad_tok, 0, 0) * der).astype(BF16)
        small[0:patches, :] += dot(y1, grad_pre, 1, 1)
        small[400:408, :] += dot(ones, grad_pre, 1, 1)
        up = dot(tw1[...], grad_pre, 1, 0)
        vacc[0:1, :] += jnp.sum(up * normed, 0, keepdims=True)
        vacc[1:2, :] += jnp.sum(up, 0, keepdims=True)
        q = up * vec(0)
        mean = jnp.mean(q, -1, keepdims=True)
        proj = jnp.mean(q * normed, -1, keepdims=True)
        put(xb, i, grad_res + rstd * (q - mean - normed * proj))

    solo_mine = pl.ds(pl.multiple_of(aa * SOLO, 16), SOLO)
    solo_other = pl.ds(pl.multiple_of((1 - aa) * SOLO, 16), SOLO)
    part = both // 2
    ring_rows = (pl.ds(0, SOLO), pl.ds(SOLO, part), pl.ds(SOLO + part, part))
    own_at = (aa * SOLO, 2 * SOLO, 2 * SOLO + part)
    last = RING - 1

    def own_rows(place, size):
        return pl.ds(pl.multiple_of(ba * piece + place, 16), size)

    def to_core(s, a):
        return remote(
            pb.at[s % SLOTS, a, rows_other, :],
            bar.at[s, a],
            snd_b.at[s, a],
            rcv_b.at[s, a],
            dev_c,
        )

    def to_x(s, a):
        return remote(
            bar.at[s, a, solo_other, :], xr.at[s, a], snd_h.at[s, a], rcv_h.at[s, a], dev_x
        )

    def to_ring(s, a, c):
        return remote(
            rs.at[s, a, ring_rows[c], :],
            rs.at[s + 1, a, ring_rows[c], :],
            snd_r.at[s, a, c],
            rcv_r.at[s, a, c],
            dev_ring[a],
        )

    def swap(a, c):
        src = rs.at[last, a, ring_rows[c], :]
        dst = fs.at[a, solo_mine, :] if c == 0 else xs.at[a, pl.ds((c - 1) * part, part), :]
        return remote(src, dst, snd_e.at[0, a, c], rcv_e.at[0, a, c], dev_x)

    arrived = set()

    def core_arrival(s, a):
        if (s, a) not in arrived:
            arrived.add((s, a))
            to_core(s, a).wait_recv()

    def lefts(k):
        return mod(pos + 1 + 2 * k), mod(pos + 2 + 2 * k)

    def weight_out(j):
        if j >= SLOTS:
            to_core(j - SLOTS, 0).wait_send()
        pb[j % SLOTS, 0] = dot(act[mod(pos - 1 - j)], gb[...], 0, 0).astype(BF16)
        to_core(j, 0).start()

    def weight_in(j):
        if j >= SLOTS:
            to_core(j - SLOTS, 1).wait_send()
        pb[j % SLOTS, 1] = dot(dg[mod(pos + 1 + j)], y2b[...], 0, 0).astype(BF16)
        to_core(j, 1).start()

    def grad_hidden(k):
        pair = lefts(k)
        rows = jnp.concatenate([w2b[n] for n in pair], axis=0)
        slope = jnp.concatenate([dg[n] for n in pair], axis=1).astype(F32)
        grad = (dot(gb[...], rows, 1, 1) * slope).astype(BF16)
        total = jnp.sum(grad.astype(F32), 0, keepdims=True)
        for n, left in enumerate(pair):
            dg[left] = grad[:, n * cols : (n + 1) * cols]
            small[pl.ds(416 + left, 1), :] = total[:, n * cols : (n + 1) * cols]

    def grad_rows(k):
        pair = lefts(k)
        grad = jnp.concatenate([dg[n] for n in pair], axis=1)
        new = dot(grad, jnp.concatenate([w1b[n] for n in pair], axis=0), 1, 0)
        acc[...] = new if k == 0 else acc[...] + new

    def first_sum(s, a):
        core_arrival(s, a)
        own = own_rows((1 - aa) * SOLO, SOLO)
        total = pb[s % SLOTS, a, own, :].astype(F32) + bar[s, a, solo_other, :].astype(F32)
        bar[s, a, solo_other, :] = total.astype(BF16)
        to_x(s, a).start()
        own = own_rows(aa * SOLO, SOLO)
        held[s, a] = pb[s % SLOTS, a, own, :].astype(F32) + bar[s, a, solo_mine, :].astype(F32)

    def pass_sum(s, a, c, total):
        if s > 0:
            to_ring(s - 1, a, c).wait_recv()
            total = total + rs[s, a, ring_rows[c], :].astype(F32)
        total = total.astype(BF16)
        rs[s, a, ring_rows[c], :] = total
        if s < last:
            to_ring(s, a, c).start()
        else:
            if c == 0:
                fs[a, solo_mine, :] = total
            swap(a, c).start()

    def shared_sum(s, a, c):
        core_arrival(s, a)
        total = pb[s % SLOTS, a, own_rows(own_at[c], part), :].astype(F32)
        pass_sum(s, a, c, total + bar[s, a, pl.ds(own_at[c], part), :].astype(F32))

    def solo_sum(s, a):
        to_x(s, a).wait()
        pass_sum(s, a, 0, held[s, a] + xr[s, a].astype(F32))

    def send_out(i):
        out_local(i).start()
        out_remote(i, aa).start()

    def send_grad(i):
        grad_local(i).start()
        grad_remote(i, aa).start()

    results = (d2_o, d1_o)
    gather_rows = (pl.ds(0, 2 * SOLO), pl.ds(2 * SOLO, part), pl.ds(2 * SOLO + part, part))

    def gather(t, a, c, src):
        q = mod(pos - t) if a == 0 else mod(pos + t)
        dst = results[a].at[q, gather_rows[c], :]
        return remote(
            dst if src is None else src, dst, snd_g.at[t, a, c], rcv_g.at[t, a, c], dev_ring[a]
        )

    def gather_arrival(t, a, c):
        q = mod(pos - 1 - t) if a == 0 else mod(pos + 1 + t)
        dst = results[a].at[q, gather_rows[c], :]
        return remote(dst, dst, snd_g.at[t, a, c], rcv_g.at[t, a, c], dev_ring[a])

    def keep(a, c):
        return pltpu.make_async_copy(
            fs.at[a, gather_rows[c], :], results[a].at[pos, gather_rows[c], :], loc_g.at[a, c]
        )

    def start_gather(a, c):
        rows = gather_rows[c]
        swap(a, c).wait_send()
        if c == 0:
            region = fs.at[a, solo_other, :]
            remote(region, region, snd_e.at[0, a, c], rcv_e.at[0, a, c], dev_x).wait_recv()
        else:
            swap(a, c).wait_recv()
            fs[a, rows, :] = (
                rs[last, a, ring_rows[c], :].astype(F32)
                + xs[a, (c - 1) * part : c * part, :].astype(F32)
            ).astype(BF16)
        for k, dev in enumerate(dev_hi):
            landed = xh.at[k, a, rows, :]
            near = bar.at[0, a, pl.ds(0, rows.size), :]
            copy = remote(
                fs.at[a, rows, :], landed, snd_e.at[1 + k, a, c], rcv_e.at[1 + k, a, c], dev
            )
            copy.start()
            copy.wait()
            back = pltpu.make_async_copy(landed, near, loc_g.at[a, c])
            back.start()
            back.wait()
            fs[a, rows, :] = (
                fs[a, rows, :].astype(F32) + bar[0, a, : rows.size, :].astype(F32)
            ).astype(BF16)
        gather(0, a, c, fs.at[a, rows, :]).start()
        keep(a, c).start()

    def pass_on(t, a, c):
        gather_arrival(t, a, c).wait_recv()
        if t + 1 < RING - 1:
            gather(t + 1, a, c, None).start()

    total_rows = small.shape[0]
    half_rows, quarter = total_rows // 2, total_rows // 4
    own_half = pl.ds(pl.multiple_of(ba * half_rows, 32), half_rows)
    other_half = pl.ds(pl.multiple_of((1 - ba) * half_rows, 32), half_rows)
    own_quarter = pl.ds(pl.multiple_of(ba * half_rows + aa * quarter, 16), quarter)
    other_quarter = pl.ds(pl.multiple_of(ba * half_rows + (1 - aa) * quarter, 16), quarter)
    flies = len(dev_fly)

    small_steps = [
        remote(small.at[other_half, :], small_c, snd_s.at[0], rcv_s.at[0], dev_c),
        remote(small.at[other_quarter, :], small_x, snd_s.at[1], rcv_s.at[1], dev_x),
    ]
    for k, dev in enumerate(dev_fly):
        small_steps.append(
            remote(small_s.at[k], small_r.at[k], snd_s.at[2 + k], rcv_s.at[2 + k], dev)
        )
    for k, (rows, dev) in enumerate(((own_quarter, dev_x), (own_half, dev_c))):
        region = small_o.at[rows, :]
        n = 2 + flies + k
        small_steps.append(remote(region, region, snd_s.at[n], rcv_s.at[n], dev))

    def small_start(n):
        if n == 2:
            small_s[0] = small[own_quarter, :].astype(BF16)
        small_steps[n].start()

    def small_finish(n):
        if n < 2 + flies:
            small_steps[n].wait()
        if n == 0:
            small[own_half, :] += small_c[...]
        elif n == 1:
            small[own_quarter, :] += small_x[...]
        elif n < 2 + flies:
            total = small_s[n - 2].astype(F32) + small_r[n - 2].astype(F32)
            if n + 1 < 2 + flies:
                small_s[n - 1] = total.astype(BF16)
            else:
                small_o[own_quarter, :] = total.astype(BF16)
        else:
            rows = other_quarter if n == 2 + flies else other_half
            region = small_o.at[rows, :]
            small_steps[n].wait_send()
            remote(region, region, snd_s.at[n], rcv_s.at[n], dev_x).wait_recv()

    def small_step(n):
        if n == 0:
            small[424:432, :] = vacc[:, :half]
            small[432:440, :] = vacc[:, half:]
        else:
            small_finish(n - 1)
        if n < len(small_steps):
            small_start(n)

    work = {
        "D": weight_out,
        "I": weight_in,
        "G": grad_hidden,
        "Y": grad_rows,
        "F": first_sum,
        "S": shared_sum,
        "Z": solo_sum,
        "E": start_gather,
        "P": pass_on,
        "T": token_backward,
        "M": send_grad,
        "O": send_out,
        "R": small_step,
    }
    for name, *index in PLAN:
        work[name](*index)
    for n in range(SMALL_STEPS + 1, len(small_steps) + 1):
        small_step(n)

    for s in range(RING - SLOTS, RING):
        for a in range(2):
            to_core(s, a).wait_send()
    for a in range(2):
        for c in range(3):
            keep(a, c).wait()

    def drain_images(i, carry):
        out_local(i).wait()
        out_remote(i, 1 - aa).wait()
        grad_local(i).wait()
        grad_remote(i, 1 - aa).wait()
        return carry

    lax.fori_loop(0, imgs, drain_images, 0)

    for t in range(RING - 1):
        for a in range(2):
            for c in range(3):
                to_ring(t, a, c).wait_send()
                gather_arrival(t, a, c).wait_send()


def finish_kernel(gim, d2, d1, small, gim_o, w2_o, w1_o, tw1_o, tw2_o, tb1_o, tb2_o, b1_o, *vec_o):
    count, piece, lanes = d1.shape
    gim_o[...] = gim[...].astype(F32)
    w2_o[...] = d2[...].astype(F32)
    w1_o[...] = jnp.transpose(d1[...].reshape(count * piece, lanes)).astype(F32)

    @pl.when(pl.program_id(0) == 0)
    def _():
        aa, ba = lax.axis_index("aa"), lax.axis_index("ba")
        patches = tw1_o.shape[0]
        tw1_o[...] = small[0:patches, :].astype(F32)
        tw2_o[...] = small[200 : 200 + patches, :].astype(F32)
        tb1_o[...] = small[400:401, :].astype(F32).reshape(tb1_o.shape)
        tb2_o[...] = small[408:409, 0:patches].astype(F32).reshape(patches)
        rows = small[416:424, :].astype(F32)
        rows = jnp.where(ba == 0, rows[:, :piece], rows[:, piece:])
        rows = jnp.concatenate([rows[q : q + 1, :] for q in range(RING)], axis=1)
        b1_o[...] = rows.reshape(b1_o.shape)
        rows = jnp.where(aa == 0, small[424:432, :].astype(F32), small[432:440, :].astype(F32))
        for k, ref in enumerate(vec_o):
            ref[...] = rows[k : k + 1, :].reshape(ref.shape)


def local(groups, images, counts, ln1_gain, ln1_bias, tok_w1, tok_b1, tok_w2, tok_b2,
          ln2_gain, ln2_bias, ch_w1, ch_b1, ch_w2, ch_b2, cotangent):
    slots, patches, half = images.shape
    chans = 2 * half
    imgs = slots // 2
    pad = -(-patches // 16) * 16
    hidden = ch_w1.shape[1]
    piece = hidden // RING
    both = piece - 2 * SOLO
    keep_rows = SOLO + both
    hid_tok = tok_w1.shape[1]
    total = 448
    flies = 3
    while RING * groups > 2**flies:
        flies += 1
    his = max(flies - 3, 1)
    vmem = pl.BlockSpec(memory_space=pltpu.VMEM)
    hbm = pl.BlockSpec(memory_space=pl.ANY)
    dma = pltpu.SemaphoreType.DMA
    per_image = [dma((imgs,))] * 3
    out, gim, d2, d1, small, _ = pl.pallas_call(
        functools.partial(layer_kernel, groups),
        out_shape=[
            jax.ShapeDtypeStruct((slots, patches, half), BF16),
            jax.ShapeDtypeStruct((slots, patches, half), BF16),
            jax.ShapeDtypeStruct((RING, piece, chans), BF16),
            jax.ShapeDtypeStruct((RING, piece, chans), BF16),
            jax.ShapeDtypeStruct((total, hid_tok), BF16),
            jax.ShapeDtypeStruct((his, 2, piece if groups > 1 else 16, chans), BF16),
        ],
        in_specs=[pl.BlockSpec(memory_space=pltpu.SMEM), hbm, hbm]
        + [vmem] * 9
        + [hbm] * 2
        + [vmem],
        out_specs=[hbm] * 4 + [vmem, hbm],
        scratch_shapes=[
            pltpu.VMEM((2, imgs, patches, half), BF16),
            pltpu.VMEM((2, imgs, patches, half), BF16),
            pltpu.VMEM((imgs * pad, chans), BF16),
            pltpu.VMEM((imgs * pad, chans), BF16),
            pltpu.VMEM((imgs, patches, chans), F32),
            pltpu.VMEM((imgs * pad, chans), F32),
            pltpu.VMEM((RING, 2 * piece, chans), BF16),
            pltpu.VMEM((RING, 2 * piece, chans), BF16),
            pltpu.VMEM((RING, imgs * pad, 2 * piece), BF16),
            pltpu.VMEM((RING, imgs * pad, 2 * piece), BF16),
            pltpu.VMEM((imgs, patches, 4), F32),
            pltpu.VMEM((SLOTS, 2, 2 * piece, chans), BF16),
            pltpu.VMEM((RING, 2, piece, chans), BF16),
            pltpu.VMEM((RING, 2, SOLO, chans), BF16),
            pltpu.VMEM((RING, 2, SOLO, chans), F32),
            pltpu.VMEM((RING, 2, keep_rows, chans), BF16),
            pltpu.VMEM((2, both, chans), BF16),
            pltpu.VMEM((2, piece, chans), BF16),
            pltpu.VMEM((2, 8, half), F32),
            pltpu.VMEM((2, 1, hidden), F32),
            pltpu.VMEM((RING, 2 * piece), F32),
            pltpu.VMEM((hid_tok, 1), F32),
            pltpu.VMEM((patches, 1), F32),
            pltpu.VMEM((8, chans), F32),
            pltpu.VMEM((total, hid_tok), F32),
            pltpu.VMEM((total // 2, hid_tok), F32),
            pltpu.VMEM((total // 4, hid_tok), F32),
            pltpu.VMEM((flies, total // 4, hid_tok), BF16),
            pltpu.VMEM((flies, total // 4, hid_tok), BF16),
            *per_image,
            *per_image,
            dma((5,)),
            dma((4,)),
            dma((4,)),
            dma((RING, 2)),
            dma((RING, 2)),
            dma((RING, 2)),
            dma((RING, 2)),
            dma((RING, 2, 3)),
            dma((RING, 2, 3)),
            dma((1 + his, 2, 3)),
            dma((1 + his, 2, 3)),
            dma((RING, 2, 3)),
            dma((RING, 2, 3)),
            dma((2, 3)),
            *per_image,
            *per_image,
            dma((4 + flies,)),
            dma((4 + flies,)),
        ],
        compiler_params=pltpu.CompilerParams(
            collective_id=0, has_side_effects=True, vmem_limit_bytes=65100 * 1024
        ),
    )(
        counts,
        images,
        cotangent,
        ln1_gain,
        ln1_bias,
        ln2_gain,
        ln2_bias,
        ch_b2,
        tok_w1,
        tok_b1,
        tok_w2.T,
        tok_b2,
        ch_w1,
        ch_w2.reshape(RING, piece, chans),
        ch_b1,
    )
    steps = chans // 128
    row = jax.ShapeDtypeStruct((half,), F32)

    def whole(*shape):
        return pl.BlockSpec(shape, lambda k: (0,) * len(shape))

    some = pl.BlockSpec((slots // steps, patches, half), lambda k: (k, 0, 0))
    gim, w2, w1, tw1, tw2, tb1, tb2, b1, g1, n1, g2, n2, c2 = pl.pallas_call(
        finish_kernel,
        grid=(steps,),
        out_shape=[
            jax.ShapeDtypeStruct((slots, patches, half), F32),
            jax.ShapeDtypeStruct((hidden, chans), F32),
            jax.ShapeDtypeStruct((chans, hidden), F32),
            jax.ShapeDtypeStruct((patches, hid_tok), F32),
            jax.ShapeDtypeStruct((patches, hid_tok), F32),
            jax.ShapeDtypeStruct((hid_tok,), F32),
            jax.ShapeDtypeStruct((patches,), F32),
            jax.ShapeDtypeStruct((hidden,), F32),
        ]
        + [row] * 5,
        in_specs=[
            some,
            pl.BlockSpec((hidden // steps, chans), lambda k: (k, 0)),
            pl.BlockSpec((RING, piece, 128), lambda k: (0, 0, k)),
            whole(total, hid_tok),
        ],
        out_specs=[
            some,
            pl.BlockSpec((hidden // steps, chans), lambda k: (k, 0)),
            pl.BlockSpec((128, hidden), lambda k: (k, 0)),
            whole(patches, hid_tok),
            whole(patches, hid_tok),
            whole(hid_tok),
            whole(patches),
            whole(hidden),
        ]
        + [whole(half)] * 5,
        compiler_params=pltpu.CompilerParams(vmem_limit_bytes=62 * 2**20),
    )(gim, d2.reshape(hidden, chans), d1, small)
    return out, gim, g1, n1, tw1, tb1, tw2.T, tb2, g2, n2, w1, b1, w2, c2


def solution(mesh):
    rows = P(("dp", "ba"), None, "aa")
    chan = P("aa")
    placed = (rows, P(("dp", "ba")), chan, chan, P(), P(), P(), P(), chan, chan,
              P(None, "ba"), P("ba"), P("ba", None), chan, rows)
    given = (rows, rows, chan, chan, P(), P(), P(), P(), chan, chan,
             P(None, "ba"), P("ba"), P("ba", None), chan)
    return jax.shard_map(
        functools.partial(local, mesh.shape["dp"] // RING),
        mesh=mesh,
        in_specs=placed,
        out_specs=given,
        check_vma=False,
    )
```

```python
import functools

import jax
import jax.numpy as jnp
from jax import lax
from jax.experimental import pallas as pl
from jax.experimental.pallas import tpu as pltpu
from jax.sharding import PartitionSpec as P

MESH = pl.DeviceIdType.MESH
EPS = 1e-06
C0 = 0.7978845608028654
C1 = C0 * 0.044715
RING = 8
CHUNKS = 3
SOLO = 48
SLOTS = 3
SMALL_STEPS = 7
PLAN = (
    ("D", 0), ("G", 0), ("I", 0), ("S", 0, 0, 1), ("S", 0, 0, 2), ("F", 0, 0), ("D", 1), ("I", 1),
    ("S", 0, 1, 1), ("S", 0, 1, 2), ("F", 0, 1), ("D", 2), ("S", 1, 0, 1), ("F", 1, 0),
    ("Z", 0, 0), ("G", 1), ("S", 1, 1, 1), ("S", 1, 0, 2), ("F", 1, 1), ("F", 2, 0), ("Z", 0, 1),
    ("I", 2), ("S", 1, 1, 2), ("S", 2, 0, 1), ("D", 3), ("Z", 1, 0), ("O", 0), ("I", 3),
    ("S", 2, 1, 1), ("F", 2, 1), ("S", 2, 0, 2), ("D", 4), ("F", 3, 0), ("Z", 1, 1), ("G", 2),
    ("S", 2, 1, 2), ("S", 3, 0, 1), ("F", 3, 1), ("F", 4, 0), ("Z", 2, 0), ("S", 3, 1, 1),
    ("I", 4), ("S", 3, 0, 2), ("D", 5), ("Z", 2, 1), ("I", 5), ("S", 3, 1, 2), ("S", 4, 0, 1),
    ("F", 4, 1), ("D", 6), ("S", 4, 1, 1), ("F", 5, 0), ("Z", 3, 0), ("G", 3), ("S", 4, 0, 2),
    ("F", 5, 1), ("F", 6, 0), ("Z", 3, 1), ("S", 5, 0, 1), ("I", 6), ("S", 4, 1, 2), ("D", 7),
    ("S", 5, 1, 1), ("Z", 4, 0), ("I", 7), ("S", 5, 0, 2), ("F", 6, 1), ("Z", 4, 1), ("Y", 0),
    ("S", 5, 1, 2), ("S", 6, 0, 1), ("F", 7, 0), ("F", 7, 1), ("Y", 1), ("S", 6, 1, 1),
    ("Z", 5, 0), ("S", 6, 0, 2), ("Y", 2), ("S", 7, 0, 1), ("Z", 5, 1), ("S", 6, 1, 2), ("Y", 3),
    ("S", 7, 1, 1), ("Z", 6, 0), ("T", 0), ("E", 0, 1), ("S", 7, 0, 2), ("S", 7, 1, 2),
    ("Z", 6, 1), ("E", 1, 1), ("Z", 7, 0), ("T", 1), ("P", 0, 0, 1), ("E", 0, 2), ("Z", 7, 1),
    ("T", 2), ("E", 1, 2), ("P", 0, 1, 1), ("O", 1), ("P", 1, 0, 1), ("E", 0, 0), ("T", 3),
    ("E", 1, 0), ("P", 0, 0, 2), ("P", 0, 1, 2), ("O", 2), ("P", 2, 0, 1), ("T", 4),
    ("P", 1, 1, 1), ("O", 3), ("T", 5), ("P", 0, 0, 0), ("P", 0, 1, 0), ("P", 1, 0, 2), ("R", 0),
    ("O", 4), ("P", 1, 1, 2), ("P", 3, 0, 1), ("R", 1), ("P", 2, 1, 1), ("P", 1, 0, 0),
    ("P", 1, 1, 0), ("P", 2, 0, 2), ("P", 2, 1, 2), ("P", 4, 0, 1), ("O", 5), ("P", 3, 1, 1),
    ("R", 2), ("P", 2, 0, 0), ("M", 0), ("P", 2, 1, 0), ("P", 3, 0, 2), ("P", 3, 1, 2),
    ("P", 5, 0, 1), ("M", 1), ("P", 4, 1, 1), ("R", 3), ("M", 2), ("P", 3, 1, 0), ("P", 3, 0, 0),
    ("P", 4, 1, 2), ("P", 4, 0, 2), ("M", 3), ("P", 5, 1, 1), ("P", 6, 0, 1), ("M", 4), ("R", 4),
    ("P", 4, 0, 0), ("P", 4, 1, 0), ("P", 5, 0, 2), ("M", 5), ("P", 5, 1, 2), ("P", 6, 1, 1),
    ("R", 5), ("P", 5, 0, 0), ("P", 5, 1, 0), ("P", 6, 0, 2), ("P", 6, 1, 2), ("R", 6), ("R", 7),
    ("P", 6, 0, 0), ("P", 6, 1, 0),
)
F32 = jnp.float32
BF16 = jnp.bfloat16


def dot(left, right, left_dim, right_dim):
    return lax.dot_general(
        left, right, (((left_dim,), (right_dim,)), ((), ())), preferred_element_type=F32
    )


def gelu(v):
    return v * (0.5 * jnp.tanh(v * (C0 + C1 * (v * v))) + 0.5)


def gelu_both(v):
    v2 = v * v
    h = 0.5 * jnp.tanh(v * (C0 + C1 * v2)) + 0.5
    return v * h, h + (h - h * h) * (v * (2 * C0 + 6 * C1 * v2))


def mod(v):
    return lax.rem(v + 2 * RING, RING)


def flip(index, step):
    return index + step - 2 * step * lax.rem(lax.div(index, step), 2)


def column(row, length):
    return jnp.transpose(jnp.broadcast_to(row.reshape(1, length), (8, length)))[:, 0:1]


def layer_kernel(
    groups,
    counts,
    images,
    cot,
    gain1,
    bias1,
    gain2,
    bias2,
    biasc,
    tw1,
    tb1,
    tw2,
    tb2,
    w1_own,
    w2_own,
    b1_own,
    out_o,
    gim_o,
    d2_o,
    d1_o,
    small_o,
    xh,
    xb,
    cb,
    y2b,
    gb,
    res,
    acc,
    w1b,
    w2b,
    act,
    dg,
    stat,
    pb,
    bar,
    xr,
    held,
    rs,
    xs,
    fs,
    vecb,
    b1h,
    b1v,
    t1v,
    t2v,
    vacc,
    small,
    small_c,
    small_x,
    small_s,
    small_r,
    loc_x,
    snd_x,
    rcv_x,
    loc_c,
    snd_c,
    rcv_c,
    loc_w,
    snd_w,
    rcv_w,
    snd_b,
    rcv_b,
    snd_h,
    rcv_h,
    snd_r,
    rcv_r,
    snd_e,
    rcv_e,
    snd_g,
    rcv_g,
    loc_g,
    loc_o,
    snd_o,
    rcv_o,
    loc_i,
    snd_i,
    rcv_i,
    snd_s,
    rcv_s,
):
    _, imgs, patches, half = xb.shape
    chans = 2 * half
    pad = y2b.shape[0] // imgs
    piece = w2_own.shape[1]
    both = piece - 2 * SOLO
    dp, aa, ba = lax.axis_index("dp"), lax.axis_index("aa"), lax.axis_index("ba")
    lo, hi = lax.rem(dp, RING), lax.div(dp, RING)
    pos = jnp.where(lax.rem(lo, 2) == 0, lax.div(lo, 2), RING - 1 - lax.div(lo, 2))

    def at(place):
        place = mod(place)
        return hi * RING + jnp.where(
            place < RING // 2, 2 * place, 2 * (RING - 1 - place) + 1
        )

    dev_x = (dp, 1 - aa, ba)
    dev_c = (dp, aa, 1 - ba)
    dev_ring = ((at(pos + 1), aa, ba), (at(pos - 1), aa, ba))
    dev_fly = []
    step = 1
    while step < RING * groups:
        dev_fly.append((flip(dp, step), aa, ba))
        step *= 2
    dev_hi = dev_fly[3:]
    peers = [dev_x, dev_c, *dev_ring, *dev_fly]
    barrier = pltpu.get_barrier_semaphore()
    for peer in peers:
        pl.semaphore_signal(barrier, inc=1, device_id=peer, device_id_type=MESH)

    rows_mine = pl.ds(pl.multiple_of(ba * piece, 64), piece)
    rows_other = pl.ds(pl.multiple_of((1 - ba) * piece, 64), piece)

    def remote(src, dst, send, recv, dev):
        return pltpu.make_async_remote_copy(
            src_ref=src,
            dst_ref=dst,
            send_sem=send,
            recv_sem=recv,
            device_id=dev,
            device_id_type=MESH,
        )

    def local_in(src, dst, sem, i):
        return pltpu.make_async_copy(src.at[aa * imgs + i], dst.at[aa, i], sem.at[i])

    def give(src, dst, send, recv, i):
        return remote(
            src.at[(1 - aa) * imgs + i], dst.at[aa, i], send.at[i], recv.at[i], dev_x
        )

    def take(src, dst, send, recv, i):
        return remote(
            src.at[(1 - aa) * imgs + i], dst.at[1 - aa, i], send.at[i], recv.at[i], dev_x
        )

    def wide(ref, i):
        return jnp.concatenate([ref[0, i], ref[1, i]], axis=1).astype(F32)

    def put(ref, i, rows):
        rows = rows.astype(BF16)
        ref[0, i] = rows[:, :half]
        ref[1, i] = rows[:, half:]

    cols = 2 * piece
    parts = w1_own.shape[1] // cols

    def w1_in(k):
        return pltpu.make_async_copy(
            w1_own.at[:, pl.ds(k * cols, cols)], act.at[k, pl.ds(0, chans), :], loc_w.at[1 + k]
        )

    for k in range(parts):
        w1_in(k).start()
    for i in range(imgs):
        local_in(images, xb, loc_x, i).start()
    w2_local = pltpu.make_async_copy(w2_own, w2b.at[:, rows_mine, :], loc_w.at[0])
    w2_local.start()
    for i in range(imgs):
        local_in(cot, cb, loc_c, i).start()
    for k, ref in enumerate((gain1, bias1, gain2, bias2, biasc)):
        vecb[aa, k : k + 1, :] = ref[...].reshape(1, half)
    b1h[ba] = b1_own[...].reshape(1, parts * cols)

    pl.semaphore_wait(barrier, len(peers))

    vec_copy = remote(vecb.at[aa], vecb.at[aa], snd_w.at[2], rcv_w.at[2], dev_x)
    vec_copy.start()
    for i in range(imgs):
        give(images, xb, snd_x, rcv_x, i).start()
    for i in range(imgs):
        give(cot, cb, snd_c, rcv_c, i).start()
    b1_copy = remote(b1h.at[ba], b1h.at[ba], snd_w.at[3], rcv_w.at[3], dev_c)
    b1_copy.start()
    w2_copy = remote(w2_own, w2b.at[:, rows_mine, :], snd_w.at[0], rcv_w.at[0], dev_c)
    w2_copy.start()
    y2b[...] = jnp.zeros(y2b.shape, BF16)
    gb[...] = jnp.zeros(gb.shape, BF16)
    vacc[...] = jnp.zeros(vacc.shape, F32)
    small[...] = jnp.zeros(small.shape, F32)
    t1v[...] = column(tb1[...], t1v.shape[0])
    t2v[...] = column(tb2[...], patches)
    for k in range(parts):
        w1_in(k).wait()
        turned = jnp.transpose(act[k, 0:chans, :])
        w1b[2 * k, rows_mine, :] = turned[:piece]
        w1b[2 * k + 1, rows_mine, :] = turned[piece:]
    w1_copy = remote(
        w1b.at[:, rows_mine, :], w1b.at[:, rows_mine, :], snd_w.at[1], rcv_w.at[1], dev_c
    )
    w1_copy.start()
    vec_copy.wait_send()
    remote(vecb.at[aa], vecb.at[1 - aa], snd_w.at[2], rcv_w.at[2], dev_x).wait_recv()
    b1_copy.wait_send()
    remote(b1h.at[ba], b1h.at[1 - ba], snd_w.at[3], rcv_w.at[3], dev_c).wait_recv()
    for q in range(RING):
        b1v[q : q + 1, :] = jnp.concatenate(
            [b1h[0, :, q * piece : (q + 1) * piece], b1h[1, :, q * piece : (q + 1) * piece]],
            axis=1,
        )

    def vec(k):
        return jnp.concatenate([vecb[0, k : k + 1, :], vecb[1, k : k + 1, :]], axis=1)

    def token_forward(i):
        local_in(images, xb, loc_x, i).wait()
        take(images, xb, snd_x, rcv_x, i).wait()

        x = wide(xb, i)
        mean = jnp.mean(x, -1, keepdims=True)
        xc = x - mean
        rstd = lax.rsqrt(jnp.mean(xc * xc, -1, keepdims=True) + EPS)
        stat[i, :, 0 : 1] = mean
        stat[i, :, 1 : 2] = rstd
        y1 = (xc * rstd * vec(0) + vec(1)).astype(BF16)
        hid = gelu(dot(tw1[...], y1, 0, 0) + t1v[...]).astype(BF16)
        row = x + dot(tw2[...], hid, 1, 0) + t2v[...]
        res[i] = row
        mean = jnp.mean(row, -1, keepdims=True)
        xc = row - mean
        rstd = lax.rsqrt(jnp.mean(xc * xc, -1, keepdims=True) + EPS)
        stat[i, :, 2 : 3] = mean
        stat[i, :, 3 : 4] = rstd
        y2 = (xc * rstd * vec(2) + vec(3)).astype(BF16)
        y2b[pl.ds(pl.multiple_of(i * pad, 16), patches), :] = y2

    def weight(i):
        return jnp.where(aa * imgs + i < counts[0], 1.0, 0.0).astype(F32)

    chunks = 3
    size = y2b.shape[0] // chunks
    each = imgs // chunks

    def chan_forward(chunk, pair):
        rows = pl.ds(pl.multiple_of(chunk * size, 16), size)
        win = w1b[pl.ds(2 * pair, 2)].reshape(2 * cols, chans)
        wout = w2b[pl.ds(2 * pair, 2)].reshape(2 * cols, chans)
        bias = jnp.concatenate(
            [b1v[pl.ds(2 * pair, 1), :], b1v[pl.ds(2 * pair + 1, 1), :]], axis=1
        )
        val, der = gelu_both(dot(y2b[rows, :], win, 1, 1) + bias)
        val = val.astype(BF16)
        der = der.astype(BF16)
        act[2 * pair, rows, :] = val[:, :cols]
        act[2 * pair + 1, rows, :] = val[:, cols:]
        dg[2 * pair, rows, :] = der[:, :cols]
        dg[2 * pair + 1, rows, :] = der[:, cols:]
        new = dot(val, wout, 1, 0)
        acc[rows, :] = jnp.where(pair == 0, 0.0, acc[rows, :]) + new

    def forward_chunk(chunk, carry):
        def one(k, carry):
            token_forward(chunk * each + k)
            return carry

        lax.fori_loop(0, each, one, 0)

        @pl.when(chunk == 0)
        def _():
            w2_local.wait()
            w2_copy.wait_send()
            remote(
                w2_own, w2b.at[:, rows_other, :], snd_w.at[0], rcv_w.at[0], dev_c
            ).wait_recv()
            w1_copy.wait_send()
            remote(
                w1b.at[:, rows_mine, :], w1b.at[:, rows_other, :], snd_w.at[1], rcv_w.at[1], dev_c
            ).wait_recv()

        def two(k, carry):
            chan_forward(chunk, k)
            return carry

        lax.fori_loop(0, RING // 2, two, 0)
        return carry

    lax.fori_loop(0, chunks, forward_chunk, 0)
    def out_local(i):
        return pltpu.make_async_copy(cb.at[aa, i], out_o.at[aa * imgs + i], loc_o.at[i])

    def out_remote(i, sender):
        return remote(
            cb.at[1 - aa, i], out_o.at[sender * imgs + i], snd_o.at[i], rcv_o.at[i], dev_x
        )

    def mask_cot(i, carry):
        local_in(cot, cb, loc_c, i).wait()
        take(cot, cb, snd_c, rcv_c, i).wait()
        rows = pl.ds(pl.multiple_of(i * pad, 16), patches)
        scale = weight(i)
        gb[rows, :] = (wide(cb, i) * scale).astype(BF16)
        put(cb, i, scale * (res[i] + acc[rows, :] + vec(4)))
        return carry

    lax.fori_loop(0, imgs, mask_cot, 0)

    def grad_local(i):
        return pltpu.make_async_copy(xb.at[aa, i], gim_o.at[aa * imgs + i], loc_i.at[i])

    def grad_remote(i, sender):
        return remote(
            xb.at[1 - aa, i], gim_o.at[sender * imgs + i], snd_i.at[i], rcv_i.at[i], dev_x
        )

    ones = jnp.ones((8, chans), BF16)

    def token_backward(i):
        rows = pl.ds(i * pad, patches)
        up = acc[rows, :]
        grad_out = gb[rows, :].astype(F32)
        rstd = stat[i, :, 3 : 4]
        normed = (res[i] - stat[i, :, 2 : 3]) * rstd
        vacc[2:3, :] += jnp.sum(up * normed, 0, keepdims=True)
        vacc[3:4, :] += jnp.sum(up, 0, keepdims=True)
        vacc[4:5, :] += jnp.sum(grad_out, 0, keepdims=True)
        q = up * vec(2)
        mean = jnp.mean(q, -1, keepdims=True)
        proj = jnp.mean(q * normed, -1, keepdims=True)
        grad_res = grad_out + rstd * (q - mean - normed * proj)
        grad_tok = grad_res.astype(BF16)
        rstd = stat[i, :, 1 : 2]
        normed = (wide(xb, i) - stat[i, :, 0 : 1]) * rstd
        y1 = (normed * vec(0) + vec(1)).astype(BF16)
        val, der = gelu_both(dot(tw1[...], y1, 0, 0) + t1v[...])
        small[200 : 200 + patches, :] += dot(grad_tok, val.astype(BF16), 1, 1)
        small[408:416, 0:patches] += dot(ones, grad_tok, 1, 1)
        grad_pre = (dot(tw2[...], grad_tok, 0, 0) * der).astype(BF16)
        small[0:patches, :] += dot(y1, grad_pre, 1, 1)
        small[400:408, :] += dot(ones, grad_pre, 1, 1)
        up = dot(tw1[...], grad_pre, 1, 0)
        vacc[0:1, :] += jnp.sum(up * normed, 0, keepdims=True)
        vacc[1:2, :] += jnp.sum(up, 0, keepdims=True)
        q = up * vec(0)
        mean = jnp.mean(q, -1, keepdims=True)
        proj = jnp.mean(q * normed, -1, keepdims=True)
        put(xb, i, grad_res + rstd * (q - mean - normed * proj))

    solo_mine = pl.ds(pl.multiple_of(aa * SOLO, 16), SOLO)
    solo_other = pl.ds(pl.multiple_of((1 - aa) * SOLO, 16), SOLO)
    part = both // 2
    ring_rows = (pl.ds(0, SOLO), pl.ds(SOLO, part), pl.ds(SOLO + part, part))
    own_at = (aa * SOLO, 2 * SOLO, 2 * SOLO + part)
    last = RING - 1

    def own_rows(place, size):
        return pl.ds(pl.multiple_of(ba * piece + place, 16), size)

    def to_core(s, a):
        return remote(
            pb.at[s % SLOTS, a, rows_other, :],
            bar.at[s, a],
            snd_b.at[s, a],
            rcv_b.at[s, a],
            dev_c,
        )

    def to_x(s, a):
        return remote(
            bar.at[s, a, solo_other, :], xr.at[s, a], snd_h.at[s, a], rcv_h.at[s, a], dev_x
        )

    def to_ring(s, a, c):
        return remote(
            rs.at[s, a, ring_rows[c], :],
            rs.at[s + 1, a, ring_rows[c], :],
            snd_r.at[s, a, c],
            rcv_r.at[s, a, c],
            dev_ring[a],
        )

    def swap(a, c):
        src = rs.at[last, a, ring_rows[c], :]
        dst = fs.at[a, solo_mine, :] if c == 0 else xs.at[a, pl.ds((c - 1) * part, part), :]
        return remote(src, dst, snd_e.at[0, a, c], rcv_e.at[0, a, c], dev_x)

    arrived = set()

    def core_arrival(s, a):
        if (s, a) not in arrived:
            arrived.add((s, a))
            to_core(s, a).wait_recv()

    def lefts(k):
        return mod(pos + 1 + 2 * k), mod(pos + 2 + 2 * k)

    def weight_out(j):
        if j >= SLOTS:
            to_core(j - SLOTS, 0).wait_send()
        pb[j % SLOTS, 0] = dot(act[mod(pos - 1 - j)], gb[...], 0, 0).astype(BF16)
        to_core(j, 0).start()

    def weight_in(j):
        if j >= SLOTS:
            to_core(j - SLOTS, 1).wait_send()
        pb[j % SLOTS, 1] = dot(dg[mod(pos + 1 + j)], y2b[...], 0, 0).astype(BF16)
        to_core(j, 1).start()

    def grad_hidden(k):
        pair = lefts(k)
        rows = jnp.concatenate([w2b[n] for n in pair], axis=0)
        slope = jnp.concatenate([dg[n] for n in pair], axis=1).astype(F32)
        grad = (dot(gb[...], rows, 1, 1) * slope).astype(BF16)
        total = jnp.sum(grad.astype(F32), 0, keepdims=True)
        for n, left in enumerate(pair):
            dg[left] = grad[:, n * cols : (n + 1) * cols]
            small[pl.ds(416 + left, 1), :] = total[:, n * cols : (n + 1) * cols]

    def grad_rows(k):
        pair = lefts(k)
        grad = jnp.concatenate([dg[n] for n in pair], axis=1)
        new = dot(grad, jnp.concatenate([w1b[n] for n in pair], axis=0), 1, 0)
        acc[...] = new if k == 0 else acc[...] + new

    def first_sum(s, a):
        core_arrival(s, a)
        own = own_rows((1 - aa) * SOLO, SOLO)
        total = pb[s % SLOTS, a, own, :].astype(F32) + bar[s, a, solo_other, :].astype(F32)
        bar[s, a, solo_other, :] = total.astype(BF16)
        to_x(s, a).start()
        own = own_rows(aa * SOLO, SOLO)
        held[s, a] = pb[s % SLOTS, a, own, :].astype(F32) + bar[s, a, solo_mine, :].astype(F32)

    def pass_sum(s, a, c, total):
        if s > 0:
            to_ring(s - 1, a, c).wait_recv()
            total = total + rs[s, a, ring_rows[c], :].astype(F32)
        total = total.astype(BF16)
        rs[s, a, ring_rows[c], :] = total
        if s < last:
            to_ring(s, a, c).start()
        else:
            if c == 0:
                fs[a, solo_mine, :] = total
            swap(a, c).start()

    def shared_sum(s, a, c):
        core_arrival(s, a)
        total = pb[s % SLOTS, a, own_rows(own_at[c], part), :].astype(F32)
        pass_sum(s, a, c, total + bar[s, a, pl.ds(own_at[c], part), :].astype(F32))

    def solo_sum(s, a):
        to_x(s, a).wait()
        pass_sum(s, a, 0, held[s, a] + xr[s, a].astype(F32))

    def send_out(i):
        out_local(i).start()
        out_remote(i, aa).start()

    def send_grad(i):
        grad_local(i).start()
        grad_remote(i, aa).start()

    results = (d2_o, d1_o)
    gather_rows = (pl.ds(0, 2 * SOLO), pl.ds(2 * SOLO, part), pl.ds(2 * SOLO + part, part))

    def gather(t, a, c, src):
        q = mod(pos - t) if a == 0 else mod(pos + t)
        dst = results[a].at[q, gather_rows[c], :]
        return remote(
            dst if src is None else src, dst, snd_g.at[t, a, c], rcv_g.at[t, a, c], dev_ring[a]
        )

    def gather_arrival(t, a, c):
        q = mod(pos - 1 - t) if a == 0 else mod(pos + 1 + t)
        dst = results[a].at[q, gather_rows[c], :]
        return remote(dst, dst, snd_g.at[t, a, c], rcv_g.at[t, a, c], dev_ring[a])

    def keep(a, c):
        return pltpu.make_async_copy(
            fs.at[a, gather_rows[c], :], results[a].at[pos, gather_rows[c], :], loc_g.at[a, c]
        )

    def start_gather(a, c):
        rows = gather_rows[c]
        swap(a, c).wait_send()
        if c == 0:
            region = fs.at[a, solo_other, :]
            remote(region, region, snd_e.at[0, a, c], rcv_e.at[0, a, c], dev_x).wait_recv()
        else:
            swap(a, c).wait_recv()
            fs[a, rows, :] = (
                rs[last, a, ring_rows[c], :].astype(F32)
                + xs[a, (c - 1) * part : c * part, :].astype(F32)
            ).astype(BF16)
        for k, dev in enumerate(dev_hi):
            landed = xh.at[k, a, rows, :]
            near = bar.at[0, a, pl.ds(0, rows.size), :]
            copy = remote(
                fs.at[a, rows, :], landed, snd_e.at[1 + k, a, c], rcv_e.at[1 + k, a, c], dev
            )
            copy.start()
            copy.wait()
            back = pltpu.make_async_copy(landed, near, loc_g.at[a, c])
            back.start()
            back.wait()
            fs[a, rows, :] = (
                fs[a, rows, :].astype(F32) + bar[0, a, : rows.size, :].astype(F32)
            ).astype(BF16)
        gather(0, a, c, fs.at[a, rows, :]).start()
        keep(a, c).start()

    def pass_on(t, a, c):
        gather_arrival(t, a, c).wait_recv()
        if t + 1 < RING - 1:
            gather(t + 1, a, c, None).start()

    total_rows = small.shape[0]
    half_rows, quarter = total_rows // 2, total_rows // 4
    own_half = pl.ds(pl.multiple_of(ba * half_rows, 32), half_rows)
    other_half = pl.ds(pl.multiple_of((1 - ba) * half_rows, 32), half_rows)
    own_quarter = pl.ds(pl.multiple_of(ba * half_rows + aa * quarter, 16), quarter)
    other_quarter = pl.ds(pl.multiple_of(ba * half_rows + (1 - aa) * quarter, 16), quarter)
    flies = len(dev_fly)

    small_steps = [
        remote(small.at[other_half, :], small_c, snd_s.at[0], rcv_s.at[0], dev_c),
        remote(small.at[other_quarter, :], small_x, snd_s.at[1], rcv_s.at[1], dev_x),
    ]
    for k, dev in enumerate(dev_fly):
        small_steps.append(
            remote(small_s.at[k], small_r.at[k], snd_s.at[2 + k], rcv_s.at[2 + k], dev)
        )
    for k, (rows, dev) in enumerate(((own_quarter, dev_x), (own_half, dev_c))):
        region = small_o.at[rows, :]
        n = 2 + flies + k
        small_steps.append(remote(region, region, snd_s.at[n], rcv_s.at[n], dev))

    def small_start(n):
        if n == 2:
            small_s[0] = small[own_quarter, :].astype(BF16)
        small_steps[n].start()

    def small_finish(n):
        if n < 2 + flies:
            small_steps[n].wait()
        if n == 0:
            small[own_half, :] += small_c[...]
        elif n == 1:
            small[own_quarter, :] += small_x[...]
        elif n < 2 + flies:
            total = small_s[n - 2].astype(F32) + small_r[n - 2].astype(F32)
            if n + 1 < 2 + flies:
                small_s[n - 1] = total.astype(BF16)
            else:
                small_o[own_quarter, :] = total.astype(BF16)
        else:
            rows = other_quarter if n == 2 + flies else other_half
            region = small_o.at[rows, :]
            small_steps[n].wait_send()
            remote(region, region, snd_s.at[n], rcv_s.at[n], dev_x).wait_recv()

    def small_step(n):
        if n == 0:
            small[424:432, :] = vacc[:, :half]
            small[432:440, :] = vacc[:, half:]
        else:
            small_finish(n - 1)
        if n < len(small_steps):
            small_start(n)

    work = {
        "D": weight_out,
        "I": weight_in,
        "G": grad_hidden,
        "Y": grad_rows,
        "F": first_sum,
        "S": shared_sum,
        "Z": solo_sum,
        "E": start_gather,
        "P": pass_on,
        "T": token_backward,
        "M": send_grad,
        "O": send_out,
        "R": small_step,
    }
    for name, *index in PLAN:
        work[name](*index)
    for n in range(SMALL_STEPS + 1, len(small_steps) + 1):
        small_step(n)

    for s in range(RING - SLOTS, RING):
        for a in range(2):
            to_core(s, a).wait_send()
    for a in range(2):
        for c in range(3):
            keep(a, c).wait()

    def drain_images(i, carry):
        out_local(i).wait()
        out_remote(i, 1 - aa).wait()
        grad_local(i).wait()
        grad_remote(i, 1 - aa).wait()
        return carry

    lax.fori_loop(0, imgs, drain_images, 0)

    for t in range(RING - 1):
        for a in range(2):
            for c in range(3):
                to_ring(t, a, c).wait_send()
                gather_arrival(t, a, c).wait_send()


def finish_kernel(gim, d2, d1, small, gim_o, w2_o, w1_o, tw1_o, tw2_o, tb1_o, tb2_o, b1_o, *rest):
    vec_o = rest[:5]
    gim_i, d2_i, d1_i, gim_f, d2_f, d1_f, sem_i, sem_o = rest[5:]
    count, piece, chans = d1.shape
    size = chans // CHUNKS
    rows = count * piece // CHUNKS
    some = gim.shape[0] // CHUNKS

    def parts(c, fetch):
        lanes, block, slots = (pl.ds(c * n, n) for n in (size, rows, some))
        if fetch:
            pairs = (
                (d1.at[:, :, lanes], d1_i.at[:, :, lanes]),
                (d2.at[block], d2_i.at[block]),
                (gim.at[slots], gim_i.at[slots]),
            )
        else:
            pairs = (
                (d1_f.at[lanes], w1_o.at[lanes]),
                (d2_f.at[block], w2_o.at[block]),
                (gim_f.at[slots], gim_o.at[slots]),
            )
        sem = sem_i if fetch else sem_o
        return [pltpu.make_async_copy(*pair, sem.at[c, n]) for n, pair in enumerate(pairs)]

    for c in range(CHUNKS):
        for copy in parts(c, True):
            copy.start()
    for c in range(CHUNKS):
        fetched, stored = parts(c, True), parts(c, False)
        fetched[0].wait()
        turned = d1_i[:, :, c * size : (c + 1) * size].reshape(count * piece, size)
        d1_f[c * size : (c + 1) * size] = jnp.transpose(turned).astype(F32)
        stored[0].start()
        fetched[1].wait()
        d2_f[c * rows : (c + 1) * rows] = d2_i[c * rows : (c + 1) * rows].astype(F32)
        stored[1].start()
        fetched[2].wait()
        gim_f[c * some : (c + 1) * some] = gim_i[c * some : (c + 1) * some].astype(F32)
        stored[2].start()
    aa, ba = lax.axis_index("aa"), lax.axis_index("ba")
    patches = tw1_o.shape[0]
    tw1_o[...] = small[0:patches, :].astype(F32)
    tw2_o[...] = small[200 : 200 + patches, :].astype(F32)
    tb1_o[...] = small[400:401, :].astype(F32).reshape(tb1_o.shape)
    tb2_o[...] = small[408:409, 0:patches].astype(F32).reshape(patches)
    vals = small[416:424, :].astype(F32)
    vals = jnp.where(ba == 0, vals[:, :piece], vals[:, piece:])
    vals = jnp.concatenate([vals[q : q + 1, :] for q in range(RING)], axis=1)
    b1_o[...] = vals.reshape(b1_o.shape)
    vals = jnp.where(aa == 0, small[424:432, :].astype(F32), small[432:440, :].astype(F32))
    for k, ref in enumerate(vec_o):
        ref[...] = vals[k : k + 1, :].reshape(ref.shape)
    for c in range(CHUNKS):
        for copy in parts(c, False):
            copy.wait()


def local(groups, images, counts, ln1_gain, ln1_bias, tok_w1, tok_b1, tok_w2, tok_b2,
          ln2_gain, ln2_bias, ch_w1, ch_b1, ch_w2, ch_b2, cotangent):
    slots, patches, half = images.shape
    chans = 2 * half
    imgs = slots // 2
    pad = -(-patches // 16) * 16
    hidden = ch_w1.shape[1]
    piece = hidden // RING
    both = piece - 2 * SOLO
    keep_rows = SOLO + both
    hid_tok = tok_w1.shape[1]
    total = 448
    flies = 3
    while RING * groups > 2**flies:
        flies += 1
    his = max(flies - 3, 1)
    vmem = pl.BlockSpec(memory_space=pltpu.VMEM)
    hbm = pl.BlockSpec(memory_space=pl.ANY)
    dma = pltpu.SemaphoreType.DMA
    per_image = [dma((imgs,))] * 3
    out, gim, d2, d1, small, _ = pl.pallas_call(
        functools.partial(layer_kernel, groups),
        out_shape=[
            jax.ShapeDtypeStruct((slots, patches, half), BF16),
            jax.ShapeDtypeStruct((slots, patches, half), BF16),
            jax.ShapeDtypeStruct((RING, piece, chans), BF16),
            jax.ShapeDtypeStruct((RING, piece, chans), BF16),
            jax.ShapeDtypeStruct((total, hid_tok), BF16),
            jax.ShapeDtypeStruct((his, 2, piece if groups > 1 else 16, chans), BF16),
        ],
        in_specs=[pl.BlockSpec(memory_space=pltpu.SMEM), hbm, hbm]
        + [vmem] * 9
        + [hbm] * 2
        + [vmem],
        out_specs=[hbm] * 4 + [vmem, hbm],
        scratch_shapes=[
            pltpu.VMEM((2, imgs, patches, half), BF16),
            pltpu.VMEM((2, imgs, patches, half), BF16),
            pltpu.VMEM((imgs * pad, chans), BF16),
            pltpu.VMEM((imgs * pad, chans), BF16),
            pltpu.VMEM((imgs, patches, chans), F32),
            pltpu.VMEM((imgs * pad, chans), F32),
            pltpu.VMEM((RING, 2 * piece, chans), BF16),
            pltpu.VMEM((RING, 2 * piece, chans), BF16),
            pltpu.VMEM((RING, imgs * pad, 2 * piece), BF16),
            pltpu.VMEM((RING, imgs * pad, 2 * piece), BF16),
            pltpu.VMEM((imgs, patches, 4), F32),
            pltpu.VMEM((SLOTS, 2, 2 * piece, chans), BF16),
            pltpu.VMEM((RING, 2, piece, chans), BF16),
            pltpu.VMEM((RING, 2, SOLO, chans), BF16),
            pltpu.VMEM((RING, 2, SOLO, chans), F32),
            pltpu.VMEM((RING, 2, keep_rows, chans), BF16),
            pltpu.VMEM((2, both, chans), BF16),
            pltpu.VMEM((2, piece, chans), BF16),
            pltpu.VMEM((2, 8, half), F32),
            pltpu.VMEM((2, 1, hidden), F32),
            pltpu.VMEM((RING, 2 * piece), F32),
            pltpu.VMEM((hid_tok, 1), F32),
            pltpu.VMEM((patches, 1), F32),
            pltpu.VMEM((8, chans), F32),
            pltpu.VMEM((total, hid_tok), F32),
            pltpu.VMEM((total // 2, hid_tok), F32),
            pltpu.VMEM((total // 4, hid_tok), F32),
            pltpu.VMEM((flies, total // 4, hid_tok), BF16),
            pltpu.VMEM((flies, total // 4, hid_tok), BF16),
            *per_image,
            *per_image,
            dma((5,)),
            dma((4,)),
            dma((4,)),
            dma((RING, 2)),
            dma((RING, 2)),
            dma((RING, 2)),
            dma((RING, 2)),
            dma((RING, 2, 3)),
            dma((RING, 2, 3)),
            dma((1 + his, 2, 3)),
            dma((1 + his, 2, 3)),
            dma((RING, 2, 3)),
            dma((RING, 2, 3)),
            dma((2, 3)),
            *per_image,
            *per_image,
            dma((4 + flies,)),
            dma((4 + flies,)),
        ],
        compiler_params=pltpu.CompilerParams(
            collective_id=0, has_side_effects=True, vmem_limit_bytes=65100 * 1024
        ),
    )(
        counts,
        images,
        cotangent,
        ln1_gain,
        ln1_bias,
        ln2_gain,
        ln2_bias,
        ch_b2,
        tok_w1,
        tok_b1,
        tok_w2.T,
        tok_b2,
        ch_w1,
        ch_w2.reshape(RING, piece, chans),
        ch_b1,
    )
    row = jax.ShapeDtypeStruct((half,), F32)
    gim, w2, w1, tw1, tw2, tb1, tb2, b1, g1, n1, g2, n2, c2 = pl.pallas_call(
        finish_kernel,
        out_shape=[
            jax.ShapeDtypeStruct((slots, patches, half), F32),
            jax.ShapeDtypeStruct((hidden, chans), F32),
            jax.ShapeDtypeStruct((chans, hidden), F32),
            jax.ShapeDtypeStruct((patches, hid_tok), F32),
            jax.ShapeDtypeStruct((patches, hid_tok), F32),
            jax.ShapeDtypeStruct((hid_tok,), F32),
            jax.ShapeDtypeStruct((patches,), F32),
            jax.ShapeDtypeStruct((hidden,), F32),
        ]
        + [row] * 5,
        in_specs=[hbm] * 3 + [vmem],
        out_specs=[hbm] * 3 + [vmem] * 10,
        scratch_shapes=[
            pltpu.VMEM((slots, patches, half), BF16),
            pltpu.VMEM((hidden, chans), BF16),
            pltpu.VMEM((RING, piece, chans), BF16),
            pltpu.VMEM((slots, patches, half), F32),
            pltpu.VMEM((hidden, chans), F32),
            pltpu.VMEM((chans, hidden), F32),
            dma((CHUNKS, 3)),
            dma((CHUNKS, 3)),
        ],
        compiler_params=pltpu.CompilerParams(vmem_limit_bytes=62 * 2**20),
    )(gim, d2.reshape(hidden, chans), d1, small)
    return out, gim, g1, n1, tw1, tb1, tw2.T, tb2, g2, n2, w1, b1, w2, c2


def solution(mesh):
    rows = P(("dp", "ba"), None, "aa")
    chan = P("aa")
    placed = (rows, P(("dp", "ba")), chan, chan, P(), P(), P(), P(), chan, chan,
              P(None, "ba"), P("ba"), P("ba", None), chan, rows)
    given = (rows, rows, chan, chan, P(), P(), P(), P(), chan, chan,
             P(None, "ba"), P("ba"), P("ba", None), chan)
    return jax.shard_map(
        functools.partial(local, mesh.shape["dp"] // RING),
        mesh=mesh,
        in_specs=placed,
        out_specs=given,
        check_vma=False,
    )
```

```python
import functools

import jax
import jax.numpy as jnp
from jax import lax
from jax.experimental import pallas as pl
from jax.experimental.pallas import tpu as pltpu
from jax.sharding import PartitionSpec as P

MESH = pl.DeviceIdType.MESH
EPS = 1e-06
C0 = 0.7978845608028654
C1 = C0 * 0.044715
RING = 8
CHUNKS = 3
SOLO = 48
SLOTS = 3
SMALL_STEPS = 7
PLAN = (
    ("D", 0), ("G", 0), ("I", 0), ("S", 0, 0, 1), ("S", 0, 0, 2), ("F", 0, 0), ("D", 1), ("I", 1),
    ("S", 0, 1, 1), ("S", 0, 1, 2), ("F", 0, 1), ("D", 2), ("S", 1, 0, 1), ("F", 1, 0),
    ("Z", 0, 0), ("G", 1), ("S", 1, 1, 1), ("S", 1, 0, 2), ("F", 1, 1), ("F", 2, 0), ("Z", 0, 1),
    ("I", 2), ("S", 1, 1, 2), ("S", 2, 0, 1), ("D", 3), ("Z", 1, 0), ("O", 0), ("I", 3),
    ("S", 2, 1, 1), ("F", 2, 1), ("S", 2, 0, 2), ("D", 4), ("F", 3, 0), ("Z", 1, 1), ("G", 2),
    ("S", 2, 1, 2), ("S", 3, 0, 1), ("F", 3, 1), ("F", 4, 0), ("Z", 2, 0), ("S", 3, 1, 1),
    ("I", 4), ("S", 3, 0, 2), ("D", 5), ("Z", 2, 1), ("I", 5), ("S", 3, 1, 2), ("S", 4, 0, 1),
    ("F", 4, 1), ("D", 6), ("S", 4, 1, 1), ("F", 5, 0), ("Z", 3, 0), ("G", 3), ("S", 4, 0, 2),
    ("F", 5, 1), ("F", 6, 0), ("Z", 3, 1), ("S", 5, 0, 1), ("I", 6), ("S", 4, 1, 2), ("D", 7),
    ("S", 5, 1, 1), ("Z", 4, 0), ("I", 7), ("S", 5, 0, 2), ("F", 6, 1), ("Z", 4, 1), ("Y", 0),
    ("S", 5, 1, 2), ("S", 6, 0, 1), ("F", 7, 0), ("F", 7, 1), ("Y", 1), ("S", 6, 1, 1),
    ("Z", 5, 0), ("S", 6, 0, 2), ("Y", 2), ("S", 7, 0, 1), ("Z", 5, 1), ("S", 6, 1, 2), ("Y", 3),
    ("S", 7, 1, 1), ("Z", 6, 0), ("T", 0), ("E", 0, 1), ("S", 7, 0, 2), ("S", 7, 1, 2),
    ("Z", 6, 1), ("E", 1, 1), ("Z", 7, 0), ("T", 1), ("P", 0, 0, 1), ("E", 0, 2), ("Z", 7, 1),
    ("T", 2), ("E", 1, 2), ("P", 0, 1, 1), ("O", 1), ("P", 1, 0, 1), ("E", 0, 0), ("T", 3),
    ("E", 1, 0), ("P", 0, 0, 2), ("P", 0, 1, 2), ("O", 2), ("P", 2, 0, 1), ("T", 4),
    ("P", 1, 1, 1), ("O", 3), ("T", 5), ("P", 0, 0, 0), ("P", 0, 1, 0), ("P", 1, 0, 2), ("R", 0),
    ("O", 4), ("P", 1, 1, 2), ("P", 3, 0, 1), ("R", 1), ("P", 2, 1, 1), ("P", 1, 0, 0),
    ("P", 1, 1, 0), ("P", 2, 0, 2), ("P", 2, 1, 2), ("P", 4, 0, 1), ("O", 5), ("P", 3, 1, 1),
    ("R", 2), ("P", 2, 0, 0), ("M", 0), ("P", 2, 1, 0), ("P", 3, 0, 2), ("P", 3, 1, 2),
    ("P", 5, 0, 1), ("M", 1), ("P", 4, 1, 1), ("R", 3), ("M", 2), ("P", 3, 1, 0), ("P", 3, 0, 0),
    ("P", 4, 1, 2), ("P", 4, 0, 2), ("M", 3), ("P", 5, 1, 1), ("P", 6, 0, 1), ("M", 4), ("R", 4),
    ("P", 4, 0, 0), ("P", 4, 1, 0), ("P", 5, 0, 2), ("M", 5), ("P", 5, 1, 2), ("P", 6, 1, 1),
    ("R", 5), ("P", 5, 0, 0), ("P", 5, 1, 0), ("P", 6, 0, 2), ("P", 6, 1, 2), ("R", 6), ("R", 7),
    ("P", 6, 0, 0), ("P", 6, 1, 0),
)
F32 = jnp.float32
BF16 = jnp.bfloat16


def dot(left, right, left_dim, right_dim):
    return lax.dot_general(
        left, right, (((left_dim,), (right_dim,)), ((), ())), preferred_element_type=F32
    )


def gelu(v):
    return v * (0.5 * jnp.tanh(v * (C0 + C1 * (v * v))) + 0.5)


def gelu_both(v):
    v2 = v * v
    h = 0.5 * jnp.tanh(v * (C0 + C1 * v2)) + 0.5
    return v * h, h + (h - h * h) * (v * (2 * C0 + 6 * C1 * v2))


def mod(v):
    return lax.rem(v + 2 * RING, RING)


def flip(index, step):
    return index + step - 2 * step * lax.rem(lax.div(index, step), 2)


def column(row, length):
    return jnp.transpose(jnp.broadcast_to(row.reshape(1, length), (8, length)))[:, 0:1]


def layer_kernel(
    groups,
    counts,
    images,
    cot,
    gain1,
    bias1,
    gain2,
    bias2,
    biasc,
    tw1,
    tb1,
    tw2,
    tb2,
    w1_own,
    w2_own,
    b1_own,
    out_o,
    gim_o,
    d2_o,
    d1_o,
    small_o,
    xh,
    xb,
    cb,
    y2b,
    gb,
    res,
    acc,
    w1b,
    w2b,
    act,
    dg,
    stat,
    pb,
    bar,
    xr,
    held,
    rs,
    xs,
    fs,
    vecb,
    b1h,
    b1v,
    t1v,
    t2v,
    vacc,
    small,
    small_c,
    small_x,
    small_s,
    small_r,
    loc_x,
    snd_x,
    rcv_x,
    loc_c,
    snd_c,
    rcv_c,
    loc_w,
    snd_w,
    rcv_w,
    snd_b,
    rcv_b,
    snd_h,
    rcv_h,
    snd_r,
    rcv_r,
    snd_e,
    rcv_e,
    snd_g,
    rcv_g,
    loc_g,
    loc_o,
    snd_o,
    rcv_o,
    loc_i,
    snd_i,
    rcv_i,
    snd_s,
    rcv_s,
):
    _, imgs, patches, half = xb.shape
    chans = 2 * half
    pad = y2b.shape[0] // imgs
    piece = w2_own.shape[1]
    both = piece - 2 * SOLO
    dp, aa, ba = lax.axis_index("dp"), lax.axis_index("aa"), lax.axis_index("ba")
    lo, hi = lax.rem(dp, RING), lax.div(dp, RING)
    pos = jnp.where(lax.rem(lo, 2) == 0, lax.div(lo, 2), RING - 1 - lax.div(lo, 2))

    def at(place):
        place = mod(place)
        return hi * RING + jnp.where(
            place < RING // 2, 2 * place, 2 * (RING - 1 - place) + 1
        )

    dev_x = (dp, 1 - aa, ba)
    dev_c = (dp, aa, 1 - ba)
    dev_ring = ((at(pos + 1), aa, ba), (at(pos - 1), aa, ba))
    dev_fly = []
    step = 1
    while step < RING * groups:
        dev_fly.append((flip(dp, step), aa, ba))
        step *= 2
    dev_hi = dev_fly[3:]
    peers = [dev_x, dev_c, *dev_ring, *dev_hi]
    barrier = pltpu.get_barrier_semaphore()
    for peer in peers:
        pl.semaphore_signal(barrier, inc=1, device_id=peer, device_id_type=MESH)

    rows_mine = pl.ds(pl.multiple_of(ba * piece, 64), piece)
    rows_other = pl.ds(pl.multiple_of((1 - ba) * piece, 64), piece)

    def remote(src, dst, send, recv, dev):
        return pltpu.make_async_remote_copy(
            src_ref=src,
            dst_ref=dst,
            send_sem=send,
            recv_sem=recv,
            device_id=dev,
            device_id_type=MESH,
        )

    def local_in(src, dst, sem, i):
        return pltpu.make_async_copy(src.at[aa * imgs + i], dst.at[aa, i], sem.at[i])

    def give(src, dst, send, recv, i):
        return remote(
            src.at[(1 - aa) * imgs + i], dst.at[aa, i], send.at[i], recv.at[i], dev_x
        )

    def take(src, dst, send, recv, i):
        return remote(
            src.at[(1 - aa) * imgs + i], dst.at[1 - aa, i], send.at[i], recv.at[i], dev_x
        )

    def wide(ref, i):
        return jnp.concatenate([ref[0, i], ref[1, i]], axis=1).astype(F32)

    def put(ref, i, rows):
        rows = rows.astype(BF16)
        ref[0, i] = rows[:, :half]
        ref[1, i] = rows[:, half:]

    cols = 2 * piece
    parts = w1_own.shape[1] // cols

    def w1_in(k):
        return pltpu.make_async_copy(
            w1_own.at[:, pl.ds(k * cols, cols)], act.at[k, pl.ds(0, chans), :], loc_w.at[1 + k]
        )

    for k in range(parts):
        w1_in(k).start()
    for i in range(imgs):
        local_in(images, xb, loc_x, i).start()
    w2_local = pltpu.make_async_copy(w2_own, w2b.at[:, rows_mine, :], loc_w.at[0])
    w2_local.start()
    for i in range(imgs):
        local_in(cot, cb, loc_c, i).start()
    for k, ref in enumerate((gain1, bias1, gain2, bias2, biasc)):
        vecb[aa, k : k + 1, :] = ref[...].reshape(1, half)
    b1h[ba] = b1_own[...].reshape(1, parts * cols)

    pl.semaphore_wait(barrier, len(peers))

    vec_copy = remote(vecb.at[aa], vecb.at[aa], snd_w.at[2], rcv_w.at[2], dev_x)
    vec_copy.start()
    for i in range(imgs):
        give(images, xb, snd_x, rcv_x, i).start()
    for i in range(imgs):
        give(cot, cb, snd_c, rcv_c, i).start()
    b1_copy = remote(b1h.at[ba], b1h.at[ba], snd_w.at[3], rcv_w.at[3], dev_c)
    b1_copy.start()
    w2_copy = remote(w2_own, w2b.at[:, rows_mine, :], snd_w.at[0], rcv_w.at[0], dev_c)
    w2_copy.start()
    y2b[...] = jnp.zeros(y2b.shape, BF16)
    gb[...] = jnp.zeros(gb.shape, BF16)
    vacc[...] = jnp.zeros(vacc.shape, F32)
    small[...] = jnp.zeros(small.shape, F32)
    t1v[...] = column(tb1[...], t1v.shape[0])
    t2v[...] = column(tb2[...], patches)
    for k in range(parts):
        w1_in(k).wait()
        turned = jnp.transpose(act[k, 0:chans, :])
        w1b[2 * k, rows_mine, :] = turned[:piece]
        w1b[2 * k + 1, rows_mine, :] = turned[piece:]
    w1_copy = remote(
        w1b.at[:, rows_mine, :], w1b.at[:, rows_mine, :], snd_w.at[1], rcv_w.at[1], dev_c
    )
    w1_copy.start()
    vec_copy.wait_send()
    remote(vecb.at[aa], vecb.at[1 - aa], snd_w.at[2], rcv_w.at[2], dev_x).wait_recv()
    b1_copy.wait_send()
    remote(b1h.at[ba], b1h.at[1 - ba], snd_w.at[3], rcv_w.at[3], dev_c).wait_recv()
    for q in range(RING):
        b1v[q : q + 1, :] = jnp.concatenate(
            [b1h[0, :, q * piece : (q + 1) * piece], b1h[1, :, q * piece : (q + 1) * piece]],
            axis=1,
        )

    def vec(k):
        return jnp.concatenate([vecb[0, k : k + 1, :], vecb[1, k : k + 1, :]], axis=1)

    def token_forward(i):
        local_in(images, xb, loc_x, i).wait()
        take(images, xb, snd_x, rcv_x, i).wait()

        x = wide(xb, i)
        mean = jnp.mean(x, -1, keepdims=True)
        xc = x - mean
        rstd = lax.rsqrt(jnp.mean(xc * xc, -1, keepdims=True) + EPS)
        stat[i, :, 0 : 1] = mean
        stat[i, :, 1 : 2] = rstd
        y1 = (xc * rstd * vec(0) + vec(1)).astype(BF16)
        hid = gelu(dot(tw1[...], y1, 0, 0) + t1v[...]).astype(BF16)
        row = x + dot(tw2[...], hid, 1, 0) + t2v[...]
        res[i] = row
        mean = jnp.mean(row, -1, keepdims=True)
        xc = row - mean
        rstd = lax.rsqrt(jnp.mean(xc * xc, -1, keepdims=True) + EPS)
        stat[i, :, 2 : 3] = mean
        stat[i, :, 3 : 4] = rstd
        y2 = (xc * rstd * vec(2) + vec(3)).astype(BF16)
        y2b[pl.ds(pl.multiple_of(i * pad, 16), patches), :] = y2

    def weight(i):
        return jnp.where(aa * imgs + i < counts[0], 1.0, 0.0).astype(F32)

    chunks = 3
    size = y2b.shape[0] // chunks
    each = imgs // chunks

    def chan_forward(chunk, pair):
        rows = pl.ds(pl.multiple_of(chunk * size, 16), size)
        win = w1b[pl.ds(2 * pair, 2)].reshape(2 * cols, chans)
        wout = w2b[pl.ds(2 * pair, 2)].reshape(2 * cols, chans)
        bias = jnp.concatenate(
            [b1v[pl.ds(2 * pair, 1), :], b1v[pl.ds(2 * pair + 1, 1), :]], axis=1
        )
        val, der = gelu_both(dot(y2b[rows, :], win, 1, 1) + bias)
        val = val.astype(BF16)
        der = der.astype(BF16)
        act[2 * pair, rows, :] = val[:, :cols]
        act[2 * pair + 1, rows, :] = val[:, cols:]
        dg[2 * pair, rows, :] = der[:, :cols]
        dg[2 * pair + 1, rows, :] = der[:, cols:]
        new = dot(val, wout, 1, 0)
        acc[rows, :] = jnp.where(pair == 0, 0.0, acc[rows, :]) + new

    def forward_chunk(chunk, carry):
        def one(k, carry):
            token_forward(chunk * each + k)
            return carry

        lax.fori_loop(0, each, one, 0)

        @pl.when(chunk == 0)
        def _():
            w2_local.wait()
            w2_copy.wait_send()
            remote(
                w2_own, w2b.at[:, rows_other, :], snd_w.at[0], rcv_w.at[0], dev_c
            ).wait_recv()
            w1_copy.wait_send()
            remote(
                w1b.at[:, rows_mine, :], w1b.at[:, rows_other, :], snd_w.at[1], rcv_w.at[1], dev_c
            ).wait_recv()

        def two(k, carry):
            chan_forward(chunk, k)
            return carry

        lax.fori_loop(0, RING // 2, two, 0)
        return carry

    lax.fori_loop(0, chunks, forward_chunk, 0)
    def out_local(i):
        return pltpu.make_async_copy(cb.at[aa, i], out_o.at[aa * imgs + i], loc_o.at[i])

    def out_remote(i, sender):
        return remote(
            cb.at[1 - aa, i], out_o.at[sender * imgs + i], snd_o.at[i], rcv_o.at[i], dev_x
        )

    def mask_cot(i, carry):
        local_in(cot, cb, loc_c, i).wait()
        take(cot, cb, snd_c, rcv_c, i).wait()
        rows = pl.ds(pl.multiple_of(i * pad, 16), patches)
        scale = weight(i)
        gb[rows, :] = (wide(cb, i) * scale).astype(BF16)
        put(cb, i, scale * (res[i] + acc[rows, :] + vec(4)))
        return carry

    lax.fori_loop(0, imgs, mask_cot, 0)

    def grad_local(i):
        return pltpu.make_async_copy(xb.at[aa, i], gim_o.at[aa * imgs + i], loc_i.at[i])

    def grad_remote(i, sender):
        return remote(
            xb.at[1 - aa, i], gim_o.at[sender * imgs + i], snd_i.at[i], rcv_i.at[i], dev_x
        )

    ones = jnp.ones((8, chans), BF16)

    def token_backward(i):
        rows = pl.ds(i * pad, patches)
        up = acc[rows, :]
        grad_out = gb[rows, :].astype(F32)
        rstd = stat[i, :, 3 : 4]
        normed = (res[i] - stat[i, :, 2 : 3]) * rstd
        vacc[2:3, :] += jnp.sum(up * normed, 0, keepdims=True)
        vacc[3:4, :] += jnp.sum(up, 0, keepdims=True)
        vacc[4:5, :] += jnp.sum(grad_out, 0, keepdims=True)
        q = up * vec(2)
        mean = jnp.mean(q, -1, keepdims=True)
        proj = jnp.mean(q * normed, -1, keepdims=True)
        grad_res = grad_out + rstd * (q - mean - normed * proj)
        grad_tok = grad_res.astype(BF16)
        rstd = stat[i, :, 1 : 2]
        normed = (wide(xb, i) - stat[i, :, 0 : 1]) * rstd
        y1 = (normed * vec(0) + vec(1)).astype(BF16)
        val, der = gelu_both(dot(tw1[...], y1, 0, 0) + t1v[...])
        small[200 : 200 + patches, :] += dot(grad_tok, val.astype(BF16), 1, 1)
        small[408:416, 0:patches] += dot(ones, grad_tok, 1, 1)
        grad_pre = (dot(tw2[...], grad_tok, 0, 0) * der).astype(BF16)
        small[0:patches, :] += dot(y1, grad_pre, 1, 1)
        small[400:408, :] += dot(ones, grad_pre, 1, 1)
        up = dot(tw1[...], grad_pre, 1, 0)
        vacc[0:1, :] += jnp.sum(up * normed, 0, keepdims=True)
        vacc[1:2, :] += jnp.sum(up, 0, keepdims=True)
        q = up * vec(0)
        mean = jnp.mean(q, -1, keepdims=True)
        proj = jnp.mean(q * normed, -1, keepdims=True)
        put(xb, i, grad_res + rstd * (q - mean - normed * proj))

    solo_mine = pl.ds(pl.multiple_of(aa * SOLO, 16), SOLO)
    solo_other = pl.ds(pl.multiple_of((1 - aa) * SOLO, 16), SOLO)
    part = both // 2
    ring_rows = (pl.ds(0, SOLO), pl.ds(SOLO, part), pl.ds(SOLO + part, part))
    own_at = (aa * SOLO, 2 * SOLO, 2 * SOLO + part)
    last = RING - 1

    def own_rows(place, size):
        return pl.ds(pl.multiple_of(ba * piece + place, 16), size)

    def to_core(s, a):
        return remote(
            pb.at[s % SLOTS, a, rows_other, :],
            bar.at[s, a],
            snd_b.at[s, a],
            rcv_b.at[s, a],
            dev_c,
        )

    def to_x(s, a):
        return remote(
            bar.at[s, a, solo_other, :], xr.at[s, a], snd_h.at[s, a], rcv_h.at[s, a], dev_x
        )

    def to_ring(s, a, c):
        return remote(
            rs.at[s, a, ring_rows[c], :],
            rs.at[s + 1, a, ring_rows[c], :],
            snd_r.at[s, a, c],
            rcv_r.at[s, a, c],
            dev_ring[a],
        )

    def swap(a, c):
        src = rs.at[last, a, ring_rows[c], :]
        dst = fs.at[a, solo_mine, :] if c == 0 else xs.at[a, pl.ds((c - 1) * part, part), :]
        return remote(src, dst, snd_e.at[0, a, c], rcv_e.at[0, a, c], dev_x)

    arrived = set()

    def core_arrival(s, a):
        if (s, a) not in arrived:
            arrived.add((s, a))
            to_core(s, a).wait_recv()

    def lefts(k):
        return mod(pos + 1 + 2 * k), mod(pos + 2 + 2 * k)

    def weight_out(j):
        if j >= SLOTS:
            to_core(j - SLOTS, 0).wait_send()
        pb[j % SLOTS, 0] = dot(act[mod(pos - 1 - j)], gb[...], 0, 0).astype(BF16)
        to_core(j, 0).start()

    def weight_in(j):
        if j >= SLOTS:
            to_core(j - SLOTS, 1).wait_send()
        pb[j % SLOTS, 1] = dot(dg[mod(pos + 1 + j)], y2b[...], 0, 0).astype(BF16)
        to_core(j, 1).start()

    def grad_hidden(k):
        pair = lefts(k)
        rows = jnp.concatenate([w2b[n] for n in pair], axis=0)
        slope = jnp.concatenate([dg[n] for n in pair], axis=1).astype(F32)
        grad = (dot(gb[...], rows, 1, 1) * slope).astype(BF16)
        total = jnp.sum(grad.astype(F32), 0, keepdims=True)
        for n, left in enumerate(pair):
            dg[left] = grad[:, n * cols : (n + 1) * cols]
            small[pl.ds(416 + left, 1), :] = total[:, n * cols : (n + 1) * cols]

    def grad_rows(k):
        pair = lefts(k)
        grad = jnp.concatenate([dg[n] for n in pair], axis=1)
        new = dot(grad, jnp.concatenate([w1b[n] for n in pair], axis=0), 1, 0)
        acc[...] = new if k == 0 else acc[...] + new

    def first_sum(s, a):
        core_arrival(s, a)
        own = own_rows((1 - aa) * SOLO, SOLO)
        total = pb[s % SLOTS, a, own, :].astype(F32) + bar[s, a, solo_other, :].astype(F32)
        bar[s, a, solo_other, :] = total.astype(BF16)
        to_x(s, a).start()
        own = own_rows(aa * SOLO, SOLO)
        held[s, a] = pb[s % SLOTS, a, own, :].astype(F32) + bar[s, a, solo_mine, :].astype(F32)

    def pass_sum(s, a, c, total):
        if s > 0:
            to_ring(s - 1, a, c).wait_recv()
            total = total + rs[s, a, ring_rows[c], :].astype(F32)
        total = total.astype(BF16)
        rs[s, a, ring_rows[c], :] = total
        if s < last:
            to_ring(s, a, c).start()
        else:
            if c == 0:
                fs[a, solo_mine, :] = total
            swap(a, c).start()

    def shared_sum(s, a, c):
        core_arrival(s, a)
        total = pb[s % SLOTS, a, own_rows(own_at[c], part), :].astype(F32)
        pass_sum(s, a, c, total + bar[s, a, pl.ds(own_at[c], part), :].astype(F32))

    def solo_sum(s, a):
        to_x(s, a).wait()
        pass_sum(s, a, 0, held[s, a] + xr[s, a].astype(F32))

    def send_out(i):
        out_local(i).start()
        out_remote(i, aa).start()

    def send_grad(i):
        grad_local(i).start()
        grad_remote(i, aa).start()

    results = (d2_o, d1_o)
    gather_rows = (pl.ds(0, 2 * SOLO), pl.ds(2 * SOLO, part), pl.ds(2 * SOLO + part, part))

    def gather(t, a, c, src):
        q = mod(pos - t) if a == 0 else mod(pos + t)
        dst = results[a].at[q, gather_rows[c], :]
        return remote(
            dst if src is None else src, dst, snd_g.at[t, a, c], rcv_g.at[t, a, c], dev_ring[a]
        )

    def gather_arrival(t, a, c):
        q = mod(pos - 1 - t) if a == 0 else mod(pos + 1 + t)
        dst = results[a].at[q, gather_rows[c], :]
        return remote(dst, dst, snd_g.at[t, a, c], rcv_g.at[t, a, c], dev_ring[a])

    def keep(a, c):
        return pltpu.make_async_copy(
            fs.at[a, gather_rows[c], :], results[a].at[pos, gather_rows[c], :], loc_g.at[a, c]
        )

    def start_gather(a, c):
        rows = gather_rows[c]
        swap(a, c).wait_send()
        if c == 0:
            region = fs.at[a, solo_other, :]
            remote(region, region, snd_e.at[0, a, c], rcv_e.at[0, a, c], dev_x).wait_recv()
        else:
            swap(a, c).wait_recv()
            fs[a, rows, :] = (
                rs[last, a, ring_rows[c], :].astype(F32)
                + xs[a, (c - 1) * part : c * part, :].astype(F32)
            ).astype(BF16)
        for k, dev in enumerate(dev_hi):
            landed = xh.at[k, a, rows, :]
            near = bar.at[0, a, pl.ds(0, rows.size), :]
            copy = remote(
                fs.at[a, rows, :], landed, snd_e.at[1 + k, a, c], rcv_e.at[1 + k, a, c], dev
            )
            copy.start()
            copy.wait()
            back = pltpu.make_async_copy(landed, near, loc_g.at[a, c])
            back.start()
            back.wait()
            fs[a, rows, :] = (
                fs[a, rows, :].astype(F32) + bar[0, a, : rows.size, :].astype(F32)
            ).astype(BF16)
        gather(0, a, c, fs.at[a, rows, :]).start()
        keep(a, c).start()

    def pass_on(t, a, c):
        gather_arrival(t, a, c).wait_recv()
        if t + 1 < RING - 1:
            gather(t + 1, a, c, None).start()

    total_rows = small.shape[0]
    half_rows, quarter = total_rows // 2, total_rows // 4
    own_half = pl.ds(pl.multiple_of(ba * half_rows, 32), half_rows)
    other_half = pl.ds(pl.multiple_of((1 - ba) * half_rows, 32), half_rows)
    own_quarter = pl.ds(pl.multiple_of(ba * half_rows + aa * quarter, 16), quarter)
    other_quarter = pl.ds(pl.multiple_of(ba * half_rows + (1 - aa) * quarter, 16), quarter)
    flies = len(dev_fly)

    small_steps = [
        remote(small.at[other_half, :], small_c, snd_s.at[0], rcv_s.at[0], dev_c),
        remote(small.at[other_quarter, :], small_x, snd_s.at[1], rcv_s.at[1], dev_x),
    ]
    for k, dev in enumerate(dev_fly):
        small_steps.append(
            remote(small_s.at[k], small_r.at[k], snd_s.at[2 + k], rcv_s.at[2 + k], dev)
        )
    for k, (rows, dev) in enumerate(((own_quarter, dev_x), (own_half, dev_c))):
        region = small_o.at[rows, :]
        n = 2 + flies + k
        small_steps.append(remote(region, region, snd_s.at[n], rcv_s.at[n], dev))

    def small_start(n):
        if n == 2:
            small_s[0] = small[own_quarter, :].astype(BF16)
        small_steps[n].start()

    def small_finish(n):
        if n < 2 + flies:
            small_steps[n].wait()
        if n == 0:
            small[own_half, :] += small_c[...]
        elif n == 1:
            small[own_quarter, :] += small_x[...]
        elif n < 2 + flies:
            total = small_s[n - 2].astype(F32) + small_r[n - 2].astype(F32)
            if n + 1 < 2 + flies:
                small_s[n - 1] = total.astype(BF16)
            else:
                small_o[own_quarter, :] = total.astype(BF16)
        else:
            rows = other_quarter if n == 2 + flies else other_half
            region = small_o.at[rows, :]
            small_steps[n].wait_send()
            remote(region, region, snd_s.at[n], rcv_s.at[n], dev_x).wait_recv()

    def small_step(n):
        if n == 0:
            small[424:432, :] = vacc[:, :half]
            small[432:440, :] = vacc[:, half:]
        else:
            small_finish(n - 1)
        if n < len(small_steps):
            small_start(n)

    work = {
        "D": weight_out,
        "I": weight_in,
        "G": grad_hidden,
        "Y": grad_rows,
        "F": first_sum,
        "S": shared_sum,
        "Z": solo_sum,
        "E": start_gather,
        "P": pass_on,
        "T": token_backward,
        "M": send_grad,
        "O": send_out,
        "R": small_step,
    }
    for name, *index in PLAN:
        work[name](*index)
    for n in range(SMALL_STEPS + 1, len(small_steps) + 1):
        small_step(n)

    for s in range(RING - SLOTS, RING):
        for a in range(2):
            to_core(s, a).wait_send()
    for a in range(2):
        for c in range(3):
            keep(a, c).wait()

    def drain_images(i, carry):
        out_local(i).wait()
        out_remote(i, 1 - aa).wait()
        grad_local(i).wait()
        grad_remote(i, 1 - aa).wait()
        return carry

    lax.fori_loop(0, imgs, drain_images, 0)

    for t in range(RING - 1):
        for a in range(2):
            for c in range(3):
                to_ring(t, a, c).wait_send()
                gather_arrival(t, a, c).wait_send()


def finish_kernel(gim, d2, d1, small, gim_o, w2_o, w1_o, tw1_o, tw2_o, tb1_o, tb2_o, b1_o, *rest):
    vec_o = rest[:5]
    gim_i, d2_i, d1_i, gim_f, d2_f, d1_f, sem_i, sem_o = rest[5:]
    count, piece, chans = d1.shape
    size = chans // CHUNKS
    rows = count * piece // CHUNKS
    some = gim.shape[0] // CHUNKS

    def parts(c, fetch):
        lanes, block, slots = (pl.ds(c * n, n) for n in (size, rows, some))
        if fetch:
            pairs = (
                (d1.at[:, :, lanes], d1_i.at[:, :, lanes]),
                (d2.at[block], d2_i.at[block]),
                (gim.at[slots], gim_i.at[slots]),
            )
        else:
            pairs = (
                (d1_f.at[lanes], w1_o.at[lanes]),
                (d2_f.at[block], w2_o.at[block]),
                (gim_f.at[slots], gim_o.at[slots]),
            )
        sem = sem_i if fetch else sem_o
        return [pltpu.make_async_copy(*pair, sem.at[c, n]) for n, pair in enumerate(pairs)]

    for c in range(CHUNKS):
        for copy in parts(c, True):
            copy.start()
    for c in range(CHUNKS):
        fetched, stored = parts(c, True), parts(c, False)
        fetched[0].wait()
        turned = d1_i[:, :, c * size : (c + 1) * size].reshape(count * piece, size)
        d1_f[c * size : (c + 1) * size] = jnp.transpose(turned).astype(F32)
        stored[0].start()
        fetched[1].wait()
        d2_f[c * rows : (c + 1) * rows] = d2_i[c * rows : (c + 1) * rows].astype(F32)
        stored[1].start()
        fetched[2].wait()
        gim_f[c * some : (c + 1) * some] = gim_i[c * some : (c + 1) * some].astype(F32)
        stored[2].start()
    aa, ba = lax.axis_index("aa"), lax.axis_index("ba")
    patches = tw1_o.shape[0]
    tw1_o[...] = small[0:patches, :].astype(F32)
    tw2_o[...] = small[200 : 200 + patches, :].astype(F32)
    tb1_o[...] = small[400:401, :].astype(F32).reshape(tb1_o.shape)
    tb2_o[...] = small[408:409, 0:patches].astype(F32).reshape(patches)
    vals = small[416:424, :].astype(F32)
    vals = jnp.where(ba == 0, vals[:, :piece], vals[:, piece:])
    vals = jnp.concatenate([vals[q : q + 1, :] for q in range(RING)], axis=1)
    b1_o[...] = vals.reshape(b1_o.shape)
    vals = jnp.where(aa == 0, small[424:432, :].astype(F32), small[432:440, :].astype(F32))
    for k, ref in enumerate(vec_o):
        ref[...] = vals[k : k + 1, :].reshape(ref.shape)
    for c in range(CHUNKS):
        for copy in parts(c, False):
            copy.wait()


def local(groups, images, counts, ln1_gain, ln1_bias, tok_w1, tok_b1, tok_w2, tok_b2,
          ln2_gain, ln2_bias, ch_w1, ch_b1, ch_w2, ch_b2, cotangent):
    slots, patches, half = images.shape
    chans = 2 * half
    imgs = slots // 2
    pad = -(-patches // 16) * 16
    hidden = ch_w1.shape[1]
    piece = hidden // RING
    both = piece - 2 * SOLO
    keep_rows = SOLO + both
    hid_tok = tok_w1.shape[1]
    total = 448
    flies = 3
    while RING * groups > 2**flies:
        flies += 1
    his = max(flies - 3, 1)
    vmem = pl.BlockSpec(memory_space=pltpu.VMEM)
    hbm = pl.BlockSpec(memory_space=pl.ANY)
    dma = pltpu.SemaphoreType.DMA
    per_image = [dma((imgs,))] * 3
    out, gim, d2, d1, small, _ = pl.pallas_call(
        functools.partial(layer_kernel, groups),
        out_shape=[
            jax.ShapeDtypeStruct((slots, patches, half), BF16),
            jax.ShapeDtypeStruct((slots, patches, half), BF16),
            jax.ShapeDtypeStruct((RING, piece, chans), BF16),
            jax.ShapeDtypeStruct((RING, piece, chans), BF16),
            jax.ShapeDtypeStruct((total, hid_tok), BF16),
            jax.ShapeDtypeStruct((his, 2, piece if groups > 1 else 16, chans), BF16),
        ],
        in_specs=[pl.BlockSpec(memory_space=pltpu.SMEM), hbm, hbm]
        + [vmem] * 9
        + [hbm] * 2
        + [vmem],
        out_specs=[hbm] * 4 + [vmem, hbm],
        scratch_shapes=[
            pltpu.VMEM((2, imgs, patches, half), BF16),
            pltpu.VMEM((2, imgs, patches, half), BF16),
            pltpu.VMEM((imgs * pad, chans), BF16),
            pltpu.VMEM((imgs * pad, chans), BF16),
            pltpu.VMEM((imgs, patches, chans), F32),
            pltpu.VMEM((imgs * pad, chans), F32),
            pltpu.VMEM((RING, 2 * piece, chans), BF16),
            pltpu.VMEM((RING, 2 * piece, chans), BF16),
            pltpu.VMEM((RING, imgs * pad, 2 * piece), BF16),
            pltpu.VMEM((RING, imgs * pad, 2 * piece), BF16),
            pltpu.VMEM((imgs, patches, 4), F32),
            pltpu.VMEM((SLOTS, 2, 2 * piece, chans), BF16),
            pltpu.VMEM((RING, 2, piece, chans), BF16),
            pltpu.VMEM((RING, 2, SOLO, chans), BF16),
            pltpu.VMEM((RING, 2, SOLO, chans), F32),
            pltpu.VMEM((RING, 2, keep_rows, chans), BF16),
            pltpu.VMEM((2, both, chans), BF16),
            pltpu.VMEM((2, piece, chans), BF16),
            pltpu.VMEM((2, 8, half), F32),
            pltpu.VMEM((2, 1, hidden), F32),
            pltpu.VMEM((RING, 2 * piece), F32),
            pltpu.VMEM((hid_tok, 1), F32),
            pltpu.VMEM((patches, 1), F32),
            pltpu.VMEM((8, chans), F32),
            pltpu.VMEM((total, hid_tok), F32),
            pltpu.VMEM((total // 2, hid_tok), F32),
            pltpu.VMEM((total // 4, hid_tok), F32),
            pltpu.VMEM((flies, total // 4, hid_tok), BF16),
            pltpu.VMEM((flies, total // 4, hid_tok), BF16),
            *per_image,
            *per_image,
            dma((5,)),
            dma((4,)),
            dma((4,)),
            dma((RING, 2)),
            dma((RING, 2)),
            dma((RING, 2)),
            dma((RING, 2)),
            dma((RING, 2, 3)),
            dma((RING, 2, 3)),
            dma((1 + his, 2, 3)),
            dma((1 + his, 2, 3)),
            dma((RING, 2, 3)),
            dma((RING, 2, 3)),
            dma((2, 3)),
            *per_image,
            *per_image,
            dma((4 + flies,)),
            dma((4 + flies,)),
        ],
        compiler_params=pltpu.CompilerParams(
            collective_id=0, has_side_effects=True, vmem_limit_bytes=65100 * 1024
        ),
    )(
        counts,
        images,
        cotangent,
        ln1_gain,
        ln1_bias,
        ln2_gain,
        ln2_bias,
        ch_b2,
        tok_w1,
        tok_b1,
        tok_w2.T,
        tok_b2,
        ch_w1,
        ch_w2.reshape(RING, piece, chans),
        ch_b1,
    )
    row = jax.ShapeDtypeStruct((half,), F32)
    gim, w2, w1, tw1, tw2, tb1, tb2, b1, g1, n1, g2, n2, c2 = pl.pallas_call(
        finish_kernel,
        out_shape=[
            jax.ShapeDtypeStruct((slots, patches, half), F32),
            jax.ShapeDtypeStruct((hidden, chans), F32),
            jax.ShapeDtypeStruct((chans, hidden), F32),
            jax.ShapeDtypeStruct((patches, hid_tok), F32),
            jax.ShapeDtypeStruct((patches, hid_tok), F32),
            jax.ShapeDtypeStruct((hid_tok,), F32),
            jax.ShapeDtypeStruct((patches,), F32),
            jax.ShapeDtypeStruct((hidden,), F32),
        ]
        + [row] * 5,
        in_specs=[hbm] * 3 + [vmem],
        out_specs=[hbm] * 3 + [vmem] * 10,
        scratch_shapes=[
            pltpu.VMEM((slots, patches, half), BF16),
            pltpu.VMEM((hidden, chans), BF16),
            pltpu.VMEM((RING, piece, chans), BF16),
            pltpu.VMEM((slots, patches, half), F32),
            pltpu.VMEM((hidden, chans), F32),
            pltpu.VMEM((chans, hidden), F32),
            dma((CHUNKS, 3)),
            dma((CHUNKS, 3)),
        ],
        compiler_params=pltpu.CompilerParams(vmem_limit_bytes=62 * 2**20),
    )(gim, d2.reshape(hidden, chans), d1, small)
    return out, gim, g1, n1, tw1, tb1, tw2.T, tb2, g2, n2, w1, b1, w2, c2


def solution(mesh):
    rows = P(("dp", "ba"), None, "aa")
    chan = P("aa")
    placed = (rows, P(("dp", "ba")), chan, chan, P(), P(), P(), P(), chan, chan,
              P(None, "ba"), P("ba"), P("ba", None), chan, rows)
    given = (rows, rows, chan, chan, P(), P(), P(), P(), chan, chan,
             P(None, "ba"), P("ba"), P("ba", None), chan)
    return jax.shard_map(
        functools.partial(local, mesh.shape["dp"] // RING),
        mesh=mesh,
        in_specs=placed,
        out_specs=given,
        check_vma=False,
    )
```
